32 devices in a mesh: tab: 2 (over x), fsdp: 16 (over z, y, core).
Axes of the slice: x: 2, y: 2, z: 4, core: 2. Of those that a mesh axis runs over, the one named last changes fastest.
Arguments:
- features: bfloat16 [16, 2048, 100], P('fsdp', 'tab'), may hold values from -6 to 6
- feature_counts: int32 [16], P('fsdp'), may hold values from 3 to 100
- row_flags: int32 [16, 2048], P('fsdp', 'tab'), may hold values from 0 to 1, as said below
- target_bins: int32 [16, 2048], P('fsdp', 'tab'), may hold values from 0 to 4999
- emb_weight: float32 [100, 768], P(None, 'fsdp'), may hold values from -0.625 to 0.625
- qkv_weight: float32 [768, 2304], P('fsdp'), may hold values from -0.21875 to 0.21875
- out_weight: float32 [768, 768], P('fsdp'), may hold values from -0.875 to 0.875
- up_weight: float32 [768, 3072], P('fsdp'), may hold values from -0.21875 to 0.21875
- down_weight: float32 [3072, 768], P('fsdp'), may hold values from -0.109375 to 0.109375
- head_weight: float32 [768, 5000], P('fsdp'), may hold values from -0.21875 to 0.21875
- vectors: float32 [4, 768], P(None, 'fsdp')
- mom_emb: float32 [100, 768], P(None, 'fsdp'), may hold values from -2.2888184e-05 to 2.2888184e-05
- mom_qkv: float32 [768, 2304], P('fsdp'), may hold values from -2.2888184e-05 to 2.2888184e-05
- mom_out: float32 [768, 768], P('fsdp'), may hold values from -2.2888184e-05 to 2.2888184e-05
- mom_up: float32 [768, 3072], P('fsdp'), may hold values from -2.2888184e-05 to 2.2888184e-05
- mom_down: float32 [3072, 768], P('fsdp'), may hold values from -2.2888184e-05 to 2.2888184e-05
- mom_head: float32 [768, 5000], P('fsdp'), may hold values from -2.2888184e-05 to 2.2888184e-05
- mom_vectors: float32 [4, 768], P(None, 'fsdp'), may hold values from -0.00010681152 to 0.00010681152
- ema_emb: float32 [100, 768], P(None, 'fsdp'), may hold values from -0.625 to 0.625
- ema_qkv: float32 [768, 2304], P('fsdp'), may hold values from -0.21875 to 0.21875
- ema_out: float32 [768, 768], P('fsdp'), may hold values from -0.875 to 0.875
- ema_up: float32 [768, 3072], P('fsdp'), may hold values from -0.21875 to 0.21875
- ema_down: float32 [3072, 768], P('fsdp'), may hold values from -0.109375 to 0.109375
- ema_head: float32 [768, 5000], P('fsdp'), may hold values from -0.21875 to 0.21875
- ema_vectors: float32 [4, 768], P(None, 'fsdp'), may hold values from 0.5 to 1.5
Outputs:
- loss_sum: float32 [], replicated
- row_count: float32 [], replicated
- rms_sums: float32 [3], replicated
- clip_norm: float32 [], replicated
- new_mom_emb: float32 [100, 768], P(None, 'fsdp')
- new_mom_qkv: float32 [768, 2304], P('fsdp')
- new_mom_out: float32 [768, 768], P('fsdp')
- new_mom_up: float32 [768, 3072], P('fsdp')
- new_mom_down: float32 [3072, 768], P('fsdp')
- new_mom_head: float32 [768, 5000], P('fsdp')
- new_mom_vectors: float32 [4, 768], P(None, 'fsdp')
- new_emb: float32 [100, 768], P(None, 'fsdp')
- new_qkv: float32 [768, 2304], P('fsdp')
- new_out: float32 [768, 768], P('fsdp')
- new_up: float32 [768, 3072], P('fsdp')
- new_down: float32 [3072, 768], P('fsdp')
- new_head: float32 [768, 5000], P('fsdp')
- new_vectors: float32 [4, 768], P(None, 'fsdp')
- new_ema_emb: float32 [100, 768], P(None, 'fsdp')
- new_ema_qkv: float32 [768, 2304], P('fsdp')
- new_ema_out: float32 [768, 768], P('fsdp')
- new_ema_up: float32 [768, 3072], P('fsdp')
- new_ema_down: float32 [3072, 768], P('fsdp')
- new_ema_head: float32 [768, 5000], P('fsdp')
- new_ema_vectors: float32 [4, 768], P(None, 'fsdp')
The draws below stay inside these ranges and needn't reach their ends.
Inputs may be any that keep to these rules, and one draw needn't show every extreme that they name: `row_flags`: in every table the first row is a context row and the last a query row.
All inputs are finite; a program needn't handle non-finite values.
Results may differ from the reference program's by a relative error of at most 0.012.
The reference program's roundings to bfloat16 on the way count: a program that leaves them out, or rounds other values in their place, can miss the bound.
Values may be sent and summed in bfloat16 or wider, within the bound.
No kernel may reach another device: no remote copies, remote signals or barrier semaphores. Data moves between devices by JAX's collectives and lax.ppermute only.
A program may use at most 256 MiB of HBM per device.

```python
import jax
import jax.numpy as jnp
from jax import lax

D = 768
HEADS = 12
HEAD_DIM = 64
FF = 3072
BINS = 5000
F = 100
TAB_LEN = 2048
TABLES = 16


def draw_row_flags(key, part):
    key = jax.random.fold_in(key, 7)
    table = jnp.arange(TABLES, dtype=jnp.int32)[:, None]
    row = jnp.arange(TAB_LEN, dtype=jnp.int32)[None, :]
    share = 1200 * (TABLES - 1 + 2 * table) // max(TABLES - 1, 1)
    limit = share * (TAB_LEN + 2 * row) // (2 * TAB_LEN)
    drawn = jax.random.randint(key, (TABLES, TAB_LEN), 0, 10000, dtype=jnp.int32)
    flags = (drawn < limit).astype(jnp.int32)
    flags = jnp.where(row == 0, 0, flags)
    flags = jnp.where(row == TAB_LEN - 1, 1, flags)
    return flags.astype(jnp.int32)


def draw_vectors(key, part):
    key = jax.random.fold_in(key, 11)
    place = jnp.arange(D, dtype=jnp.float32) / D
    noise = jax.random.uniform(key, (3, D), jnp.float32, 0.85, 1.15)
    ramp = 0.6 + 1.2 * place
    label_row = jax.random.normal(jax.random.fold_in(key, 1), (1, D), jnp.float32)
    return jnp.concatenate([ramp[None, :] * noise, label_row], axis=0)


def with_ends(values, own_key, smallest, high):
    shape = values.shape
    spot = [jax.random.randint(jax.random.fold_in(own_key, axis), (), 0, shape[axis]) for axis in range(len(shape))]
    values = values.at[tuple(spot)].set(smallest)
    longest = shape.index(max(shape))
    spot[longest] = (spot[longest] + 1) % shape[longest]
    return values.at[tuple(spot)].set(high)


def steps_of(rng, extent, shards, smallest, high):
    def one(position, parts):
        draws = jax.random.uniform(jax.random.fold_in(jax.random.fold_in(rng, 6), position), (parts,), jnp.float32, smallest / len(shards), high / len(shards))
        return jnp.repeat(jnp.exp(draws), extent[position] // parts).reshape((-1,) + (1,) * (len(extent) - position - 1))

    factor_of = one(*shards[0])
    for cut in shards[1:]:
        factor_of = factor_of * one(*cut)
    return factor_of


def centred(key, dims, spread, bound, shards=(), held_as=jnp.bfloat16):
    values = spread * jax.random.normal(key, dims, jnp.float32)
    if shards:
        values = values * steps_of(key, dims, shards, -0.22, 0.18)
    return jnp.clip(values, -bound, bound).astype(held_as)


def setup_inputs(seed: int = 0) -> dict:
    key_of = jax.random.split(jax.random.key(seed), 26)
    features = centred(key_of[0], (TABLES, TAB_LEN, F), 1.0, 6.0, ((0, 16), (1, 2)))
    feature_counts = with_ends(jax.random.randint(key_of[1], (TABLES,), 3, F + 1), jax.random.fold_in(key_of[1], 1), 3, F).astype(jnp.int32)
    row_flags = draw_row_flags(jax.random.fold_in(key_of[25], 71), 0)
    target_bins = with_ends(jax.random.randint(key_of[3], (TABLES, TAB_LEN), 0, BINS), jax.random.fold_in(key_of[3], 1), 0, BINS - 1).astype(jnp.int32)
    emb_weight = centred(key_of[4], (F, D), F ** -0.5, 0.625, ((1, 16),), jnp.float32)
    qkv_weight = centred(key_of[5], (D, 3 * D), D ** -0.5, 0.21875, ((0, 16),), jnp.float32)
    out_weight = centred(key_of[6], (D, D), (D // 16) ** -0.5, 0.875, ((0, 16),), jnp.float32)
    up_weight = centred(key_of[7], (D, FF), D ** -0.5, 0.21875, ((0, 16),), jnp.float32)
    down_weight = centred(key_of[8], (FF, D), FF ** -0.5, 0.109375, ((0, 16),), jnp.float32)
    head_weight = centred(key_of[9], (D, BINS), D ** -0.5, 0.21875, ((0, 16),), jnp.float32)
    vectors = draw_vectors(jax.random.fold_in(key_of[25], 71), 0)
    mom_emb = centred(key_of[11], (F, D), (0.005 / (F * D + 4 * D * D + 2 * D * FF + D * BINS + 4 * D) ** 0.5), 2.288818359375e-05, ((1, 16),), jnp.float32)
    mom_qkv = centred(key_of[12], (D, 3 * D), (0.005 / (F * D + 4 * D * D + 2 * D * FF + D * BINS + 4 * D) ** 0.5), 2.288818359375e-05, ((0, 16),), jnp.float32)
    mom_out = centred(key_of[13], (D, D), (0.005 / (F * D + 4 * D * D + 2 * D * FF + D * BINS + 4 * D) ** 0.5), 2.288818359375e-05, ((0, 16),), jnp.float32)
    mom_up = centred(key_of[14], (D, FF), (0.005 / (F * D + 4 * D * D + 2 * D * FF + D * BINS + 4 * D) ** 0.5), 2.288818359375e-05, ((0, 16),), jnp.float32)
    mom_down = centred(key_of[15], (FF, D), (0.005 / (F * D + 4 * D * D + 2 * D * FF + D * BINS + 4 * D) ** 0.5), 2.288818359375e-05, ((0, 16),), jnp.float32)
    mom_head = centred(key_of[16], (D, BINS), (0.005 / (F * D + 4 * D * D + 2 * D * FF + D * BINS + 4 * D) ** 0.5), 2.288818359375e-05, ((0, 16),), jnp.float32)
    mom_vectors = centred(key_of[17], (4, D), (0.025 / (F * D + 4 * D * D + 2 * D * FF + D * BINS + 4 * D) ** 0.5), 0.00010681152, ((1, 16),), jnp.float32)
    ema_emb = centred(key_of[18], (F, D), F ** -0.5, 0.625, ((1, 16),), jnp.float32)
    ema_qkv = centred(key_of[19], (D, 3 * D), D ** -0.5, 0.21875, ((0, 16),), jnp.float32)
    ema_out = centred(key_of[20], (D, D), (D // 16) ** -0.5, 0.875, ((0, 16),), jnp.float32)
    ema_up = centred(key_of[21], (D, FF), D ** -0.5, 0.21875, ((0, 16),), jnp.float32)
    ema_down = centred(key_of[22], (FF, D), FF ** -0.5, 0.109375, ((0, 16),), jnp.float32)
    ema_head = centred(key_of[23], (D, BINS), D ** -0.5, 0.21875, ((0, 16),), jnp.float32)
    ema_vectors = jnp.clip(1.0 + 0.1 * jax.random.normal(key_of[24], (4, D), jnp.float32), 0.5, 1.5)
    return {"features": features, "feature_counts": feature_counts, "row_flags": row_flags, "target_bins": target_bins, "emb_weight": emb_weight, "qkv_weight": qkv_weight, "out_weight": out_weight, "up_weight": up_weight, "down_weight": down_weight, "head_weight": head_weight, "vectors": vectors, "mom_emb": mom_emb, "mom_qkv": mom_qkv, "mom_out": mom_out, "mom_up": mom_up, "mom_down": mom_down, "mom_head": mom_head, "mom_vectors": mom_vectors, "ema_emb": ema_emb, "ema_qkv": ema_qkv, "ema_out": ema_out, "ema_up": ema_up, "ema_down": ema_down, "ema_head": ema_head, "ema_vectors": ema_vectors}


CLIP = 0.005
RATE = 10000.0
MOMENTUM = 0.5
AVERAGE = 0.5
HIGH = lax.Precision.HIGHEST

@jax.custom_vjp
def low(v):
    return lax.optimization_barrier(v.astype(jnp.bfloat16)).astype(jnp.float32)

@jax.custom_vjp
def low_back(v):
    return v

def low_keep(v):
    return (low(v), None)

def low_pass(kept, grad):
    return (grad,)

def back_keep(v):
    return (v, None)

def back_low(kept, grad):
    return (low(grad),)
low.defvjp(low_keep, low_pass)
low_back.defvjp(back_keep, back_low)

def matmul(left, right):
    return jnp.dot(left, right, precision=HIGH, preferred_element_type=jnp.float32)

def rms_norm(stream, gain):
    return stream * lax.rsqrt(lax.optimization_barrier(jnp.mean(stream * stream, axis=-1, keepdims=True)) + 1e-06) * gain

def row_rms(stream):
    return jnp.sqrt(lax.optimization_barrier(jnp.mean(stream * stream, axis=-1)) + 1e-06)

def table_loss(params, feats, count, flags, targets):
    emb_weight, qkv_weight, out_weight, up_weight, down_weight, head_weight, vectors = params
    width = qkv_weight.shape[0]
    nfeat = feats.shape[-1]
    rows = feats.shape[0]
    gains = low(vectors)
    keep = (jnp.arange(nfeat) < count).astype(jnp.float32)
    scale = jnp.sqrt(nfeat / count.astype(jnp.float32))
    x_in = low(feats * keep[None, :] * scale)
    context = (flags == 0).astype(jnp.float32)
    query = (flags == 1).astype(jnp.float32)
    label = (targets.astype(jnp.float32) + 0.5) * (2.0 / BINS) - 1.0
    stream0 = low_back(matmul(x_in, low(emb_weight))) + (context * label)[:, None] * gains[3][None, :]
    normed = low(rms_norm(stream0, gains[0]))
    project = low_back(matmul(normed, low(qkv_weight)))
    queries = low(project[:, :width]).reshape(rows, HEADS, HEAD_DIM)
    keys_h = low(project[:, width:2 * width]).reshape(rows, HEADS, HEAD_DIM)
    values_h = low(project[:, 2 * width:]).reshape(rows, HEADS, HEAD_DIM)
    scores = jnp.einsum('qhd,khd->hqk', queries, keys_h, precision=HIGH) * HEAD_DIM ** (-0.5)
    scores = low_back(jnp.where(context[None, None, :] > 0, scores, -1e+30))
    probs = jax.nn.softmax(scores, axis=-1)
    attended = jnp.einsum('hqk,khd->qhd', low(probs), values_h, precision=HIGH).reshape(rows, width)
    attn_branch = low_back(matmul(low_back(low(attended)), low(out_weight)))
    stream1 = stream0 + attn_branch
    normed2 = low(rms_norm(stream1, gains[1]))
    upper = low_back(matmul(normed2, low(up_weight)))
    activ = low(jax.nn.gelu(upper))
    mlp_branch = low_back(matmul(activ, low(down_weight)))
    stream2 = stream1 + mlp_branch
    normed3 = low(rms_norm(stream2, gains[2]))
    logits = low_back(matmul(normed3, low(head_weight)))
    logsum = jax.nn.logsumexp(logits, axis=-1)
    target_logit = jnp.take_along_axis(logits, targets[:, None].astype(jnp.int32), axis=-1)[:, 0]
    stats = jnp.stack([jnp.sum(query * row_rms(stream2)), jnp.sum(query * row_rms(attn_branch)), jnp.sum(query * row_rms(mlp_branch))])
    return (jnp.sum((logsum - target_logit) * query), stats)

def reference(features, feature_counts, row_flags, target_bins, emb_weight, qkv_weight, out_weight, up_weight, down_weight, head_weight, vectors, mom_emb, mom_qkv, mom_out, mom_up, mom_down, mom_head, mom_vectors, ema_emb, ema_qkv, ema_out, ema_up, ema_down, ema_head, ema_vectors):
    params = (emb_weight, qkv_weight, out_weight, up_weight, down_weight, head_weight, vectors)
    moms = (mom_emb, mom_qkv, mom_out, mom_up, mom_down, mom_head, mom_vectors)
    emas = (ema_emb, ema_qkv, ema_out, ema_up, ema_down, ema_head, ema_vectors)
    feats = features.astype(jnp.float32)
    row_count = jnp.sum((row_flags == 1).astype(jnp.float32))
    one_table = jax.checkpoint(table_loss)

    def total(weights):
        per_table, per_stats = lax.map(lambda items: one_table(weights, *items), (feats, feature_counts, row_flags, target_bins))
        return (jnp.sum(per_table), lax.optimization_barrier(jnp.sum(per_stats, axis=0)))
    loss_sum, pullback, rms_sums = jax.vjp(total, params, has_aux=True)
    grads = pullback(jnp.float32(1.0) / row_count)[0]
    squares = sum((jnp.sum(grad * grad) for grad in grads))
    clip_norm = jnp.sqrt(squares)
    factor = jnp.minimum(1.0, CLIP / clip_norm)
    new_moms, new_weights, new_emas = ([], [], [])
    for weight, grad, moment, average in zip(params, grads, moms, emas):
        clipped = grad * factor
        moment_new = MOMENTUM * moment + clipped
        weight_new = weight - RATE * (clipped + MOMENTUM * moment_new)
        new_moms.append(moment_new)
        new_weights.append(weight_new)
        new_emas.append(AVERAGE * average + (1.0 - AVERAGE) * weight_new)
    return (loss_sum, row_count, rms_sums, clip_norm, new_moms[0], new_moms[1], new_moms[2], new_moms[3], new_moms[4], new_moms[5], new_moms[6], new_weights[0], new_weights[1], new_weights[2], new_weights[3], new_weights[4], new_weights[5], new_weights[6], new_emas[0], new_emas[1], new_emas[2], new_emas[3], new_emas[4], new_emas[5], new_emas[6])
```

```python
import functools

import jax
import jax.numpy as jnp
import numpy as np
from jax import lax
from jax.experimental import pallas as pl
from jax.experimental.pallas import tpu as pltpu
from jax.sharding import PartitionSpec as P

HEADS = 12
BINS = 5000
CLIP = 0.005
RATE = 10000.0
MOMENTUM = 0.5
AVERAGE = 0.5

BF = jnp.bfloat16
F32 = jnp.float32
LANES = 128
QB = 256
CB = 512
HC = 512
VMEM = 60 * 1024 * 1024
LOW = -1e30


def mm(left, right):
    return jnp.dot(left, right, preferred_element_type=F32)


def mm_tn(left, right):
    return lax.dot_general(left, right, (((0,), (0,)), ((), ())), preferred_element_type=F32)


def mm_nt(left, right):
    return lax.dot_general(left, right, (((1,), (1,)), ((), ())), preferred_element_type=F32)


def iota(shape, axis):
    return lax.broadcasted_iota(jnp.int32, shape, axis)


def block(index, size):
    return pl.ds(pl.multiple_of(index * size, size), size)


def inverse_rms(stream):
    return lax.rsqrt(jnp.mean(stream * stream, axis=-1, keepdims=True) + 1e-06)


def rms_back(stream, gain, upstream):
    scale = inverse_rms(stream)
    unit = stream * scale
    weighted = upstream * gain
    back = scale * (weighted - unit * jnp.mean(weighted * unit, axis=-1, keepdims=True))
    return back, jnp.sum(upstream * unit, axis=0, keepdims=True)


def params(*semantics):
    return pltpu.CompilerParams(vmem_limit_bytes=VMEM)


def anywhere():
    return pl.BlockSpec(memory_space=pl.ANY)


def in_vmem():
    return pl.BlockSpec(memory_space=pltpu.VMEM)


def in_smem():
    return pl.BlockSpec(memory_space=pltpu.SMEM)


def shape(dims, dtype):
    return jax.ShapeDtypeStruct(dims, dtype)


class Group:
    def __init__(self, axis_bits, rows, parts, count):
        self.steps = axis_bits
        self.rows = rows
        self.parts = parts
        self.count = count
        self.width = sum(width * blocks for width, blocks in parts)
        self.pieces = 2 ** len(axis_bits)
        self.direct = rows % 16 == 0

    def place(self, piece, core):
        across, half = core, 0
        for bit, step in enumerate(self.steps):
            if piece >> bit & 1:
                if step == "tab":
                    half ^= 1
                else:
                    across ^= step
        return across, half

    def spans(self):
        start = 0
        for part, (width, blocks) in enumerate(self.parts):
            for at in range(blocks):
                yield part, start, width, at, blocks
                start += width

    def full_shapes(self):
        return [(2, self.count * self.rows * blocks, width) for width, blocks in self.parts]

    def table(self):
        order = np.zeros((2, self.count), np.int32)
        for core in range(2):
            for piece in range(self.pieces):
                across, half = self.place(piece, core)
                order[half, across] = core * self.pieces + piece
        return order

    def to_whole(self, near, far, me, tab):
        halves = np.arange(2, dtype=np.int32)[:, None] ^ tab
        places = np.arange(self.count, dtype=np.int32)[None, :] ^ me
        index = jnp.asarray(self.table())[halves, places]
        every = jnp.take(jnp.concatenate([near, far]), index, axis=0)
        whole = [[] for _ in self.parts]
        for part, start, width, _, _ in self.spans():
            whole[part].append(every[..., start : start + width])
        return [
            jnp.stack(found, axis=2).reshape(dims) for found, dims in zip(whole, self.full_shapes())
        ]

    def to_pieces(self, wholes, me, tab):
        columns = []
        for part, _, width, at, blocks in self.spans():
            split = wholes[part].reshape(2, self.count, blocks, self.rows, width)
            columns.append(split[:, :, at])
        every = jnp.concatenate(columns, axis=-1).reshape(2 * self.count, self.rows, self.width)
        where = np.array(
            [
                self.place(piece, core)
                for core in range(2)
                for piece in range(self.pieces)
            ],
            np.int32,
        )
        index = (where[:, 1] ^ tab) * self.count + (where[:, 0] ^ me)
        found = jnp.take(every, index, axis=0)
        return found[: self.pieces], found[self.pieces :]

    def load(self, sources, wholes, sems, me, tab):
        if not self.direct:
            for source, whole, sem in zip(sources, wholes, sems):
                pltpu.make_async_copy(source, whole, sem).start()
            return
        for core in range(2):
            for piece in range(self.pieces):
                across, half = self.place(piece, core)
                shard = lax.bitwise_xor(me, jnp.int32(across))
                side = lax.bitwise_xor(tab, jnp.int32(half))
                for part, start, width, at, blocks in self.spans():
                    first = pl.multiple_of((shard * blocks + at) * self.rows, self.rows)
                    pltpu.make_async_copy(
                        sources[core].at[piece, :, pl.ds(start, width)],
                        wholes[part].at[side, pl.ds(first, self.rows), :],
                        sems[part],
                    ).start()

    def store(self, wholes, targets, sems, me, tab, parts=None):
        if not self.direct:
            for whole, target, sem in zip(wholes, targets, sems):
                pltpu.make_async_copy(whole, target, sem).start()
            return
        for core in range(2):
            for piece in range(self.pieces):
                across, half = self.place(piece, core)
                shard = lax.bitwise_xor(me, jnp.int32(across))
                side = lax.bitwise_xor(tab, jnp.int32(half))
                for part, start, width, at, blocks in self.spans():
                    first = pl.multiple_of((shard * blocks + at) * self.rows, self.rows)
                    pltpu.make_async_copy(
                        wholes[part].at[side, pl.ds(first, self.rows), :],
                        targets[core].at[piece, :, pl.ds(start, width)],
                        sems[core],
                    ).start()

    def stored(self, targets, sems):
        for target, sem in zip(targets, sems):
            pltpu.make_async_copy(target, target, sem).wait()

    def out_shapes(self):
        if self.direct:
            return [shape((self.pieces, self.rows, self.width), BF)] * 2
        return [shape(dims, BF) for dims in self.full_shapes()]

    def sources(self, near, far, me, tab):
        return [near, far] if self.direct else self.to_whole(near, far, me, tab)

    def targets(self, outs, me, tab):
        return tuple(outs) if self.direct else self.to_pieces(outs, me, tab)


def loaded(whole, sem):
    pltpu.make_async_copy(whole, whole, sem).wait()


def swap(value, step, count):
    if step == "tab":
        return lax.ppermute(value, "tab", [(0, 1), (1, 0)])
    return lax.ppermute(value, "fsdp", [(i, i ^ step) for i in range(count)])


def gather_group(group, piece):
    held = piece[None]
    for step in group.steps:
        held = jnp.concatenate([held, swap(held, step, group.count)])
    return held, swap(held, 1, group.count)


def scatter_group(group, near, far):
    held = near + swap(far, 1, group.count)
    for step in reversed(group.steps):
        half = held.shape[0] // 2
        other = swap(held[half:], step, group.count)
        held = held[:half].astype(F32) + other.astype(F32)
        if half > 1:
            held = held.astype(BF)
    return held[0]


def sort_rows(nfeat, count, table, marks, x_query, t_query, x_context, y_context):
    total, _ = table.shape
    rows = total // LANES
    flags = marks[...]
    inside = mm(flags.astype(BF), (iota((LANES, LANES), 0) <= iota((LANES, LANES), 1)).astype(F32).astype(BF))
    sums = jnp.broadcast_to(jnp.sum(flags, axis=1, keepdims=True), (rows, LANES))
    below = (iota((rows, rows), 1) < iota((rows, rows), 0)).astype(F32)
    upto = inside + mm(below.astype(BF), sums.astype(BF))
    spot = (iota((rows, LANES), 0) * LANES + iota((rows, LANES), 1)).astype(F32)
    as_query = jnp.where(flags > 0, upto - 1.0, -1.0)
    as_context = jnp.where(flags > 0, -1.0, spot - upto)
    held = count[6]
    scale = jnp.sqrt(F32(nfeat) / jnp.full((1, LANES), held, jnp.int32).astype(F32))

    def pick(rank, dest):
        hot = jnp.concatenate(
            [(rank[k : k + 1, :] == dest).astype(F32).astype(BF) for k in range(rows)], axis=1
        )
        found = mm(hot, table[...])
        kept = jnp.where(iota(found.shape, 1) < held, found * scale, 0.0).astype(BF)
        return kept, found[:, nfeat + 1 : nfeat + 2] * 64.0 + found[:, nfeat + 2 : nfeat + 3]

    def query(i, _):
        dest = (2 * (i * QB + iota((QB, LANES), 0)) + count[5]).astype(F32)
        kept, target = pick(as_query, dest)
        x_query[block(i, QB), :] = kept
        t_query[block(i, QB), :] = jnp.broadcast_to(target, (QB, LANES))
        return 0

    def context(i, _):
        dest = i * QB + iota((QB, LANES), 0)
        kept, target = pick(as_context, dest.astype(F32))
        x_context[block(i, QB), :] = kept
        label = (jnp.broadcast_to(target, (QB, LANES)) + 0.5) * (2.0 / BINS) - 1.0
        y_context[block(i, QB), :] = jnp.where(dest < count[1], label, 0.0)
        return 0

    lax.fori_loop(0, count[2], query, 0)
    lax.fori_loop(0, count[3] * (CB // QB), context, 0)


def sort_rows_call(nfeat, count, table, marks):
    total = table.shape[0]
    local = total // 2
    return pl.pallas_call(
        functools.partial(sort_rows, nfeat),
        out_shape=(
            shape((local, LANES), BF),
            shape((local, LANES), F32),
            shape((total, LANES), BF),
            shape((total, LANES), F32),
        ),
        in_specs=[in_smem(), in_vmem(), in_vmem()],
        out_specs=(in_vmem(),) * 4,
        compiler_params=params(),
        name="sort_rows",
    )(count, table, marks)


def project(group, nfeat, count, x_query, x_context, y_context, *rest):
    sources = rest[: 2 if group.direct else 1]
    (q_out, k_out, v_out, aq_out, ac_out, h_out, gains, weight, sem) = rest[len(sources) :]
    step = pl.program_id(0)
    blocks_q = pl.num_programs(0) - k_blocks(ac_out, count)
    third = q_out.shape[1] // 2

    @pl.when(step == 0)
    def _():
        group.load(sources, [weight], [sem.at[0]], count[4], count[5])
        loaded(weight, sem.at[0])
        vectors = weight[1, :, 3 * third :].astype(F32).T
        embedding = weight[0, :, 3 * third :].astype(F32).T
        high = jnp.sum(vectors[4:5, :]) + jnp.sum(embedding[nfeat : nfeat + 1, :])
        low = jnp.sum(vectors[5:6, :]) + jnp.sum(embedding[nfeat + 1 : nfeat + 2, :])
        width = vectors.shape[1]
        gains[...] = jnp.where(iota((8, width), 0) < 4, vectors[:8, :], high * 32.0 + low)

    def normed(stream):
        return (stream * inverse_rms(stream) * gains[0:1, :]).astype(BF)

    @pl.when(step < count[2])
    def _():
        stream = mm_nt(x_query[...], weight[0, :, 3 * third :])
        h_out[...] = stream
        a = normed(stream)
        aq_out[...] = a
        for side in range(2):
            q_out[:, side * third : (side + 1) * third] = mm(a, weight[side, :, :third]).astype(BF)

    @pl.when((step >= blocks_q) & (step < blocks_q + count[3]))
    def _():
        stream = mm_nt(x_context[...], weight[0, :, 3 * third :]) + y_context[:, 0:1] * gains[3:4, :]
        a = normed(stream)
        ac_out[...] = a
        for side in range(2):
            columns = slice(side * third, (side + 1) * third)
            k_out[:, columns] = mm(a, weight[side, :, third : 2 * third]).astype(BF)
            v_out[:, columns] = mm(a, weight[side, :, 2 * third : 3 * third]).astype(BF)


def k_blocks(ref, count):
    return 4


def project_call(group, nfeat, count, x_query, x_context, y_context, sources, model):
    local, total = x_query.shape[0], x_context.shape[0]
    blocks_q, blocks_c = local // QB, total // CB
    assert blocks_c == 4

    def q_map(i, c):
        return (jnp.minimum(i, c[2] - 1), 0)

    def c_map(i, c):
        return (jnp.clip(i - blocks_q, 0, c[3] - 1), 0)

    def same(i, c):
        return (0, 0)

    return pl.pallas_call(
        functools.partial(project, group, nfeat),
        grid_spec=pltpu.PrefetchScalarGridSpec(
            num_scalar_prefetch=1,
            grid=(blocks_q + blocks_c,),
            in_specs=[
                pl.BlockSpec((QB, LANES), q_map),
                pl.BlockSpec((CB, LANES), c_map),
                pl.BlockSpec((CB, LANES), c_map),
            ]
            + [anywhere()] * len(sources),
            out_specs=(
                pl.BlockSpec((QB, model), q_map),
                pl.BlockSpec((CB, model), c_map),
                pl.BlockSpec((CB, model), c_map),
                pl.BlockSpec((QB, model), q_map),
                pl.BlockSpec((CB, model), c_map),
                pl.BlockSpec((QB, model), q_map),
                pl.BlockSpec((8, model), same),
            ),
            scratch_shapes=[
                pltpu.VMEM(group.full_shapes()[0], BF),
                pltpu.SemaphoreType.DMA((1,)),
            ],
        ),
        out_shape=(
            shape((local, model), BF),
            shape((total, model), BF),
            shape((total, model), BF),
            shape((local, model), BF),
            shape((total, model), BF),
            shape((local, model), F32),
            shape((8, model), F32),
        ),
        compiler_params=params(),
        name="project",
    )(count, x_query, x_context, y_context, *sources)


def head_masks(size):
    low = (iota((1, LANES), 1) < size).astype(F32)
    return low.astype(BF), (1.0 - low).astype(BF)


def dead_rows(j, count):
    return jnp.where(j * CB + iota((CB, 1), 0) < count[1], 0.0, LOW)


def attend(size, count, q_ref, k_ref, v_ref, o_ref, lse_ref):
    scale = size ** (-0.5)
    masks = head_masks(size)

    def over_queries(i, _):
        queries = q_ref[block(i, QB), :] * BF(scale)
        heads = [queries * mask for mask in masks]

        def over_context(j, carry):
            keys, values = k_ref[block(j, CB), :], v_ref[block(j, CB), :]
            dead = dead_rows(j, count)
            found = []
            for head, (top, total, sums) in zip(heads, carry):
                scores = mm_nt(keys, head) + dead
                top_new = jnp.maximum(top, jnp.max(scores, axis=0, keepdims=True))
                fade = jnp.exp(top - top_new)
                expo = jnp.exp(scores - top_new)
                total = total * fade + jnp.sum(expo, axis=0, keepdims=True)
                sums = sums * fade + mm_tn(values, expo.astype(BF))
                found.append((top_new, total, sums))
            return tuple(found)

        start = (
            jnp.full((1, QB), 3.0 * LOW, F32),
            jnp.zeros((1, QB), F32),
            jnp.zeros((LANES, QB), F32),
        )
        ends = lax.fori_loop(0, count[3], over_context, (start, start))
        joined = jnp.concatenate(
            [
                (sums / total)[side * size : (side + 1) * size]
                for side, (_, total, sums) in enumerate(ends)
            ]
        )
        o_ref[block(i, QB), :] = joined.T.astype(BF)
        for side, (top, total, _) in enumerate(ends):
            lse_ref[side : side + 1, block(i, QB)] = top + jnp.log(total)
        return 0

    lax.fori_loop(0, count[2], over_queries, 0)


def attend_call(size, count, queries, keys, values):
    local, model = queries.shape
    total = keys.shape[0]
    pairs = model // LANES

    def column(i, c):
        return (0, i)

    return pl.pallas_call(
        functools.partial(attend, size),
        grid_spec=pltpu.PrefetchScalarGridSpec(
            num_scalar_prefetch=1,
            grid=(pairs,),
            in_specs=[
                pl.BlockSpec((local, LANES), column),
                pl.BlockSpec((total, LANES), column),
                pl.BlockSpec((total, LANES), column),
            ],
            out_specs=(
                pl.BlockSpec((local, LANES), column),
                pl.BlockSpec((None, 8, local), lambda i, c: (i, 0, 0)),
            ),
        ),
        out_shape=(shape((local, model), BF), shape((pairs, 8, local), F32)),
        compiler_params=params(),
        name="attend",
    )(count, queries, keys, values)


def attend_back(size, count, q_ref, k_ref, v_ref, do_ref, o_ref, lse_ref, dq_ref, dk_ref, dv_ref, dk_sum, dv_sum):
    scale = size ** (-0.5)
    masks = head_masks(size)

    def clear(j, _):
        dk_sum[block(j, CB), :] = jnp.zeros((CB, LANES), F32)
        dv_sum[block(j, CB), :] = jnp.zeros((CB, LANES), F32)
        return 0

    lax.fori_loop(0, count[3], clear, 0)

    def over_queries(i, _):
        rows = block(i, QB)
        queries = q_ref[rows, :] * BF(scale)
        grads = do_ref[rows, :]
        heads = [queries * mask for mask in masks]
        ups = [grads * mask for mask in masks]
        both_q = jnp.concatenate(heads)
        both_up = jnp.concatenate(ups)
        product = (grads.astype(F32) * o_ref[rows, :].astype(F32)).T
        deltas = [
            jnp.sum(product[side * size : (side + 1) * size], axis=0, keepdims=True) for side in range(2)
        ]
        logs = [lse_ref[side : side + 1, rows] for side in range(2)]

        def over_context(j, carry):
            spot = block(j, CB)
            keys, values = k_ref[spot, :], v_ref[spot, :]
            dead = dead_rows(j, count)
            probs, scores_back = [], []
            for side in range(2):
                prob = jnp.exp(mm_nt(keys, heads[side]) + dead - logs[side])
                upper = mm_nt(values, ups[side])
                scores_back.append((prob * (upper - deltas[side])).astype(BF))
                probs.append(prob.astype(BF))
            dk_sum[spot, :] += mm(jnp.concatenate(scores_back, axis=1), both_q)
            dv_sum[spot, :] += mm(jnp.concatenate(probs, axis=1), both_up)
            return tuple(held + mm_tn(keys, back) for held, back in zip(carry, scores_back))

        zero = jnp.zeros((LANES, QB), F32)
        ends = lax.fori_loop(0, count[3], over_context, (zero, zero))
        joined = jnp.concatenate(
            [end[side * size : (side + 1) * size] for side, end in enumerate(ends)]
        )
        dq_ref[rows, :] = (joined.T * scale).astype(BF)
        return 0

    lax.fori_loop(0, count[2], over_queries, 0)

    def out(j, _):
        spot = block(j, CB)
        dk_ref[spot, :] = dk_sum[spot, :].astype(BF)
        dv_ref[spot, :] = dv_sum[spot, :].astype(BF)
        return 0

    lax.fori_loop(0, count[3], out, 0)


def attend_back_call(size, count, queries, keys, values, grads, outs, logs):
    local, model = queries.shape
    total = keys.shape[0]
    pairs = model // LANES

    def column(i, c):
        return (0, i)

    narrow = pl.BlockSpec((local, LANES), column)
    wide = pl.BlockSpec((total, LANES), column)
    return pl.pallas_call(
        functools.partial(attend_back, size),
        grid_spec=pltpu.PrefetchScalarGridSpec(
            num_scalar_prefetch=1,
            grid=(pairs,),
            in_specs=[
                narrow,
                wide,
                wide,
                narrow,
                narrow,
                pl.BlockSpec((None, 8, local), lambda i, c: (i, 0, 0)),
            ],
            out_specs=(narrow, wide, wide),
            scratch_shapes=[pltpu.VMEM((total, LANES), F32)] * 2,
        ),
        out_shape=(shape((local, model), BF), shape((total, model), BF), shape((total, model), BF)),
        compiler_params=params(),
        name="attend_back",
    )(count, queries, keys, values, grads, outs, logs)


def live_rows(i, count):
    return (i * QB + iota((QB, 1), 0) < count[0]).astype(F32)


def row_total(values, live):
    return jnp.sum(jnp.sqrt(jnp.mean(values * values, axis=-1, keepdims=True) + 1e-06) * live)


def gelu_both(value):
    inner = 0.7978845608028654 * (value + 0.044715 * value * value * value)
    bend = jnp.tanh(inner)
    slope = 0.7978845608028654 * (1.0 + 3.0 * 0.044715 * value * value)
    return 0.5 * value * (1.0 + bend), 0.5 * (1.0 + bend) + 0.5 * value * (1.0 - bend * bend) * slope


def feed(group, count, o_ref, h_ref, gains, *rest):
    sources = rest[: 2 if group.direct else 3]
    (h1_out, b_out, z_out, slope_out, h2_out, f_out, stats, w_out, w_up, w_down, sem) = rest[len(sources) :]
    step = pl.program_id(0)
    half = w_out.shape[2]
    hidden = w_up.shape[2]

    @pl.when(step == 0)
    def _():
        group.load(sources, [w_out, w_up, w_down], [sem.at[k] for k in range(3)], count[4], count[5])
        stats[...] = jnp.zeros(stats.shape, F32)
        for k, whole in enumerate((w_out, w_up, w_down)):
            loaded(whole, sem.at[k])

    @pl.when(step < count[2])
    def _():
        live = live_rows(step, count)
        attended = o_ref[...]
        branch = jnp.concatenate([mm(attended, w_out[0]), mm(attended, w_out[1])], axis=1)
        stream1 = h_ref[...] + branch
        h1_out[...] = stream1
        normed = (stream1 * inverse_rms(stream1) * gains[1:2, :]).astype(BF)
        b_out[...] = normed
        for side in range(2):

            def chunk(j, _, side=side):
                value, slope = gelu_both(mm(normed, w_up[side, :, block(j, HC)]))
                z_out[:, block(j + side * (hidden // HC), HC)] = value.astype(BF)
                slope_out[:, block(j + side * (hidden // HC), HC)] = slope.astype(BF)
                return 0

            lax.fori_loop(0, hidden // HC, chunk, 0)
        active = z_out[...]
        branch2 = jnp.concatenate([mm(active, w_down[0]), mm(active, w_down[1])], axis=1)
        stream2 = stream1 + branch2
        h2_out[...] = stream2
        f_out[...] = (stream2 * inverse_rms(stream2) * gains[2:3, :]).astype(BF)
        row = iota(stats.shape, 0)
        stats[...] += (
            jnp.where(row == 0, row_total(stream2, live), 0.0)
            + jnp.where(row == 1, row_total(branch, live), 0.0)
            + jnp.where(row == 2, row_total(branch2, live), 0.0)
        )


def feed_call(group, count, attended, stream0, gains, sources):
    local, model = attended.shape
    whole = group.full_shapes()
    hidden = whole[2][1]

    def rows(i, c):
        return (jnp.minimum(i, c[2] - 1), 0)

    def same(i, c):
        return (0, 0)

    narrow = pl.BlockSpec((QB, model), rows)
    wide = pl.BlockSpec((QB, hidden), rows)
    return pl.pallas_call(
        functools.partial(feed, group),
        grid_spec=pltpu.PrefetchScalarGridSpec(
            num_scalar_prefetch=1,
            grid=(local // QB,),
            in_specs=[narrow, narrow, pl.BlockSpec((8, model), same)] + [anywhere()] * len(sources),
            out_specs=(narrow, narrow, wide, wide, narrow, narrow, pl.BlockSpec((8, LANES), same)),
            scratch_shapes=[pltpu.VMEM(dims, BF) for dims in whole] + [pltpu.SemaphoreType.DMA((3,))],
        ),
        out_shape=(
            shape((local, model), F32),
            shape((local, model), BF),
            shape((local, hidden), BF),
            shape((local, hidden), BF),
            shape((local, model), F32),
            shape((local, model), BF),
            shape((8, LANES), F32),
        ),
        compiler_params=params(),
        name="feed",
    )(count, attended, stream0, gains, *sources)


def head(count, f_ref, t_ref, gains, weight, grad, df_ref, loss, logits, back, flipped):
    chunks = weight.shape[1] // HC
    loss[...] = jnp.zeros(loss.shape, F32)
    model = f_ref.shape[1]

    def over_rows(i, _):
        rows = block(i, QB)
        normed = f_ref[rows, :]
        flipped[:, rows] = normed.astype(F32).T.astype(BF)
        target = t_ref[rows, 0:1].astype(jnp.int32)
        live = live_rows(i, count)

        def column(j):
            return j * HC + iota((QB, HC), 1)

        def first(j, carry):
            top, hit = carry
            value = mm(normed, weight[:, block(j, HC)])
            place = column(j)
            value = jnp.where(place < BINS, value, LOW)
            logits[:, block(j, HC)] = value
            top = jnp.maximum(top, jnp.max(value, axis=1, keepdims=True))
            hit = hit + jnp.sum(jnp.where(place == target, value, 0.0), axis=1, keepdims=True)
            return top, hit

        top, hit = lax.fori_loop(
            0, chunks, first, (jnp.full((QB, 1), 3.0 * LOW, F32), jnp.zeros((QB, 1), F32))
        )

        def second(j, total):
            expo = jnp.exp(logits[:, block(j, HC)] - top)
            logits[:, block(j, HC)] = expo
            return total + jnp.sum(expo, axis=1, keepdims=True)

        total = lax.fori_loop(0, chunks, second, jnp.zeros((QB, 1), F32))
        weightf = live / gains[4:5, 0:1]
        share = 1.0 / total

        def third(j, held):
            hot = (column(j) == target).astype(F32)
            found = ((logits[:, block(j, HC)] * share - hot) * weightf).astype(BF)
            back[rows, block(j, HC)] = found
            return held + mm_nt(found, weight[:, block(j, HC)])

        df_ref[rows, :] = lax.fori_loop(0, chunks, third, jnp.zeros((QB, model), F32))
        loss[...] += jnp.sum(live * (top + jnp.log(total) - hit))
        return 0

    lax.fori_loop(0, count[2], over_rows, 0)

    def over_columns(j, _):
        def add(i, held):
            return held + mm(flipped[:, block(i, QB)], back[block(i, QB), block(j, HC)])

        grad[:, block(j, HC)] = lax.fori_loop(0, count[2], add, jnp.zeros((model, HC), F32)).astype(BF)
        return 0

    lax.fori_loop(0, chunks, over_columns, 0)


def head_call(count, normed, targets, gains, weight):
    local, model = normed.shape
    bins = weight.shape[1]
    return pl.pallas_call(
        head,
        out_shape=(shape((model, bins), BF), shape((local, model), F32), shape((8, LANES), F32)),
        in_specs=[in_smem()] + [in_vmem()] * 4,
        out_specs=(in_vmem(),) * 3,
        scratch_shapes=[
            pltpu.VMEM((QB, bins), F32),
            pltpu.VMEM((local, bins), BF),
            pltpu.VMEM((model, local), BF),
        ],
        compiler_params=params(),
        name="head",
    )(count, normed, targets, gains, weight)


def feed_back(group, count, df_ref, h2_ref, h1_ref, gains, o_any, b_any, z_any, slope_any, *rest):
    sources = rest[: 2 if group.direct else 3]
    rest = rest[len(sources) :]
    targets = rest[: len(group.out_shapes())]
    (
        dh1_out,
        do_out,
        gain_out,
        w_out,
        w_up,
        w_down,
        g_out,
        g_up,
        g_down,
        o_all,
        b_all,
        z_all,
        slope_all,
        dm_all,
        da_all,
        w_sem,
        r_sem,
        g_sem,
    ) = rest[len(targets) :]
    step = pl.program_id(0)
    half = w_out.shape[2]
    hidden = w_up.shape[2]
    per_side = hidden // HC
    rows = block(step, QB)
    loads = ((o_any, o_all), (b_any, b_all), (z_any, z_all), (slope_any, slope_all))

    @pl.when(step == 0)
    def _():
        group.load(sources, [w_out, w_up, w_down], [w_sem.at[k] for k in range(3)], count[4], count[5])
        gain_out[...] = jnp.zeros(gain_out.shape, F32)

        def fetch(i, _):
            for k, (source, target) in enumerate(loads):
                pltpu.make_async_copy(
                    source.at[block(i, QB)], target.at[block(i, QB)], r_sem.at[k, i]
                ).start()
            return 0

        lax.fori_loop(0, count[2], fetch, 0)
        for k, whole in enumerate((w_out, w_up, w_down)):
            loaded(whole, w_sem.at[k])

    @pl.when(step < count[2])
    def _():
        for k, (source, target) in enumerate(loads):
            pltpu.make_async_copy(source.at[rows], target.at[rows], r_sem.at[k, step]).wait()
        back, gain3 = rms_back(h2_ref[...], gains[2:3, :], df_ref[...])
        dm = back.astype(BF)
        dm_all[rows, :] = dm

        for side in range(2):

            def chunk(j, held, side=side):
                spot = block(j + side * per_side, HC)
                upper = mm_nt(dm[:, :half], w_down[0, spot, :]) + mm_nt(dm[:, half:], w_down[1, spot, :])
                found = (upper * slope_all[rows, spot].astype(F32)).astype(BF)
                slope_all[rows, spot] = found
                return held + mm_nt(found, w_up[side, :, block(j, HC)])

            db = lax.fori_loop(
                0, per_side, chunk, jnp.zeros(back.shape, F32) if side == 0 else db
            )
        back1, gain2 = rms_back(h1_ref[...], gains[1:2, :], db)
        stream = back + back1
        dh1_out[...] = stream
        da = stream.astype(BF)
        da_all[rows, :] = da
        do_out[...] = (mm_nt(da[:, :half], w_out[0]) + mm_nt(da[:, half:], w_out[1])).astype(BF)
        row = iota(gain_out.shape, 0)
        gain_out[...] += jnp.where(row == 1, gain2, 0.0) + jnp.where(row == 2, gain3, 0.0)

    @pl.when(step == pl.num_programs(0) - 1)
    def _():
        model = 2 * half

        for side in range(2):

            def columns(j, _, side=side):
                spot = block(j + side * per_side, HC)

                def add_up(i, held):
                    return held + mm_tn(b_all[block(i, QB), :], slope_all[block(i, QB), spot])

                g_up[side, :, block(j, HC)] = lax.fori_loop(
                    0, count[2], add_up, jnp.zeros((model, HC), F32)
                ).astype(BF)

                def add_down(i, held):
                    return held + mm_tn(z_all[block(i, QB), spot], dm_all[block(i, QB), :])

                down = lax.fori_loop(0, count[2], add_down, jnp.zeros((HC, model), F32)).astype(BF)
                g_down[0, spot, :] = down[:, :half]
                g_down[1, spot, :] = down[:, half:]
                return 0

            lax.fori_loop(0, per_side, columns, 0)

        def add_out(i, held):
            return held + mm_tn(o_all[block(i, QB), :], da_all[block(i, QB), :])

        whole = lax.fori_loop(0, count[2], add_out, jnp.zeros((model, model), F32)).astype(BF)
        g_out[0] = whole[:, :half]
        g_out[1] = whole[:, half:]
        sems = [g_sem.at[k] for k in range(len(targets))]
        group.store([g_out, g_up, g_down], targets, sems, count[4], count[5])
        group.stored(targets, sems)


def feed_back_call(group, count, df, stream2, stream1, gains, attended, normed, active, slope, sources):
    local, model = df.shape
    whole = group.full_shapes()
    hidden = whole[2][1]
    outs = group.out_shapes()

    def rows(i, c):
        return (jnp.minimum(i, c[2] - 1), 0)

    def same(i, c):
        return (0, 0)

    narrow = pl.BlockSpec((QB, model), rows)
    return pl.pallas_call(
        functools.partial(feed_back, group),
        grid_spec=pltpu.PrefetchScalarGridSpec(
            num_scalar_prefetch=1,
            grid=(local // QB,),
            in_specs=[narrow, narrow, narrow, pl.BlockSpec((8, model), same)]
            + [anywhere()] * (4 + len(sources)),
            out_specs=(anywhere(),) * len(outs) + (narrow, narrow, pl.BlockSpec((8, model), same)),
            scratch_shapes=[pltpu.VMEM(dims, BF) for dims in whole] * 2
            + [
                pltpu.VMEM((local, model), BF),
                pltpu.VMEM((local, model), BF),
                pltpu.VMEM((local, hidden), BF),
                pltpu.VMEM((local, hidden), BF),
                pltpu.VMEM((local, model), BF),
                pltpu.VMEM((local, model), BF),
                pltpu.SemaphoreType.DMA((3,)),
                pltpu.SemaphoreType.DMA((4, local // QB)),
                pltpu.SemaphoreType.DMA((3,)),
            ],
        ),
        out_shape=tuple(outs)
        + (shape((local, model), F32), shape((local, model), BF), shape((8, model), F32)),
        compiler_params=params(),
        name="feed_back",
    )(count, df, stream2, stream1, gains, attended, normed, active, slope, *sources)


def project_back(
    group, count, dq, aq, xq, dh1, h0, dk, dv, ac, xc, yc, gains, gains23, *rest
):
    sources = rest[: 2 if group.direct else 1]
    rest = rest[len(sources) :]
    targets = rest[: len(group.out_shapes())]
    weight, total, emb, small, out, sem, g_sem = rest[len(targets) :]
    step = pl.program_id(0)
    steps = pl.num_programs(0)
    blocks_q = steps - 4
    third = dq.shape[1] // 2

    @pl.when(step == 0)
    def _():
        group.load(sources, [weight], [sem.at[0]], count[4], count[5])
        total[...] = jnp.zeros(total.shape, F32)
        emb[...] = jnp.zeros(emb.shape, F32)
        small[...] = gains23[...]
        loaded(weight, sem.at[0])

    row = iota(small.shape, 0)

    @pl.when(step < count[2])
    def _():
        upper = jnp.zeros(dh1.shape, F32)
        a = aq[...]
        for side in range(2):
            grad = dq[:, side * third : (side + 1) * third]
            upper += mm_nt(grad, weight[side, :, :third])
            total[side, :, :third] += mm_tn(a, grad)
        back, gain1 = rms_back(h0[...], gains[0:1, :], upper)
        stream = dh1[...] + back
        emb[...] += mm_tn(stream.astype(BF), xq[...])
        small[...] += jnp.where(row == 0, gain1, 0.0)

    @pl.when((step >= blocks_q) & (step < blocks_q + count[3]))
    def _():
        a = ac[...]
        label = yc[:, 0:1]
        stream = mm_nt(xc[...], weight[0, :, 3 * third :]) + label * gains[3:4, :]
        upper = jnp.zeros(stream.shape, F32)
        for side in range(2):
            for part, ref in enumerate((dk, dv)):
                grad = ref[:, side * third : (side + 1) * third]
                columns = slice((part + 1) * third, (part + 2) * third)
                upper += mm_nt(grad, weight[side, :, columns])
                total[side, :, columns] += mm_tn(a, grad)
        back, gain1 = rms_back(stream, gains[0:1, :], upper)
        emb[...] += mm_tn(back.astype(BF), xc[...])
        small[...] += jnp.where(row == 0, gain1, 0.0) + jnp.where(
            row == 3, jnp.sum(label * back, axis=0, keepdims=True), 0.0
        )

    @pl.when(step == steps - 1)
    def _():
        for side in range(2):
            for part in range(3):
                columns = slice(part * third, (part + 1) * third)
                out[side, :, columns] = total[side, :, columns].astype(BF)
        out[0, :, 3 * third :] = emb[...].astype(BF)
        padded = jnp.concatenate([small[...], jnp.zeros((LANES - 8, small.shape[1]), F32)])
        out[1, :, 3 * third :] = padded.T.astype(BF)
        sems = [g_sem.at[k] for k in range(len(targets))]
        group.store([out], targets, sems, count[4], count[5])
        group.stored(targets, sems)


def project_back_call(group, count, dq, aq, xq, dh1, h0, dk, dv, ac, xc, yc, gains, gains23, sources):
    local, model = dq.shape
    total = dk.shape[0]
    blocks_q, blocks_c = local // QB, total // CB
    outs = group.out_shapes()

    def q_map(i, c):
        return (jnp.minimum(i, c[2] - 1), 0)

    def c_map(i, c):
        return (jnp.clip(i - blocks_q, 0, c[3] - 1), 0)

    def same(i, c):
        return (0, 0)

    query = pl.BlockSpec((QB, model), q_map)
    context = pl.BlockSpec((CB, model), c_map)
    thin = pl.BlockSpec((CB, LANES), c_map)
    fixed = pl.BlockSpec((8, model), same)
    whole = group.full_shapes()[0]
    return pl.pallas_call(
        functools.partial(project_back, group),
        grid_spec=pltpu.PrefetchScalarGridSpec(
            num_scalar_prefetch=1,
            grid=(blocks_q + blocks_c,),
            in_specs=[
                query,
                query,
                pl.BlockSpec((QB, LANES), q_map),
                query,
                query,
                context,
                context,
                context,
                thin,
                thin,
                fixed,
                fixed,
            ]
            + [anywhere()] * len(sources),
            out_specs=(anywhere(),) * len(outs),
            scratch_shapes=[
                pltpu.VMEM(whole, BF),
                pltpu.VMEM((2, whole[1], whole[2] - LANES), F32),
                pltpu.VMEM((model, LANES), F32),
                pltpu.VMEM((8, model), F32),
                pltpu.VMEM(whole, BF),
                pltpu.SemaphoreType.DMA((1,)),
                pltpu.SemaphoreType.DMA((2,)),
            ],
        ),
        out_shape=tuple(outs),
        compiler_params=params(),
        name="project_back",
    )(count, dq, aq, xq, dh1, h0, dk, dv, ac, xc, yc, gains, gains23, *sources)


def halves(tab, mine):
    other = swap(mine, "tab", 0)
    return jnp.where(tab == 0, mine, other), jnp.where(tab == 0, other, mine)


def on_device(
    count_fsdp,
    features,
    feature_counts,
    row_flags,
    target_bins,
    emb_weight,
    qkv_weight,
    out_weight,
    up_weight,
    down_weight,
    head_weight,
    vectors,
    mom_emb,
    mom_qkv,
    mom_out,
    mom_up,
    mom_down,
    mom_head,
    mom_vectors,
    ema_emb,
    ema_qkv,
    ema_out,
    ema_up,
    ema_down,
    ema_head,
    ema_vectors,
):
    masters = (emb_weight, qkv_weight, out_weight, up_weight, down_weight, head_weight, vectors)
    moms = (mom_emb, mom_qkv, mom_out, mom_up, mom_down, mom_head, mom_vectors)
    emas = (ema_emb, ema_qkv, ema_out, ema_up, ema_down, ema_head, ema_vectors)
    me = lax.axis_index("fsdp").astype(jnp.int32)
    tab = lax.axis_index("tab").astype(jnp.int32)
    local, nfeat = features.shape[1:]
    total = 2 * local
    rows = qkv_weight.shape[0]
    model = rows * count_fsdp
    half = model // 2
    hidden_half = up_weight.shape[1] // 2
    down_blocks = down_weight.shape[0] // rows
    size = model // HEADS
    flags = row_flags[0]
    targets = target_bins[0]

    high_bits = [1 << k for k in reversed(range(1, count_fsdp.bit_length() - 1))]
    group_a = Group(high_bits[:-1] + ["tab", high_bits[-1]], rows, [(3 * half + LANES, 1)], count_fsdp)
    group_b = Group(
        high_bits + ["tab"], rows, [(half, 1), (hidden_half, 1), (half, down_blocks)], count_fsdp
    )

    def side_of(weight, width):
        return jnp.where(tab == 0, weight[:, :width], weight[:, width : 2 * width])

    queries_here = jnp.sum(flags)
    marks = jnp.stack([queries_here // 32, queries_here % 32]).astype(F32)
    first_row = (jnp.arange(rows) == 0).astype(F32)[:, None]

    def tail(block_t):
        used = block_t.shape[0]
        return jnp.concatenate(
            [block_t.T, first_row * marks[None, :], jnp.zeros((rows, LANES - 2 - used), F32)], axis=1
        )

    piece_a = jnp.concatenate(
        [side_of(qkv_weight[:, k * model : (k + 1) * model], half) for k in range(3)]
        + [jnp.where(tab == 0, tail(emb_weight), tail(vectors))],
        axis=1,
    ).astype(BF)
    down_side = side_of(down_weight, half)
    piece_b = jnp.concatenate(
        [side_of(out_weight, half), side_of(up_weight, hidden_half)]
        + [down_side[k * rows : (k + 1) * rows] for k in range(down_blocks)],
        axis=1,
    ).astype(BF)
    bins = -(-head_weight.shape[1] // HC) * HC
    spare = bins - head_weight.shape[1]
    piece_h = jnp.pad(head_weight.astype(BF), ((0, 0), (0, spare)))

    near_a, far_a = gather_group(group_a, piece_a)
    near_b, far_b = gather_group(group_b, piece_b)
    head_full = lax.all_gather(piece_h, "fsdp", axis=0, tiled=True)

    pack = jnp.concatenate(
        [
            features[0],
            jnp.stack([flags, targets // 64, targets % 64], axis=1).astype(BF),
            jnp.zeros((local, LANES - 3 - nfeat), BF),
        ],
        axis=1,
    )
    lower, upper = halves(tab, pack)
    table = jnp.concatenate([lower, upper])
    flag_rows = table[:, nfeat].astype(F32).reshape(total // LANES, LANES)
    asked = jnp.sum(flag_rows).astype(jnp.int32)
    here = (asked - tab + 1) // 2
    known = total - asked
    count = jnp.stack(
        [
            here,
            known,
            jnp.maximum((here + QB - 1) // QB, 1),
            (known + CB - 1) // CB,
            me,
            tab,
            feature_counts[0],
            jnp.int32(0),
        ]
    )
    x_query, t_query, x_context, y_context = sort_rows_call(nfeat, count, table, flag_rows)

    sources_a = group_a.sources(near_a, far_a, me, tab)
    sources_b = group_b.sources(near_b, far_b, me, tab)
    queries, keys, values, a_query, a_context, stream0, gains = project_call(
        group_a, nfeat, count, x_query, x_context, y_context, sources_a, model
    )
    attended, logs = attend_call(size, count, queries, keys, values)
    stream1, normed2, active, slope, stream2, normed3, stats = feed_call(
        group_b, count, attended, stream0, gains, sources_b
    )
    grad_head, df, loss = head_call(count, normed3, t_query, gains, head_full)
    shard_h = lax.optimization_barrier(
        lax.psum_scatter(grad_head, "fsdp", scatter_dimension=0, tiled=True)
    )
    *outs_b, dh1, grad_o, gains23 = feed_back_call(
        group_b, count, df, stream2, stream1, gains, attended, normed2, active, slope, sources_b
    )
    shard_b = scatter_group(group_b, *group_b.targets(outs_b, me, tab))
    dq, dk, dv = attend_back_call(size, count, queries, keys, values, grad_o, attended, logs)
    outs_a = project_back_call(
        group_a,
        count,
        dq,
        a_query,
        x_query,
        dh1,
        stream0,
        dk,
        dv,
        a_context,
        x_context,
        y_context,
        gains,
        gains23,
        sources_a,
    )
    shard_a = scatter_group(group_a, *group_a.targets(outs_a, me, tab))

    shard_h = shard_h[:, : head_weight.shape[1]]
    grad_h = shard_h.astype(F32) + swap(shard_h, "tab", 0).astype(F32)
    a0, a1 = halves(tab, shard_a)
    b0, b1 = halves(tab, shard_b)
    grad_qkv = jnp.concatenate(
        [side[:, k * half : (k + 1) * half] for k in range(3) for side in (a0, a1)], axis=1
    )
    grad_emb = a0[:, 3 * half : 3 * half + nfeat].T
    grad_vectors = a1[:, 3 * half : 3 * half + vectors.shape[0]].T
    grad_out = jnp.concatenate([b0[:, :half], b1[:, :half]], axis=1)
    grad_up = jnp.concatenate([side[:, half : half + hidden_half] for side in (b0, b1)], axis=1)
    start = half + hidden_half
    grad_down = jnp.concatenate(
        [
            jnp.concatenate([side[:, start + k * half : start + (k + 1) * half] for side in (b0, b1)], axis=1)
            for k in range(down_blocks)
        ]
    )
    summed = (grad_emb, grad_qkv, grad_out, grad_up, grad_down, grad_h, grad_vectors)
    keep_a = jnp.where(
        jnp.arange(shard_a.shape[1])[None, :] < 3 * half + jnp.where(tab == 0, nfeat, vectors.shape[0]),
        shard_a,
        0.0,
    )
    squares = jnp.sum(keep_a * keep_a) + jnp.sum(shard_b * shard_b) + 0.5 * jnp.sum(grad_h * grad_h)
    sums = jnp.concatenate([loss[0:1, 0:1], stats[0:3, 0:1], squares.reshape(1, 1)]).reshape(1, 5)
    sums = jnp.broadcast_to(jnp.pad(sums, ((0, 0), (0, LANES - 5))), (8, LANES))
    for step in [1] + high_bits + ["tab"]:
        sums = sums + swap(sums, step, count_fsdp)
    loss_sum = sums[0, 0]
    rms_sums = sums[0, 1:4]
    clip_norm = jnp.sqrt(sums[0, 4])
    row_count = gains[4, 0]
    factor = jnp.minimum(1.0, CLIP / clip_norm)
    new_moms, new_weights, new_emas = ([], [], [])
    for weight, grad, moment, average in zip(masters, summed, moms, emas):
        clipped = grad * factor
        moment_new = MOMENTUM * moment + clipped
        weight_new = weight - RATE * (clipped + MOMENTUM * moment_new)
        new_moms.append(moment_new)
        new_weights.append(weight_new)
        new_emas.append(AVERAGE * average + (1.0 - AVERAGE) * weight_new)
    return (loss_sum, row_count, rms_sums, clip_norm, *new_moms, *new_weights, *new_emas)


def solution(mesh):
    by_row, by_column = P("fsdp", None), P(None, "fsdp")
    weights = (by_column, by_row, by_row, by_row, by_row, by_row, by_column)
    return jax.shard_map(
        functools.partial(on_device, mesh.shape["fsdp"]),
        mesh=mesh,
        in_specs=(P("fsdp", "tab", None), P("fsdp"), P("fsdp", "tab"), P("fsdp", "tab")) + weights * 3,
        out_specs=(P(), P(), P(), P()) + weights * 3,
        check_vma=False,
    )
```

```python
import functools

import jax
import jax.numpy as jnp
import numpy as np
from jax import lax
from jax.experimental import pallas as pl
from jax.experimental.pallas import tpu as pltpu
from jax.sharding import PartitionSpec as P

HEADS = 12
BINS = 5000
CLIP = 0.005
RATE = 10000.0
MOMENTUM = 0.5
AVERAGE = 0.5

BF = jnp.bfloat16
F32 = jnp.float32
LANES = 128
QB = 256
AB = 256
FB = 256
RB = 512
CB = 512
HC = 512
VMEM = 60 * 1024 * 1024
LOW = -1e30


def mm(left, right):
    return jnp.dot(left, right, preferred_element_type=F32)


def mm_tn(left, right):
    return lax.dot_general(left, right, (((0,), (0,)), ((), ())), preferred_element_type=F32)


def mm_nt(left, right):
    return lax.dot_general(left, right, (((1,), (1,)), ((), ())), preferred_element_type=F32)


def iota(shape, axis):
    return lax.broadcasted_iota(jnp.int32, shape, axis)


def block(index, size):
    return pl.ds(pl.multiple_of(index * size, size), size)


def inverse_rms(stream):
    return lax.rsqrt(jnp.mean(stream * stream, axis=-1, keepdims=True) + 1e-06)


def rms_back(stream, gain, upstream):
    scale = inverse_rms(stream)
    unit = stream * scale
    weighted = upstream * gain
    back = scale * (weighted - unit * jnp.mean(weighted * unit, axis=-1, keepdims=True))
    return back, jnp.sum(upstream * unit, axis=0, keepdims=True)


def params():
    return pltpu.CompilerParams(vmem_limit_bytes=VMEM)


def cost(flops):
    return pl.CostEstimate(flops=int(flops), bytes_accessed=1 << 20, transcendentals=0)


def anywhere():
    return pl.BlockSpec(memory_space=pl.ANY)


def in_vmem():
    return pl.BlockSpec(memory_space=pltpu.VMEM)


def in_smem():
    return pl.BlockSpec(memory_space=pltpu.SMEM)


def shape(dims, dtype):
    return jax.ShapeDtypeStruct(dims, dtype)


class Group:
    def __init__(self, axis_bits, rows, parts, count):
        self.steps = axis_bits
        self.rows = rows
        self.parts = parts
        self.count = count
        self.width = sum(width * blocks for width, blocks in parts)
        self.pieces = 2 ** len(axis_bits)
        self.direct = rows % 16 == 0

    def place(self, piece, core):
        across, half = core, 0
        for bit, step in enumerate(self.steps):
            if piece >> bit & 1:
                if step == "tab":
                    half ^= 1
                else:
                    across ^= step
        return across, half

    def spans(self):
        start = 0
        for part, (width, blocks) in enumerate(self.parts):
            for at in range(blocks):
                yield part, start, width, at, blocks
                start += width

    def full_shapes(self):
        return [(self.count * self.rows * blocks, 2 * width) for width, blocks in self.parts]

    def table(self):
        order = np.zeros((self.count, 2), np.int32)
        for core in range(2):
            for piece in range(self.pieces):
                across, half = self.place(piece, core)
                order[across, half] = core * self.pieces + piece
        return order

    def to_whole(self, near, far, me, tab):
        places = np.arange(self.count, dtype=np.int32)[:, None] ^ me
        sides = np.arange(2, dtype=np.int32)[None, :] ^ tab
        index = jnp.asarray(self.table())[places, sides]
        every = jnp.take(jnp.concatenate([near, far]), index, axis=0)
        every = every.transpose(0, 2, 1, 3)
        whole = [[] for _ in self.parts]
        for part, start, width, _, _ in self.spans():
            whole[part].append(every[..., start : start + width])
        return [
            jnp.stack(found, axis=1).reshape(dims) for found, dims in zip(whole, self.full_shapes())
        ]

    def to_pieces(self, wholes, me, tab):
        columns = []
        for part, _, width, at, blocks in self.spans():
            split = wholes[part].reshape(self.count, blocks, self.rows, 2, width)
            columns.append(split[:, at])
        every = jnp.concatenate(columns, axis=-1).transpose(0, 2, 1, 3)
        every = every.reshape(2 * self.count, self.rows, self.width)
        where = np.array(
            [self.place(piece, core) for core in range(2) for piece in range(self.pieces)], np.int32
        )
        index = (where[:, 0] ^ me) * 2 + (where[:, 1] ^ tab)
        found = jnp.take(every, index, axis=0)
        return found[: self.pieces], found[self.pieces :]

    def pairs(self, wholes, moved, me, tab):
        for core in range(2):
            for piece in range(self.pieces):
                across, half = self.place(piece, core)
                shard = lax.bitwise_xor(me, jnp.int32(across))
                side = lax.bitwise_xor(tab, jnp.int32(half))
                for part, start, width, at, blocks in self.spans():
                    first = pl.multiple_of((shard * blocks + at) * self.rows, self.rows)
                    column = pl.multiple_of(side * width, LANES)
                    yield (
                        wholes[part].at[pl.ds(first, self.rows), pl.ds(column, width)],
                        moved[core].at[piece, :, pl.ds(start, width)],
                        part,
                        core,
                    )

    def load(self, sources, wholes, sems, me, tab):
        if not self.direct:
            for source, whole, sem in zip(sources, wholes, sems):
                pltpu.make_async_copy(source, whole, sem).start()
            return
        for whole, piece, part, _ in self.pairs(wholes, sources, me, tab):
            pltpu.make_async_copy(piece, whole, sems[part]).start()

    def store(self, wholes, targets, sems, me, tab):
        if not self.direct:
            for whole, target, sem in zip(wholes, targets, sems):
                pltpu.make_async_copy(whole, target, sem).start()
            return
        for whole, piece, _, core in self.pairs(wholes, targets, me, tab):
            pltpu.make_async_copy(whole, piece, sems[core]).start()

    def stored(self, targets, sems):
        for target, sem in zip(targets, sems):
            pltpu.make_async_copy(target, target, sem).wait()

    def out_shapes(self):
        if self.direct:
            return [shape((self.pieces, self.rows, self.width), BF)] * 2
        return [shape(dims, BF) for dims in self.full_shapes()]

    def sources(self, near, far, me, tab):
        return [near, far] if self.direct else self.to_whole(near, far, me, tab)

    def targets(self, outs, me, tab):
        return tuple(outs) if self.direct else self.to_pieces(outs, me, tab)


def loaded(whole, sem):
    pltpu.make_async_copy(whole, whole, sem).wait()


def swap(value, step, count):
    if step == "tab":
        return lax.ppermute(value, "tab", [(0, 1), (1, 0)])
    return lax.ppermute(value, "fsdp", [(i, i ^ step) for i in range(count)])


def after(value, *others):
    return lax.optimization_barrier((value, others))[0]


def gather_step(groups, held, at, *first):
    found = [swap(value, group.steps[at], group.count) for group, value in zip(groups, held)]
    found = after(found, *first)
    return [jnp.concatenate(both) for both in zip(held, found)]


def scatter_step(groups, held, at, *first):
    size = held[0].shape[0] // 2
    found = [swap(value[size:], group.steps[at], group.count) for group, value in zip(groups, held)]
    found = after(found, *first)
    kind = F32 if size == 1 else BF
    return [
        (value[:size].astype(F32) + other.astype(F32)).astype(kind) for value, other in zip(held, found)
    ]


def sort_rows(nfeat, count, table, marks, x_query, t_query, x_context, y_context):
    total, _ = table.shape
    rows = total // LANES
    flags = marks[...]
    inside = mm(flags.astype(BF), (iota((LANES, LANES), 0) <= iota((LANES, LANES), 1)).astype(F32).astype(BF))
    sums = jnp.broadcast_to(jnp.sum(flags, axis=1, keepdims=True), (rows, LANES))
    below = (iota((rows, rows), 1) < iota((rows, rows), 0)).astype(F32)
    upto = inside + mm(below.astype(BF), sums.astype(BF))
    spot = (iota((rows, LANES), 0) * LANES + iota((rows, LANES), 1)).astype(F32)
    as_query = jnp.where(flags > 0, upto - 1.0, -1.0)
    as_context = jnp.where(flags > 0, -1.0, spot - upto)
    held = count[6]
    scale = jnp.sqrt(F32(nfeat) / jnp.full((1, LANES), held, jnp.int32).astype(F32))

    def pick(rank, dest):
        hot = jnp.concatenate(
            [(rank[k : k + 1, :] == dest).astype(F32).astype(BF) for k in range(rows)], axis=1
        )
        found = mm(hot, table[...])
        kept = jnp.where(iota(found.shape, 1) < held, found * scale, 0.0).astype(BF)
        return kept, found[:, nfeat + 1 : nfeat + 2] * 64.0 + found[:, nfeat + 2 : nfeat + 3]

    def query(i, _):
        dest = (2 * (i * QB + iota((QB, LANES), 0)) + count[5]).astype(F32)
        kept, target = pick(as_query, dest)
        x_query[block(i, QB), :] = kept
        t_query[block(i, QB), :] = jnp.broadcast_to(target, (QB, LANES))
        return 0

    def context(i, _):
        dest = i * QB + iota((QB, LANES), 0)
        kept, target = pick(as_context, dest.astype(F32))
        x_context[block(i, QB), :] = kept
        label = (jnp.broadcast_to(target, (QB, LANES)) + 0.5) * (2.0 / BINS) - 1.0
        y_context[block(i, QB), :] = jnp.where(dest < count[1], label, 0.0)
        return 0

    lax.fori_loop(0, count[2] * (RB // QB), query, 0)
    lax.fori_loop(0, count[3] * (CB // QB), context, 0)


def sort_rows_call(nfeat, count, table, marks):
    total = table.shape[0]
    local = total // 2
    return pl.pallas_call(
        functools.partial(sort_rows, nfeat),
        out_shape=(
            shape((local, LANES), BF),
            shape((local, LANES), F32),
            shape((total, LANES), BF),
            shape((total, LANES), F32),
        ),
        in_specs=[in_smem(), in_vmem(), in_vmem()],
        out_specs=(in_vmem(),) * 4,
        compiler_params=params(),
        cost_estimate=cost(7e9),
        name="sort_rows",
    )(count, table, marks)


def project(nfeat, blocks, count, x_query, x_context, y_context, weight, q_out, k_out, v_out, aq_out, ac_out, h_out, gains):
    step = pl.program_id(0)
    model = q_out.shape[1]
    embed = slice(3 * model, 3 * model + LANES)

    @pl.when(step == 0)
    def _():
        vectors = weight[:, 3 * model + LANES :].astype(F32).T
        many = jnp.sum(vectors[4:5, :]) * 32.0 + jnp.sum(vectors[5:6, :])
        gains[...] = jnp.where(iota((8, model), 0) < 4, vectors[:8, :], many)

    def normed(stream):
        return (stream * inverse_rms(stream) * gains[0:1, :]).astype(BF)

    @pl.when(step < count[2])
    def _():
        stream = mm_nt(x_query[...], weight[:, embed])
        h_out[...] = stream
        a = normed(stream)
        aq_out[...] = a
        q_out[...] = mm(a, weight[:, :model]).astype(BF)

    @pl.when((step >= blocks) & (step < blocks + count[3]))
    def _():
        stream = mm_nt(x_context[...], weight[:, embed]) + y_context[:, 0:1] * gains[3:4, :]
        a = normed(stream)
        ac_out[...] = a
        k_out[...] = mm(a, weight[:, model : 2 * model]).astype(BF)
        v_out[...] = mm(a, weight[:, 2 * model : 3 * model]).astype(BF)


def project_call(nfeat, count, x_query, x_context, y_context, weight):
    local, total = x_query.shape[0], x_context.shape[0]
    model = weight.shape[0]
    blocks_q, blocks_c = local // RB, total // CB

    def q_map(i, c):
        return (jnp.minimum(i, c[2] - 1), 0)

    def c_map(i, c):
        return (jnp.clip(i - blocks_q, 0, c[3] - 1), 0)

    def same(i, c):
        return (0, 0)

    return pl.pallas_call(
        functools.partial(project, nfeat, blocks_q),
        grid_spec=pltpu.PrefetchScalarGridSpec(
            num_scalar_prefetch=1,
            grid=(blocks_q + blocks_c,),
            in_specs=[
                pl.BlockSpec((RB, LANES), q_map),
                pl.BlockSpec((CB, LANES), c_map),
                pl.BlockSpec((CB, LANES), c_map),
                pl.BlockSpec(weight.shape, same),
            ],
            out_specs=(
                pl.BlockSpec((RB, model), q_map),
                pl.BlockSpec((CB, model), c_map),
                pl.BlockSpec((CB, model), c_map),
                pl.BlockSpec((RB, model), q_map),
                pl.BlockSpec((CB, model), c_map),
                pl.BlockSpec((RB, model), q_map),
                pl.BlockSpec((8, model), same),
            ),
        ),
        out_shape=(
            shape((local, model), BF),
            shape((total, model), BF),
            shape((total, model), BF),
            shape((local, model), BF),
            shape((total, model), BF),
            shape((local, model), F32),
            shape((8, model), F32),
        ),
        compiler_params=params(),
        cost_estimate=cost(12e9),
        name="project",
    )(count, x_query, x_context, y_context, weight)


def head_masks(size):
    low = (iota((1, LANES), 1) < size).astype(F32)
    return low.astype(BF), (1.0 - low).astype(BF)


def dead_rows(j, count):
    return jnp.where(j * CB + iota((CB, 1), 0) < count[1], 0.0, LOW)


def clear_rest(ref, count):
    def clear(i, _):
        ref[block(i, QB), :] = jnp.zeros((QB, ref.shape[1]), ref.dtype)
        return 0

    lax.fori_loop(count[7], count[2] * (RB // QB), clear, 0)


def over_blocks(count, total, body):
    for blocks in range(1, total // CB + 1):

        @pl.when(count[3] == blocks)
        def _(blocks=blocks):
            body(blocks)


def context_scores(k_ref, head, blocks, count):
    scores = mm_nt(k_ref[: blocks * CB, :], head)
    tail = scores[-CB:] + dead_rows(blocks - 1, count)
    return tail if blocks == 1 else jnp.concatenate([scores[:-CB], tail])


def attend(size, count, q_ref, k_ref, v_ref, o_ref, lse_ref, v_low, v_high):
    scale = size ** (-0.5)
    masks = head_masks(size)

    def body(blocks):
        live = slice(0, blocks * CB)
        v_low[live, :] = v_ref[live, :] * masks[0] + masks[1]
        v_high[live, :] = v_ref[live, :] * masks[1] + masks[0]

        def over_queries(i, _):
            queries = q_ref[block(i, QB), :] * BF(scale)
            heads = [queries * mask for mask in masks]
            joined = []
            spots = [slice(j * AB, (j + 1) * AB) for j in range(blocks * CB // AB)]
            dead = dead_rows(blocks - 1, count)
            scores = [[mm_nt(k_ref[spot, :], head) for spot in spots] for head in heads]
            for side, parts in enumerate(scores):
                for k in range(CB // AB):
                    at = len(spots) - CB // AB + k
                    parts[at] = parts[at] + dead[k * AB : (k + 1) * AB]
                top = functools.reduce(jnp.maximum, [jnp.max(part, axis=0, keepdims=True) for part in parts])
                sums = jnp.zeros((LANES, QB), F32)
                for spot, part in zip(spots, parts):
                    expo = jnp.exp(part - top)
                    sums = sums + mm_tn((v_low, v_high)[side][spot, :], expo.astype(BF))
                total = sums[(1 - side) * size : (1 - side) * size + 1]
                joined.append((sums * (1.0 / total))[side * size : (side + 1) * size])
                lse_ref[side : side + 1, block(i, QB)] = top + jnp.log(total)
            o_ref[block(i, QB), :] = jnp.concatenate(joined).T.astype(BF)
            return 0

        lax.fori_loop(0, count[7], over_queries, 0)

    over_blocks(count, k_ref.shape[0], body)
    clear_rest(o_ref, count)


def attend_call(size, count, queries, keys, values):
    local, model = queries.shape
    total = keys.shape[0]
    pairs = model // LANES

    def column(i, c):
        return (0, i)

    return pl.pallas_call(
        functools.partial(attend, size),
        grid_spec=pltpu.PrefetchScalarGridSpec(
            num_scalar_prefetch=1,
            grid=(pairs,),
            in_specs=[
                pl.BlockSpec((local, LANES), column),
                pl.BlockSpec((total, LANES), column),
                pl.BlockSpec((total, LANES), column),
            ],
            out_specs=(
                pl.BlockSpec((local, LANES), column),
                pl.BlockSpec((None, 8, local), lambda i, c: (i, 0, 0)),
            ),
            scratch_shapes=[pltpu.VMEM((total, LANES), BF)] * 2,
        ),
        out_shape=(shape((local, model), BF), shape((pairs, 8, local), F32)),
        compiler_params=params(),
        cost_estimate=cost(35e9),
        name="attend",
    )(count, queries, keys, values)


def attend_back(size, count, q_ref, k_ref, v_ref, do_ref, o_ref, lse_ref, dq_ref, dk_ref, dv_ref, dk_sum, dv_sum):
    scale = size ** (-0.5)
    masks = head_masks(size)

    def body(blocks):
        def over_queries(i, _):
            rows = block(i, QB)
            queries = q_ref[rows, :] * BF(scale)
            grads = do_ref[rows, :]
            heads = [queries * mask for mask in masks]
            ups = [grads * mask for mask in masks]
            both_q = jnp.concatenate(heads)
            both_up = jnp.concatenate(ups)
            product = (grads.astype(F32) * o_ref[rows, :].astype(F32)).T
            back, probs, joined = [], [], []
            live = slice(0, blocks * CB)
            for side, head in enumerate(heads):
                delta = jnp.sum(product[side * size : (side + 1) * size], axis=0, keepdims=True)
                prob = jnp.exp(context_scores(k_ref, head, blocks, count) - lse_ref[side : side + 1, rows])
                upper = mm_nt(v_ref[live, :], ups[side])
                found = (prob * (upper - delta)).astype(BF)
                joined.append(mm_tn(k_ref[live, :], found)[side * size : (side + 1) * size])
                back.append(found)
                probs.append(prob.astype(BF))
            dq_ref[rows, :] = (jnp.concatenate(joined).T * scale).astype(BF)

            dk = mm(jnp.concatenate(back, axis=1), both_q)
            dv = mm(jnp.concatenate(probs, axis=1), both_up)
            dk_sum[live, :] = jnp.where(i == 0, 0.0, dk_sum[live, :]) + dk
            dv_sum[live, :] = jnp.where(i == 0, 0.0, dv_sum[live, :]) + dv
            return 0

        lax.fori_loop(0, count[7], over_queries, 0)

    over_blocks(count, k_ref.shape[0], body)
    clear_rest(dq_ref, count)

    def out(j, _):
        spot = block(j, CB)
        dk_ref[spot, :] = dk_sum[spot, :].astype(BF)
        dv_ref[spot, :] = dv_sum[spot, :].astype(BF)
        return 0

    lax.fori_loop(0, count[3], out, 0)


def attend_back_call(size, count, queries, keys, values, grads, outs, logs):
    local, model = queries.shape
    total = keys.shape[0]
    pairs = model // LANES

    def column(i, c):
        return (0, i)

    narrow = pl.BlockSpec((local, LANES), column)
    wide = pl.BlockSpec((total, LANES), column)
    return pl.pallas_call(
        functools.partial(attend_back, size),
        grid_spec=pltpu.PrefetchScalarGridSpec(
            num_scalar_prefetch=1,
            grid=(pairs,),
            in_specs=[
                narrow,
                wide,
                wide,
                narrow,
                narrow,
                pl.BlockSpec((None, 8, local), lambda i, c: (i, 0, 0)),
            ],
            out_specs=(narrow, wide, wide),
            scratch_shapes=[pltpu.VMEM((total, LANES), F32)] * 2,
        ),
        out_shape=(shape((local, model), BF), shape((total, model), BF), shape((total, model), BF)),
        compiler_params=params(),
        cost_estimate=cost(35e9),
        name="attend_back",
    )(count, queries, keys, values, grads, outs, logs)


def live_rows(i, count, size=RB):
    return (i * size + iota((size, 1), 0) < count[0]).astype(F32)


def row_total(values, live):
    return jnp.sum(jnp.sqrt(jnp.mean(values * values, axis=-1, keepdims=True) + 1e-06) * live)


def gelu_both(value):
    inner = 0.7978845608028654 * (value + 0.044715 * value * value * value)
    bend = jnp.tanh(inner)
    slope = 0.7978845608028654 * (1.0 + 3.0 * 0.044715 * value * value)
    return 0.5 * value * (1.0 + bend), 0.5 * (1.0 + bend) + 0.5 * value * (1.0 - bend * bend) * slope


def load_feed(groups, sources, wholes, sem, count):
    first, second = groups
    split = 2
    first.load(sources[:split], wholes[:2], [sem.at[0], sem.at[1]], count[4], count[5])
    second.load(sources[split:], wholes[2:], [sem.at[2]], count[4], count[5])


def feed(groups, count, o_ref, h_ref, gains, *rest):
    sources = rest[: 4 if groups[0].direct else 3]
    (h1_out, b_out, z_out, slope_out, h2_out, f_out, stats, w_out, w_up, w_down, sem) = rest[len(sources) :]
    step = pl.program_id(0)
    hidden = w_up.shape[1]

    @pl.when(step == 0)
    def _():
        load_feed(groups, sources, [w_out, w_up, w_down], sem, count)
        stats[...] = jnp.zeros(stats.shape, F32)

    def need(k):
        @pl.when(step == 0)
        def _():
            loaded((w_out, w_up, w_down)[k], sem.at[k])

    @pl.when(step < count[2] * (RB // FB))
    def _():
        live = live_rows(step, count, FB)
        attended = o_ref[...]
        need(0)
        branch = mm(attended, w_out[...])
        stream1 = h_ref[...] + branch
        h1_out[...] = stream1
        normed = (stream1 * inverse_rms(stream1) * gains[1:2, :]).astype(BF)
        b_out[...] = normed

        need(1)

        def chunk(j, _):
            value, slope = gelu_both(mm(normed, w_up[:, block(j, HC)]))
            z_out[:, block(j, HC)] = value.astype(BF)
            slope_out[:, block(j, HC)] = slope.astype(BF)
            return 0

        lax.fori_loop(0, hidden // HC, chunk, 0, unroll=3)
        need(2)
        branch2 = mm(z_out[...], w_down[...])
        stream2 = stream1 + branch2
        h2_out[...] = stream2
        f_out[...] = (stream2 * inverse_rms(stream2) * gains[2:3, :]).astype(BF)
        row = iota(stats.shape, 0)
        stats[...] += (
            jnp.where(row == 0, row_total(stream2, live), 0.0)
            + jnp.where(row == 1, row_total(branch, live), 0.0)
            + jnp.where(row == 2, row_total(branch2, live), 0.0)
        )


def feed_call(groups, count, attended, stream0, gains, sources):
    local, model = attended.shape
    whole = [dims for group in groups for dims in group.full_shapes()]
    hidden = whole[2][0]

    def rows(i, c):
        return (jnp.minimum(i, c[2] * (RB // FB) - 1), 0)

    def same(i, c):
        return (0, 0)

    narrow = pl.BlockSpec((FB, model), rows)
    wide = pl.BlockSpec((FB, hidden), rows)
    return pl.pallas_call(
        functools.partial(feed, groups),
        grid_spec=pltpu.PrefetchScalarGridSpec(
            num_scalar_prefetch=1,
            grid=(local // FB,),
            in_specs=[narrow, narrow, pl.BlockSpec((8, model), same)] + [anywhere()] * len(sources),
            out_specs=(narrow, narrow, wide, wide, narrow, narrow, pl.BlockSpec((8, LANES), same)),
            scratch_shapes=[pltpu.VMEM(dims, BF) for dims in whole] + [pltpu.SemaphoreType.DMA((3,))],
        ),
        out_shape=(
            shape((local, model), F32),
            shape((local, model), BF),
            shape((local, hidden), BF),
            shape((local, hidden), BF),
            shape((local, model), F32),
            shape((local, model), BF),
            shape((8, LANES), F32),
        ),
        compiler_params=params(),
        cost_estimate=cost(20e9),
        name="feed",
    )(count, attended, stream0, gains, *sources)


def by_lanes(fold, held, value):
    for k in range(value.shape[1] // LANES):
        held = fold(held, value[:, k * LANES : (k + 1) * LANES])
    return held


def head(
    count, f_ref, t_ref, rows_all, weight_any, grad_any, df_any, loss, weight, grad, df_ref, logits, back, flipped, sems
):
    chunks = weight.shape[1] // HC

    def weight_copy(j):
        return pltpu.make_async_copy(
            weight_any.at[:, block(j, HC)], weight.at[:, block(j, HC)], sems.at[0, j]
        )

    def grad_copy(j):
        return pltpu.make_async_copy(
            grad.at[:, block(j, HC)], grad_any.at[:, block(j, HC)], sems.at[1, j]
        )

    def df_copy(i):
        return pltpu.make_async_copy(
            df_ref.at[block(i, RB), :], df_any.at[block(i, RB), :], sems.at[2, i]
        )

    for j in range(chunks):
        weight_copy(j).start()
    loss[...] = jnp.zeros(loss.shape, F32)
    model = f_ref.shape[1]
    lane = iota((RB, HC), 1)

    def over_rows(i, _):
        rows = block(i, RB)
        normed = f_ref[rows, :]
        flipped[:, rows] = normed.astype(F32).T.astype(BF)
        target = t_ref[rows, 0:1].astype(jnp.int32)
        live = live_rows(i, count)

        def values(j):
            @pl.when(i == 0)
            def _():
                weight_copy(j).wait()

            return mm(normed, weight[:, block(j, HC)])

        def first(j, top):
            value = values(j)
            logits[:, block(j, HC)] = value
            return by_lanes(jnp.maximum, top, value)

        top = lax.fori_loop(0, chunks - 1, first, jnp.full((RB, LANES), 3.0 * LOW, F32), unroll=9)
        value = jnp.where(lane < BINS - (chunks - 1) * HC, values(chunks - 1), LOW)
        logits[:, (chunks - 1) * HC :] = value
        top = jnp.max(by_lanes(jnp.maximum, top, value), axis=1, keepdims=True)

        def second(j, carry):
            total, hit = carry
            value = logits[:, block(j, HC)]
            expo = jnp.exp(value - top)
            logits[:, block(j, HC)] = expo
            hit = by_lanes(jnp.add, hit, jnp.where(lane == target - j * HC, value, 0.0))
            return by_lanes(jnp.add, total, expo), hit

        zero = jnp.zeros((RB, LANES), F32)
        total, hit = lax.fori_loop(0, chunks, second, (zero, zero), unroll=5)
        total = jnp.sum(total, axis=1, keepdims=True)
        hit = jnp.sum(hit, axis=1, keepdims=True)
        part = live / rows_all[0:1, 0:1]
        share = part / total

        def third(j, held):
            hot = jnp.where(lane == target - j * HC, part, 0.0)
            found = (logits[:, block(j, HC)] * share - hot).astype(BF)
            back[rows, block(j, HC)] = found
            return held + mm_nt(found, weight[:, block(j, HC)])

        df_ref[rows, :] = lax.fori_loop(0, chunks, third, jnp.zeros((RB, model), F32), unroll=5)
        df_copy(i).start()
        loss[...] += jnp.sum(live * (top + jnp.log(total) - hit))
        return 0

    lax.fori_loop(0, count[2], over_rows, 0)

    for blocks in range(1, f_ref.shape[0] // RB + 1):

        @pl.when(count[2] == blocks)
        def _(blocks=blocks):
            def over_columns(j, _):
                grad[:, block(j, HC)] = mm(
                    flipped[:, : blocks * RB], back[: blocks * RB, block(j, HC)]
                ).astype(BF)
                grad_copy(j).start()
                return 0

            lax.fori_loop(0, chunks, over_columns, 0, unroll=5)
            for i in range(blocks):
                df_copy(i).wait()

    for j in range(chunks):
        grad_copy(j).wait()


def head_call(count, normed, targets, rows_all, weight):
    local, model = normed.shape
    bins = weight.shape[1]
    return pl.pallas_call(
        head,
        out_shape=(shape((model, bins), BF), shape((local, model), F32), shape((8, LANES), F32)),
        in_specs=[in_smem()] + [in_vmem()] * 3 + [anywhere()],
        out_specs=(anywhere(), anywhere(), in_vmem()),
        scratch_shapes=[
            pltpu.VMEM((model, bins), BF),
            pltpu.VMEM((model, bins), BF),
            pltpu.VMEM((local, model), F32),
            pltpu.VMEM((RB, bins), F32),
            pltpu.VMEM((local, bins), BF),
            pltpu.VMEM((model, local), BF),
            pltpu.SemaphoreType.DMA((3, bins // HC)),
        ],
        compiler_params=params(),
        cost_estimate=cost(35e9),
        name="head",
    )(count, normed, targets, rows_all, weight)


def feed_back(groups, count, df_ref, h2_ref, h1_ref, gains, o_any, b_any, z_any, slope_any, *rest):
    sources = rest[: 4 if groups[0].direct else 3]
    rest = rest[len(sources) :]
    targets = rest[: 4 if groups[0].direct else 3]
    (
        dh1_out,
        do_out,
        gain_out,
        w_out,
        w_up,
        w_down,
        g_out,
        g_up,
        g_down,
        o_all,
        b_all,
        z_all,
        slope_all,
        dm_all,
        da_all,
        w_sem,
        r_sem,
        g_sem,
    ) = rest[len(targets) :]
    step = pl.program_id(0)
    hidden = w_up.shape[1]
    rows = block(step, RB)
    loads = ((o_any, o_all), (b_any, b_all), (z_any, z_all), (slope_any, slope_all))

    @pl.when(step == 0)
    def _():
        load_feed(groups, sources, [w_out, w_up, w_down], w_sem, count)
        gain_out[...] = jnp.zeros(gain_out.shape, F32)

        def fetch(i, _):
            for k, (source, target) in enumerate(loads):
                pltpu.make_async_copy(
                    source.at[block(i, RB)], target.at[block(i, RB)], r_sem.at[k, i]
                ).start()
            return 0

        lax.fori_loop(0, count[2], fetch, 0)

    def need(k):
        @pl.when(step == 0)
        def _():
            loaded((w_out, w_up, w_down)[k], w_sem.at[k])

    @pl.when(step < count[2])
    def _():
        back, gain3 = rms_back(h2_ref[...], gains[2:3, :], df_ref[...])
        dm = back.astype(BF)
        dm_all[rows, :] = dm
        for k, (source, target) in enumerate(loads):
            pltpu.make_async_copy(source.at[rows], target.at[rows], r_sem.at[k, step]).wait()
        need(2)
        need(1)

        def chunk(j, held):
            spot = block(j, HC)
            upper = mm_nt(dm, w_down[spot, :])
            found = (upper * slope_all[rows, spot].astype(F32)).astype(BF)
            slope_all[rows, spot] = found
            return held + mm_nt(found, w_up[:, spot])

        db = lax.fori_loop(0, hidden // HC, chunk, jnp.zeros(back.shape, F32), unroll=3)
        need(0)
        back1, gain2 = rms_back(h1_ref[...], gains[1:2, :], db)
        stream = back + back1
        dh1_out[...] = stream
        da = stream.astype(BF)
        da_all[rows, :] = da
        do_out[...] = mm_nt(da, w_out[...]).astype(BF)
        row = iota(gain_out.shape, 0)
        gain_out[...] += jnp.where(row == 1, gain2, 0.0) + jnp.where(row == 2, gain3, 0.0)

    @pl.when(step == pl.num_programs(0) - 1)
    def _():
        sems = [g_sem.at[k] for k in range(len(targets))]
        split = len(targets) * 2 // 4 if groups[0].direct else 2

        def over_row_blocks(body):
            for blocks in range(1, z_all.shape[0] // RB + 1):

                @pl.when(count[2] == blocks)
                def _(blocks=blocks):
                    body(slice(0, blocks * RB))

        @over_row_blocks
        def _(live):
            def columns(j, _):
                spot = block(j, HC)
                g_down[spot, :] = mm_tn(z_all[live, spot], dm_all[live, :]).astype(BF)
                return 0

            lax.fori_loop(0, hidden // HC, columns, 0, unroll=2)

        groups[1].store([g_down], targets[split:], sems[split:], count[4], count[5])

        @over_row_blocks
        def _(live):
            def columns(j, _):
                spot = block(j, HC)
                g_up[:, spot] = mm_tn(b_all[live, :], slope_all[live, spot]).astype(BF)
                return 0

            lax.fori_loop(0, hidden // HC, columns, 0, unroll=2)
            g_out[...] = mm_tn(o_all[live, :], da_all[live, :]).astype(BF)

        groups[0].store([g_out, g_up], targets[:split], sems[:split], count[4], count[5])
        groups[0].stored(targets, sems)


def feed_back_call(groups, count, df, stream2, stream1, gains, attended, normed, active, slope, sources):
    local, model = df.shape
    whole = [dims for group in groups for dims in group.full_shapes()]
    hidden = whole[2][0]
    outs = [found for group in groups for found in group.out_shapes()]

    def rows(i, c):
        return (jnp.minimum(i, c[2] - 1), 0)

    def same(i, c):
        return (0, 0)

    narrow = pl.BlockSpec((RB, model), rows)
    return pl.pallas_call(
        functools.partial(feed_back, groups),
        grid_spec=pltpu.PrefetchScalarGridSpec(
            num_scalar_prefetch=1,
            grid=(local // RB,),
            in_specs=[narrow, narrow, narrow, pl.BlockSpec((8, model), same)]
            + [anywhere()] * (4 + len(sources)),
            out_specs=(anywhere(),) * len(outs) + (narrow, narrow, pl.BlockSpec((8, model), same)),
            scratch_shapes=[pltpu.VMEM(dims, BF) for dims in whole] * 2
            + [
                pltpu.VMEM((local, model), BF),
                pltpu.VMEM((local, model), BF),
                pltpu.VMEM((local, hidden), BF),
                pltpu.VMEM((local, hidden), BF),
                pltpu.VMEM((local, model), BF),
                pltpu.VMEM((local, model), BF),
                pltpu.SemaphoreType.DMA((3,)),
                pltpu.SemaphoreType.DMA((4, local // RB)),
                pltpu.SemaphoreType.DMA((4,)),
            ],
        ),
        out_shape=tuple(outs)
        + (shape((local, model), F32), shape((local, model), BF), shape((8, model), F32)),
        compiler_params=params(),
        cost_estimate=cost(35e9),
        name="feed_back",
    )(count, df, stream2, stream1, gains, attended, normed, active, slope, *sources)


def project_back(
    groups, blocks, count, dq, aq, xq, dh1, h0, dk, dv, ac, xc, yc, gains, gains23, weight, *rest
):
    targets = rest[: 4 if groups[0].direct else 2]
    total, emb, small, out0, out1, g_sem = rest[len(targets) :]
    step = pl.program_id(0)
    steps = pl.num_programs(0)
    model = dq.shape[1]
    embed = slice(3 * model, 3 * model + LANES)

    @pl.when(step == 0)
    def _():
        total[...] = jnp.zeros(total.shape, F32)
        emb[...] = jnp.zeros(emb.shape, F32)
        small[...] = gains23[...]

    row = iota(small.shape, 0)

    @pl.when(step < count[2])
    def _():
        grad = dq[...]
        upper = mm_nt(grad, weight[:, :model])
        total[:, :model] += mm_tn(aq[...], grad)
        back, gain1 = rms_back(h0[...], gains[0:1, :], upper)
        stream = dh1[...] + back
        emb[...] += mm_tn(stream.astype(BF), xq[...])
        small[...] += jnp.where(row == 0, gain1, 0.0)

    @pl.when((step >= blocks) & (step < blocks + count[3]))
    def _():
        a = ac[...]
        label = yc[:, 0:1]
        stream = mm_nt(xc[...], weight[:, embed]) + label * gains[3:4, :]
        upper = jnp.zeros(stream.shape, F32)
        for part, ref in enumerate((dk, dv)):
            grad = ref[...]
            columns = slice((part + 1) * model, (part + 2) * model)
            upper += mm_nt(grad, weight[:, columns])
            total[:, columns] += mm_tn(a, grad)
        back, gain1 = rms_back(stream, gains[0:1, :], upper)
        emb[...] += mm_tn(back.astype(BF), xc[...])
        small[...] += jnp.where(row == 0, gain1, 0.0) + jnp.where(
            row == 3, jnp.sum(label * back, axis=0, keepdims=True), 0.0
        )

    @pl.when(step == steps - 1)
    def _():
        middle = out0.shape[1]
        out0[...] = total[:, :middle].astype(BF)
        out1[:, : 3 * model - middle] = total[:, middle:].astype(BF)
        out1[:, 3 * model - middle : 3 * model - middle + LANES] = emb[...].astype(BF)
        padded = jnp.concatenate([small[...], jnp.zeros((LANES - 8, small.shape[1]), F32)])
        out1[:, 3 * model - middle + LANES :] = padded.T.astype(BF)
        sems = [g_sem.at[k] for k in range(len(targets))]
        size = len(targets) // 2
        for k, (group, out) in enumerate(zip(groups, (out0, out1))):
            some = slice(k * size, (k + 1) * size)
            group.store([out], targets[some], sems[some], count[4], count[5])
        group.stored(targets, sems)


def project_back_call(groups, count, dq, aq, xq, dh1, h0, dk, dv, ac, xc, yc, gains, gains23, weight):
    local, model = dq.shape
    total = dk.shape[0]
    blocks_q, blocks_c = local // RB, total // CB
    outs = [found for group in groups for found in group.out_shapes()]

    def q_map(i, c):
        return (jnp.minimum(i, c[2] - 1), 0)

    def c_map(i, c):
        return (jnp.clip(i - blocks_q, 0, c[3] - 1), 0)

    def same(i, c):
        return (0, 0)

    query = pl.BlockSpec((RB, model), q_map)
    context = pl.BlockSpec((CB, model), c_map)
    thin = pl.BlockSpec((CB, LANES), c_map)
    fixed = pl.BlockSpec((8, model), same)
    return pl.pallas_call(
        functools.partial(project_back, groups, blocks_q),
        grid_spec=pltpu.PrefetchScalarGridSpec(
            num_scalar_prefetch=1,
            grid=(blocks_q + blocks_c,),
            in_specs=[
                query,
                query,
                pl.BlockSpec((RB, LANES), q_map),
                query,
                query,
                context,
                context,
                context,
                thin,
                thin,
                fixed,
                fixed,
                pl.BlockSpec(weight.shape, same),
            ],
            out_specs=(anywhere(),) * len(outs),
            scratch_shapes=[
                pltpu.VMEM((model, 3 * model), F32),
                pltpu.VMEM((model, LANES), F32),
                pltpu.VMEM((8, model), F32),
                pltpu.VMEM(groups[0].full_shapes()[0], BF),
                pltpu.VMEM(groups[1].full_shapes()[0], BF),
                pltpu.SemaphoreType.DMA((4,)),
            ],
        ),
        out_shape=tuple(outs),
        compiler_params=params(),
        cost_estimate=cost(20e9),
        name="project_back",
    )(count, dq, aq, xq, dh1, h0, dk, dv, ac, xc, yc, gains, gains23, weight)


def halves(tab, mine):
    other = swap(mine, "tab", 0)
    return jnp.where(tab == 0, mine, other), jnp.where(tab == 0, other, mine)


def on_device(
    count_fsdp,
    features,
    feature_counts,
    row_flags,
    target_bins,
    emb_weight,
    qkv_weight,
    out_weight,
    up_weight,
    down_weight,
    head_weight,
    vectors,
    mom_emb,
    mom_qkv,
    mom_out,
    mom_up,
    mom_down,
    mom_head,
    mom_vectors,
    ema_emb,
    ema_qkv,
    ema_out,
    ema_up,
    ema_down,
    ema_head,
    ema_vectors,
):
    masters = (emb_weight, qkv_weight, out_weight, up_weight, down_weight, head_weight, vectors)
    moms = (mom_emb, mom_qkv, mom_out, mom_up, mom_down, mom_head, mom_vectors)
    emas = (ema_emb, ema_qkv, ema_out, ema_up, ema_down, ema_head, ema_vectors)
    me = lax.axis_index("fsdp").astype(jnp.int32)
    tab = lax.axis_index("tab").astype(jnp.int32)
    local, nfeat = features.shape[1:]
    total = 2 * local
    rows = qkv_weight.shape[0]
    model = rows * count_fsdp
    half = model // 2
    hidden_half = up_weight.shape[1] // 2
    size = model // HEADS
    flags = row_flags[0]
    targets = target_bins[0]

    high_bits = [1 << k for k in reversed(range(1, count_fsdp.bit_length() - 1))]
    x_last = high_bits + ["tab"]
    y_last = high_bits[:-1] + ["tab", high_bits[-1]]
    wide = 3 * model
    quarter = (wide + 2 * LANES) // 4
    groups_a = [Group(order, rows, [(quarter, 1)], count_fsdp) for order in (x_last, y_last)]
    groups_b = [
        Group(x_last, rows, [(half, 1), (hidden_half, 1)], count_fsdp),
        Group(y_last, down_weight.shape[0], [(half, 1)], count_fsdp),
    ]

    def side_of(weight, width):
        return jnp.where(tab == 0, weight[:, :width], weight[:, width : 2 * width])

    queries_here = jnp.sum(flags)
    marks = jnp.stack([queries_here // 32, queries_here % 32]).astype(F32)
    first_row = (jnp.arange(rows) == 0).astype(F32)[:, None]

    def tail(block_t):
        used = block_t.shape[0]
        return jnp.concatenate(
            [block_t.T, first_row * marks[None, :], jnp.zeros((rows, LANES - 2 - used), F32)], axis=1
        )

    piece_a = jnp.concatenate([qkv_weight, tail(emb_weight), tail(vectors)], axis=1).astype(BF)
    pieces_b = [
        [side_of(out_weight, half), side_of(up_weight, hidden_half)],
        [side_of(down_weight, half)],
    ]
    held_b = [jnp.concatenate(found, axis=1).astype(BF)[None] for found in pieces_b]
    bins = -(-head_weight.shape[1] // HC) * HC
    spare = bins - head_weight.shape[1]
    piece_h = jnp.pad(head_weight.astype(BF), ((0, 0), (0, spare)))

    whole_a = lax.all_gather(piece_a, "fsdp", axis=0, tiled=True)

    pack = jnp.concatenate(
        [
            features[0],
            jnp.stack([flags, targets // 64, targets % 64], axis=1).astype(BF),
            jnp.zeros((local, LANES - 3 - nfeat), BF),
        ],
        axis=1,
    )
    lower, upper = halves(tab, pack)
    table = jnp.concatenate([lower, upper])
    flag_rows = table[:, nfeat].astype(F32).reshape(total // LANES, LANES)
    asked = jnp.sum(flag_rows).astype(jnp.int32)
    here = (asked - tab + 1) // 2
    known = total - asked
    count = jnp.stack(
        [
            here,
            known,
            jnp.maximum((here + RB - 1) // RB, 1),
            (known + CB - 1) // CB,
            me,
            tab,
            feature_counts[0],
            jnp.maximum((here + QB - 1) // QB, 1),
        ]
    )
    x_query, t_query, x_context, y_context = sort_rows_call(nfeat, count, table, flag_rows)

    last = len(high_bits)
    for at in range(last):
        held_b = gather_step(groups_b, held_b, at, *([x_query] if at == last - 2 else []))
        if at == last - 2:
            head_full = lax.all_gather(after(piece_h, held_b), "fsdp", axis=0, tiled=True)
    x_query = after(x_query, held_b)
    queries, keys, values, a_query, a_context, stream0, gains = project_call(
        nfeat, count, x_query, x_context, y_context, whole_a
    )
    row_count = gains[4:5, :LANES]
    row_count = row_count + swap(row_count, "tab", 0)
    attended, logs = attend_call(size, count, queries, keys, values)
    held_b = gather_step(groups_b, held_b, last, attended)
    far_b = [swap(held, 1, count_fsdp) for held in held_b]
    sources_b = [
        found
        for group, near, far in zip(groups_b, held_b, far_b)
        for found in group.sources(near, far, me, tab)
    ]
    stream1, normed2, active, slope, stream2, normed3, stats = feed_call(
        groups_b, count, attended, stream0, gains, sources_b
    )
    grad_head, df, loss = head_call(count, normed3, t_query, row_count, head_full)
    shard_h = lax.optimization_barrier(
        lax.psum_scatter(grad_head, "fsdp", scatter_dimension=0, tiled=True)
    )
    *outs_b, dh1, grad_o, gains23 = feed_back_call(
        groups_b, count, df, stream2, stream1, gains, attended, normed2, active, slope, sources_b
    )

    def core_step(groups, outs):
        size_of = len(outs) // 2 if groups[0].direct else len(groups[0].parts)
        pairs = [
            group.targets(found, me, tab) for group, found in zip(groups, (outs[:size_of], outs[size_of:]))
        ]
        return [near + swap(far, 1, count_fsdp) for near, far in pairs]

    grads_b = core_step(groups_b, outs_b)
    grad_o = after(grad_o, grads_b)
    dq, dk, dv = attend_back_call(size, count, queries, keys, values, grad_o, attended, logs)
    grads_b = scatter_step(groups_b, grads_b, last, dq)
    dq = after(dq, grads_b)
    outs_a = project_back_call(
        groups_a,
        count,
        dq,
        a_query,
        x_query,
        dh1,
        stream0,
        dk,
        dv,
        a_context,
        x_context,
        y_context,
        gains,
        gains23,
        whole_a,
    )
    grads_b = scatter_step(groups_b, grads_b, last - 1, outs_a)
    grads_a = core_step(groups_a, outs_a)
    for at in reversed(range(last + 1)):
        grads_a = scatter_step(groups_a, grads_a, at)
        if at < last - 1:
            grads_b = scatter_step(groups_b, grads_b, at)
    shards_a = [found[0] for found in grads_a]
    shards_b = [found[0] for found in grads_b]

    shard_h = shard_h[:, : head_weight.shape[1]]
    grad_h = shard_h.astype(F32) + swap(shard_h, "tab", 0).astype(F32)
    split_a = [halves(tab, found) for found in shards_a]
    split_b = [halves(tab, found) for found in shards_b]
    whole_grad = jnp.concatenate([side for found in split_a for side in found], axis=1)
    grad_qkv = whole_grad[:, :wide]
    grad_emb = whole_grad[:, wide : wide + nfeat].T
    grad_vectors = whole_grad[:, wide + LANES : wide + LANES + vectors.shape[0]].T
    grad_out = jnp.concatenate([side[:, :half] for side in split_b[0]], axis=1)
    grad_up = jnp.concatenate([side[:, half:] for side in split_b[0]], axis=1)
    grad_down = jnp.concatenate(split_b[1], axis=1)
    summed = (grad_emb, grad_qkv, grad_out, grad_up, grad_down, grad_h, grad_vectors)
    place = jnp.arange(quarter)[None, :] + (2 + tab) * quarter - wide
    real = (place < nfeat) | ((place >= LANES) & (place < LANES + vectors.shape[0]))
    keep_a = jnp.where(real, shards_a[1], 0.0)
    squares = 0.5 * jnp.sum(grad_h * grad_h)
    for found in (shards_a[0], keep_a, *shards_b):
        squares = squares + jnp.sum(found * found)
    sums = jnp.concatenate([loss[0:1, 0:1], stats[0:3, 0:1], squares.reshape(1, 1)]).reshape(1, 5)
    sums = jnp.broadcast_to(jnp.pad(sums, ((0, 0), (0, LANES - 5))), (8, LANES))
    for step in [1] + high_bits + ["tab"]:
        sums = sums + swap(sums, step, count_fsdp)
    loss_sum = sums[0, 0]
    rms_sums = sums[0, 1:4]
    clip_norm = jnp.sqrt(sums[0, 4])
    row_count = row_count[0, 0]
    factor = jnp.minimum(1.0, CLIP / clip_norm)
    new_moms, new_weights, new_emas = ([], [], [])
    for weight, grad, moment, average in zip(masters, summed, moms, emas):
        clipped = grad * factor
        moment_new = MOMENTUM * moment + clipped
        weight_new = weight - RATE * (clipped + MOMENTUM * moment_new)
        new_moms.append(moment_new)
        new_weights.append(weight_new)
        new_emas.append(AVERAGE * average + (1.0 - AVERAGE) * weight_new)
    return (loss_sum, row_count, rms_sums, clip_norm, *new_moms, *new_weights, *new_emas)


def solution(mesh):
    by_row, by_column = P("fsdp", None), P(None, "fsdp")
    weights = (by_column, by_row, by_row, by_row, by_row, by_row, by_column)
    return jax.shard_map(
        functools.partial(on_device, mesh.shape["fsdp"]),
        mesh=mesh,
        in_specs=(P("fsdp", "tab", None), P("fsdp"), P("fsdp", "tab"), P("fsdp", "tab")) + weights * 3,
        out_specs=(P(), P(), P(), P()) + weights * 3,
        check_vma=False,
    )
```

```python
import functools

import jax
import jax.numpy as jnp
import numpy as np
from jax import lax
from jax.experimental import pallas as pl
from jax.experimental.pallas import tpu as pltpu
from jax.sharding import PartitionSpec as P

HEADS = 12
BINS = 5000
CLIP = 0.005
RATE = 10000.0
MOMENTUM = 0.5
AVERAGE = 0.5

BF = jnp.bfloat16
F32 = jnp.float32
LANES = 128
QB = 256
AB = 256
FB = 256
RB = 512
CB = 512
HC = 512
VMEM = 60 * 1024 * 1024
LOW = -1e30


def mm(left, right):
    return jnp.dot(left, right, preferred_element_type=F32)


def mm_tn(left, right):
    return lax.dot_general(left, right, (((0,), (0,)), ((), ())), preferred_element_type=F32)


def mm_nt(left, right):
    return lax.dot_general(left, right, (((1,), (1,)), ((), ())), preferred_element_type=F32)


def iota(shape, axis):
    return lax.broadcasted_iota(jnp.int32, shape, axis)


def block(index, size):
    return pl.ds(pl.multiple_of(index * size, size), size)


def inverse_rms(stream):
    return lax.rsqrt(jnp.mean(stream * stream, axis=-1, keepdims=True) + 1e-06)


def rms_back(stream, gain, upstream):
    scale = inverse_rms(stream)
    unit = stream * scale
    weighted = upstream * gain
    back = scale * (weighted - unit * jnp.mean(weighted * unit, axis=-1, keepdims=True))
    return back, jnp.sum(upstream * unit, axis=0, keepdims=True)


def params():
    return pltpu.CompilerParams(vmem_limit_bytes=VMEM)


def cost(flops):
    return pl.CostEstimate(flops=int(flops), bytes_accessed=1 << 20, transcendentals=0)


def anywhere():
    return pl.BlockSpec(memory_space=pl.ANY)


def in_vmem():
    return pl.BlockSpec(memory_space=pltpu.VMEM)


def in_smem():
    return pl.BlockSpec(memory_space=pltpu.SMEM)


def shape(dims, dtype):
    return jax.ShapeDtypeStruct(dims, dtype)


class Group:
    def __init__(self, axis_bits, rows, parts, count):
        self.steps = axis_bits
        self.rows = rows
        self.parts = parts
        self.count = count
        self.width = sum(width * blocks for width, blocks in parts)
        self.pieces = 2 ** len(axis_bits)
        self.direct = rows % 16 == 0

    def place(self, piece, core):
        across, half = core, 0
        for bit, step in enumerate(self.steps):
            if piece >> bit & 1:
                if step == "tab":
                    half ^= 1
                else:
                    across ^= step
        return across, half

    def spans(self):
        start = 0
        for part, (width, blocks) in enumerate(self.parts):
            for at in range(blocks):
                yield part, start, width, at, blocks
                start += width

    def full_shapes(self):
        return [(self.count * self.rows * blocks, 2 * width) for width, blocks in self.parts]

    def table(self):
        order = np.zeros((self.count, 2), np.int32)
        for core in range(2):
            for piece in range(self.pieces):
                across, half = self.place(piece, core)
                order[across, half] = core * self.pieces + piece
        return order

    def to_whole(self, near, far, me, tab):
        places = np.arange(self.count, dtype=np.int32)[:, None] ^ me
        sides = np.arange(2, dtype=np.int32)[None, :] ^ tab
        index = jnp.asarray(self.table())[places, sides]
        every = jnp.take(jnp.concatenate([near, far]), index, axis=0)
        every = every.transpose(0, 2, 1, 3)
        whole = [[] for _ in self.parts]
        for part, start, width, _, _ in self.spans():
            whole[part].append(every[..., start : start + width])
        return [
            jnp.stack(found, axis=1).reshape(dims) for found, dims in zip(whole, self.full_shapes())
        ]

    def to_pieces(self, wholes, me, tab):
        columns = []
        for part, _, width, at, blocks in self.spans():
            split = wholes[part].reshape(self.count, blocks, self.rows, 2, width)
            columns.append(split[:, at])
        every = jnp.concatenate(columns, axis=-1).transpose(0, 2, 1, 3)
        every = every.reshape(2 * self.count, self.rows, self.width)
        where = np.array(
            [self.place(piece, core) for core in range(2) for piece in range(self.pieces)], np.int32
        )
        index = (where[:, 0] ^ me) * 2 + (where[:, 1] ^ tab)
        found = jnp.take(every, index, axis=0)
        return found[: self.pieces], found[self.pieces :]

    def pairs(self, wholes, moved, me, tab):
        for core in range(2):
            for piece in range(self.pieces):
                across, half = self.place(piece, core)
                shard = lax.bitwise_xor(me, jnp.int32(across))
                side = lax.bitwise_xor(tab, jnp.int32(half))
                for part, start, width, at, blocks in self.spans():
                    first = pl.multiple_of((shard * blocks + at) * self.rows, self.rows)
                    column = pl.multiple_of(side * width, LANES)
                    yield (
                        wholes[part].at[pl.ds(first, self.rows), pl.ds(column, width)],
                        moved[core].at[piece, :, pl.ds(start, width)],
                        part,
                        core,
                    )

    def load(self, sources, wholes, sems, me, tab):
        if not self.direct:
            for source, whole, sem in zip(sources, wholes, sems):
                pltpu.make_async_copy(source, whole, sem).start()
            return
        for whole, piece, part, _ in self.pairs(wholes, sources, me, tab):
            pltpu.make_async_copy(piece, whole, sems[part]).start()

    def store(self, wholes, targets, sems, me, tab):
        if not self.direct:
            for whole, target, sem in zip(wholes, targets, sems):
                pltpu.make_async_copy(whole, target, sem).start()
            return
        for whole, piece, _, core in self.pairs(wholes, targets, me, tab):
            pltpu.make_async_copy(whole, piece, sems[core]).start()

    def stored(self, targets, sems):
        for target, sem in zip(targets, sems):
            pltpu.make_async_copy(target, target, sem).wait()

    def out_shapes(self):
        if self.direct:
            return [shape((self.pieces, self.rows, self.width), BF)] * 2
        return [shape(dims, BF) for dims in self.full_shapes()]

    def sources(self, near, far, me, tab):
        return [near, far] if self.direct else self.to_whole(near, far, me, tab)

    def targets(self, outs, me, tab):
        return tuple(outs) if self.direct else self.to_pieces(outs, me, tab)


def loaded(whole, sem):
    pltpu.make_async_copy(whole, whole, sem).wait()


def swap(value, step, count):
    if step == "tab":
        return lax.ppermute(value, "tab", [(0, 1), (1, 0)])
    return lax.ppermute(value, "fsdp", [(i, i ^ step) for i in range(count)])


def after(value, *others):
    return lax.optimization_barrier((value, others))[0]


def gather_all(group, piece):
    held = piece[None]
    for step in group.steps:
        held = jnp.concatenate([held, swap(held, step, group.count)])
    return held, swap(held, 1, group.count)


def added(pair, part):
    return pair[0][part].astype(F32) + pair[1][part].astype(F32)


def scatter_send(group, pair, at):
    size = pair[0].shape[0] // 2
    return swap(added(pair, slice(size, None)).astype(BF), group.steps[at], group.count)


def scatter_keep(pair, found):
    size = pair[0].shape[0] // 2
    return added(pair, slice(0, size)).astype(BF), found


def sort_rows(nfeat, count, table, marks, x_query, t_query, x_context, y_context):
    total, _ = table.shape
    rows = total // LANES
    flags = marks[...]
    inside = mm(flags.astype(BF), (iota((LANES, LANES), 0) <= iota((LANES, LANES), 1)).astype(F32).astype(BF))
    sums = jnp.broadcast_to(jnp.sum(flags, axis=1, keepdims=True), (rows, LANES))
    below = (iota((rows, rows), 1) < iota((rows, rows), 0)).astype(F32)
    upto = inside + mm(below.astype(BF), sums.astype(BF))
    spot = (iota((rows, LANES), 0) * LANES + iota((rows, LANES), 1)).astype(F32)
    as_query = jnp.where(flags > 0, upto - 1.0, -1.0)
    as_context = jnp.where(flags > 0, -1.0, spot - upto)
    held = count[6]
    scale = jnp.sqrt(F32(nfeat) / jnp.full((1, LANES), held, jnp.int32).astype(F32))

    def pick(rank, dest):
        hot = jnp.concatenate(
            [(rank[k : k + 1, :] == dest).astype(F32).astype(BF) for k in range(rows)], axis=1
        )
        found = mm(hot, table[...])
        kept = jnp.where(iota(found.shape, 1) < held, found * scale, 0.0).astype(BF)
        return kept, found[:, nfeat + 1 : nfeat + 2] * 64.0 + found[:, nfeat + 2 : nfeat + 3]

    def query(i, _):
        dest = (2 * (i * QB + iota((QB, LANES), 0)) + count[5]).astype(F32)
        kept, target = pick(as_query, dest)
        x_query[block(i, QB), :] = kept
        t_query[block(i, QB), :] = jnp.broadcast_to(target, (QB, LANES))
        return 0

    def context(i, _):
        dest = i * QB + iota((QB, LANES), 0)
        kept, target = pick(as_context, dest.astype(F32))
        x_context[block(i, QB), :] = kept
        label = (jnp.broadcast_to(target, (QB, LANES)) + 0.5) * (2.0 / BINS) - 1.0
        y_context[block(i, QB), :] = jnp.where(dest < count[1], label, 0.0)
        return 0

    lax.fori_loop(0, count[2] * (RB // QB), query, 0)
    lax.fori_loop(0, count[3] * (CB // QB), context, 0)


def sort_rows_call(nfeat, count, table, marks):
    total = table.shape[0]
    local = total // 2
    return pl.pallas_call(
        functools.partial(sort_rows, nfeat),
        out_shape=(
            shape((local, LANES), BF),
            shape((local, LANES), F32),
            shape((total, LANES), BF),
            shape((total, LANES), F32),
        ),
        in_specs=[in_smem(), in_vmem(), in_vmem()],
        out_specs=(in_vmem(),) * 4,
        compiler_params=params(),
        cost_estimate=cost(7e9),
        name="sort_rows",
    )(count, table, marks)


def project(nfeat, blocks, count, x_query, x_context, y_context, weight, q_out, k_out, v_out, aq_out, ac_out, h_out, gains):
    step = pl.program_id(0)
    model = q_out.shape[1]
    embed = slice(3 * model, 3 * model + LANES)

    @pl.when(step == 0)
    def _():
        vectors = weight[:, 3 * model + LANES : 3 * model + 2 * LANES].astype(F32).T
        many = jnp.sum(vectors[4:5, :]) * 32.0 + jnp.sum(vectors[5:6, :])
        gains[...] = jnp.where(iota((8, model), 0) < 4, vectors[:8, :], many)

    def normed(stream):
        return (stream * inverse_rms(stream) * gains[0:1, :]).astype(BF)

    @pl.when(step < count[2])
    def _():
        stream = mm_nt(x_query[...], weight[:, embed])
        h_out[...] = stream
        a = normed(stream)
        aq_out[...] = a
        q_out[...] = mm(a, weight[:, :model]).astype(BF)

    @pl.when((step >= blocks) & (step < blocks + count[3]))
    def _():
        stream = mm_nt(x_context[...], weight[:, embed]) + y_context[:, 0:1] * gains[3:4, :]
        a = normed(stream)
        ac_out[...] = a
        k_out[...] = mm(a, weight[:, model : 2 * model]).astype(BF)
        v_out[...] = mm(a, weight[:, 2 * model : 3 * model]).astype(BF)


def project_call(nfeat, count, x_query, x_context, y_context, weight):
    local, total = x_query.shape[0], x_context.shape[0]
    model = weight.shape[0]
    blocks_q, blocks_c = local // RB, total // CB

    def q_map(i, c):
        return (jnp.minimum(i, c[2] - 1), 0)

    def c_map(i, c):
        return (jnp.clip(i - blocks_q, 0, c[3] - 1), 0)

    def same(i, c):
        return (0, 0)

    return pl.pallas_call(
        functools.partial(project, nfeat, blocks_q),
        grid_spec=pltpu.PrefetchScalarGridSpec(
            num_scalar_prefetch=1,
            grid=(blocks_q + blocks_c,),
            in_specs=[
                pl.BlockSpec((RB, LANES), q_map),
                pl.BlockSpec((CB, LANES), c_map),
                pl.BlockSpec((CB, LANES), c_map),
                pl.BlockSpec((model, 3 * model + 2 * LANES), same),
            ],
            out_specs=(
                pl.BlockSpec((RB, model), q_map),
                pl.BlockSpec((CB, model), c_map),
                pl.BlockSpec((CB, model), c_map),
                pl.BlockSpec((RB, model), q_map),
                pl.BlockSpec((CB, model), c_map),
                pl.BlockSpec((RB, model), q_map),
                pl.BlockSpec((8, model), same),
            ),
        ),
        out_shape=(
            shape((local, model), BF),
            shape((total, model), BF),
            shape((total, model), BF),
            shape((local, model), BF),
            shape((total, model), BF),
            shape((local, model), F32),
            shape((8, model), F32),
        ),
        compiler_params=params(),
        cost_estimate=cost(12e9),
        name="project",
    )(count, x_query, x_context, y_context, weight)


def head_masks(size):
    low = (iota((1, LANES), 1) < size).astype(F32)
    return low.astype(BF), (1.0 - low).astype(BF)


def dead_rows(j, count):
    return jnp.where(j * CB + iota((CB, 1), 0) < count[1], 0.0, LOW)


def clear_rest(ref, count):
    def clear(i, _):
        ref[block(i, QB), :] = jnp.zeros((QB, ref.shape[1]), ref.dtype)
        return 0

    lax.fori_loop(count[7], count[2] * (RB // QB), clear, 0)


def over_blocks(count, total, body):
    for blocks in range(1, total // CB + 1):

        @pl.when(count[3] == blocks)
        def _(blocks=blocks):
            body(blocks)


def context_scores(k_ref, head, blocks, count):
    scores = mm_nt(k_ref[: blocks * CB, :], head)
    tail = scores[-CB:] + dead_rows(blocks - 1, count)
    return tail if blocks == 1 else jnp.concatenate([scores[:-CB], tail])


def attend(size, count, q_ref, k_ref, v_ref, o_ref, lse_ref, v_low, v_high):
    scale = size ** (-0.5)
    masks = head_masks(size)

    def body(blocks):
        live = slice(0, blocks * CB)
        v_low[live, :] = v_ref[live, :] * masks[0] + masks[1]
        v_high[live, :] = v_ref[live, :] * masks[1] + masks[0]

        def over_queries(i, _):
            queries = q_ref[block(i, QB), :] * BF(scale)
            heads = [queries * mask for mask in masks]
            joined = []
            spots = [slice(j * AB, (j + 1) * AB) for j in range(blocks * CB // AB)]
            dead = dead_rows(blocks - 1, count)
            scores = [[mm_nt(k_ref[spot, :], head) for spot in spots] for head in heads]
            for side, parts in enumerate(scores):
                for k in range(CB // AB):
                    at = len(spots) - CB // AB + k
                    parts[at] = parts[at] + dead[k * AB : (k + 1) * AB]
                top = functools.reduce(jnp.maximum, [jnp.max(part, axis=0, keepdims=True) for part in parts])
                sums = jnp.zeros((LANES, QB), F32)
                for spot, part in zip(spots, parts):
                    expo = jnp.exp(part - top)
                    sums = sums + mm_tn((v_low, v_high)[side][spot, :], expo.astype(BF))
                total = sums[(1 - side) * size : (1 - side) * size + 1]
                joined.append((sums * (1.0 / total))[side * size : (side + 1) * size])
                lse_ref[side : side + 1, block(i, QB)] = top + jnp.log(total)
            o_ref[block(i, QB), :] = jnp.concatenate(joined).T.astype(BF)
            return 0

        lax.fori_loop(0, count[7], over_queries, 0)

    over_blocks(count, k_ref.shape[0], body)
    clear_rest(o_ref, count)


def attend_call(size, count, queries, keys, values):
    local, model = queries.shape
    total = keys.shape[0]
    pairs = model // LANES

    def column(i, c):
        return (0, i)

    return pl.pallas_call(
        functools.partial(attend, size),
        grid_spec=pltpu.PrefetchScalarGridSpec(
            num_scalar_prefetch=1,
            grid=(pairs,),
            in_specs=[
                pl.BlockSpec((local, LANES), column),
                pl.BlockSpec((total, LANES), column),
                pl.BlockSpec((total, LANES), column),
            ],
            out_specs=(
                pl.BlockSpec((local, LANES), column),
                pl.BlockSpec((None, 8, local), lambda i, c: (i, 0, 0)),
            ),
            scratch_shapes=[pltpu.VMEM((total, LANES), BF)] * 2,
        ),
        out_shape=(shape((local, model), BF), shape((pairs, 8, local), F32)),
        compiler_params=params(),
        cost_estimate=cost(35e9),
        name="attend",
    )(count, queries, keys, values)


def attend_back(size, count, q_ref, k_ref, v_ref, do_ref, o_ref, lse_ref, dq_ref, dk_ref, dv_ref, dk_sum, dv_sum):
    scale = size ** (-0.5)
    masks = head_masks(size)

    def body(blocks):
        def over_queries(i, _):
            rows = block(i, QB)
            queries = q_ref[rows, :] * BF(scale)
            grads = do_ref[rows, :]
            heads = [queries * mask for mask in masks]
            ups = [grads * mask for mask in masks]
            both_q = jnp.concatenate(heads)
            both_up = jnp.concatenate(ups)
            product = (grads.astype(F32) * o_ref[rows, :].astype(F32)).T
            back, probs, joined = [], [], []
            live = slice(0, blocks * CB)
            for side, head in enumerate(heads):
                delta = jnp.sum(product[side * size : (side + 1) * size], axis=0, keepdims=True)
                prob = jnp.exp(context_scores(k_ref, head, blocks, count) - lse_ref[side : side + 1, rows])
                upper = mm_nt(v_ref[live, :], ups[side])
                found = (prob * (upper - delta)).astype(BF)
                joined.append(mm_tn(k_ref[live, :], found)[side * size : (side + 1) * size])
                back.append(found)
                probs.append(prob.astype(BF))
            dq_ref[rows, :] = (jnp.concatenate(joined).T * scale).astype(BF)

            dk = mm(jnp.concatenate(back, axis=1), both_q)
            dv = mm(jnp.concatenate(probs, axis=1), both_up)
            dk_sum[live, :] = jnp.where(i == 0, 0.0, dk_sum[live, :]) + dk
            dv_sum[live, :] = jnp.where(i == 0, 0.0, dv_sum[live, :]) + dv
            return 0

        lax.fori_loop(0, count[7], over_queries, 0)

    over_blocks(count, k_ref.shape[0], body)
    clear_rest(dq_ref, count)

    def out(j, _):
        spot = block(j, CB)
        dk_ref[spot, :] = dk_sum[spot, :].astype(BF)
        dv_ref[spot, :] = dv_sum[spot, :].astype(BF)
        return 0

    lax.fori_loop(0, count[3], out, 0)


def attend_back_call(size, count, queries, keys, values, grads, outs, logs):
    local, model = queries.shape
    total = keys.shape[0]
    pairs = model // LANES

    def column(i, c):
        return (0, i)

    narrow = pl.BlockSpec((local, LANES), column)
    wide = pl.BlockSpec((total, LANES), column)
    return pl.pallas_call(
        functools.partial(attend_back, size),
        grid_spec=pltpu.PrefetchScalarGridSpec(
            num_scalar_prefetch=1,
            grid=(pairs,),
            in_specs=[
                narrow,
                wide,
                wide,
                narrow,
                narrow,
                pl.BlockSpec((None, 8, local), lambda i, c: (i, 0, 0)),
            ],
            out_specs=(narrow, wide, wide),
            scratch_shapes=[pltpu.VMEM((total, LANES), F32)] * 2,
        ),
        out_shape=(shape((local, model), BF), shape((total, model), BF), shape((total, model), BF)),
        compiler_params=params(),
        cost_estimate=cost(35e9),
        name="attend_back",
    )(count, queries, keys, values, grads, outs, logs)


def live_rows(i, count, size=RB):
    return (i * size + iota((size, 1), 0) < count[0]).astype(F32)


def row_total(values, live):
    return jnp.sum(jnp.sqrt(jnp.mean(values * values, axis=-1, keepdims=True) + 1e-06) * live)


def gelu_both(value):
    inner = 0.7978845608028654 * (value + 0.044715 * value * value * value)
    bend = jnp.tanh(inner)
    slope = 0.7978845608028654 * (1.0 + 3.0 * 0.044715 * value * value)
    return 0.5 * value * (1.0 + bend), 0.5 * (1.0 + bend) + 0.5 * value * (1.0 - bend * bend) * slope


def load_feed(group, sources, wholes, sem, count):
    w_out, w_up, w_down = wholes
    start = sources[0].shape[1] - w_up.shape[1]
    out = sources[0].at[:, pl.ds(start - w_out.shape[1], w_out.shape[1])]
    pltpu.make_async_copy(out, w_out, sem.at[0]).start()
    pltpu.make_async_copy(sources[0].at[:, pl.ds(start, w_up.shape[1])], w_up, sem.at[1]).start()
    group.load(sources[1:], [w_down], [sem.at[2]], count[4], count[5])


def feed(down_group, count, o_ref, h_ref, gains, *rest):
    sources = rest[: 3 if down_group.direct else 2]
    (h1_out, b_out, z_out, slope_out, h2_out, f_out, stats, w_out, w_up, w_down, sem) = rest[len(sources) :]
    step = pl.program_id(0)
    hidden = w_up.shape[1]

    @pl.when(step == 0)
    def _():
        load_feed(down_group, sources, [w_out, w_up, w_down], sem, count)
        stats[...] = jnp.zeros(stats.shape, F32)

    def need(k):
        @pl.when(step == 0)
        def _():
            loaded((w_out, w_up, w_down)[k], sem.at[k])

    @pl.when(step < count[2] * (RB // FB))
    def _():
        live = live_rows(step, count, FB)
        attended = o_ref[...]
        need(0)
        branch = mm(attended, w_out[...])
        stream1 = h_ref[...] + branch
        h1_out[...] = stream1
        normed = (stream1 * inverse_rms(stream1) * gains[1:2, :]).astype(BF)
        b_out[...] = normed

        need(1)

        def chunk(j, _):
            value, slope = gelu_both(mm(normed, w_up[:, block(j, HC)]))
            z_out[:, block(j, HC)] = value.astype(BF)
            slope_out[:, block(j, HC)] = slope.astype(BF)
            return 0

        lax.fori_loop(0, hidden // HC, chunk, 0, unroll=3)
        need(2)
        branch2 = mm(z_out[...], w_down[...])
        stream2 = stream1 + branch2
        h2_out[...] = stream2
        f_out[...] = (stream2 * inverse_rms(stream2) * gains[2:3, :]).astype(BF)
        row = iota(stats.shape, 0)
        stats[...] += (
            jnp.where(row == 0, row_total(stream2, live), 0.0)
            + jnp.where(row == 1, row_total(branch, live), 0.0)
            + jnp.where(row == 2, row_total(branch2, live), 0.0)
        )


def feed_call(down_group, count, attended, stream0, gains, sources):
    local, model = attended.shape
    hidden = down_group.full_shapes()[0][0]
    whole = [(model, model), (model, hidden), (hidden, model)]

    def rows(i, c):
        return (jnp.minimum(i, c[2] * (RB // FB) - 1), 0)

    def same(i, c):
        return (0, 0)

    narrow = pl.BlockSpec((FB, model), rows)
    wide = pl.BlockSpec((FB, hidden), rows)
    return pl.pallas_call(
        functools.partial(feed, down_group),
        grid_spec=pltpu.PrefetchScalarGridSpec(
            num_scalar_prefetch=1,
            grid=(local // FB,),
            in_specs=[narrow, narrow, pl.BlockSpec((8, model), same)] + [anywhere()] * len(sources),
            out_specs=(narrow, narrow, wide, wide, narrow, narrow, pl.BlockSpec((8, LANES), same)),
            scratch_shapes=[pltpu.VMEM(dims, BF) for dims in whole] + [pltpu.SemaphoreType.DMA((3,))],
        ),
        out_shape=(
            shape((local, model), F32),
            shape((local, model), BF),
            shape((local, hidden), BF),
            shape((local, hidden), BF),
            shape((local, model), F32),
            shape((local, model), BF),
            shape((8, LANES), F32),
        ),
        compiler_params=params(),
        cost_estimate=cost(20e9),
        name="feed",
    )(count, attended, stream0, gains, *sources)


def by_lanes(fold, held, value):
    for k in range(value.shape[1] // LANES):
        held = fold(held, value[:, k * LANES : (k + 1) * LANES])
    return held


def head(group, count, f_ref, t_ref, rows_all, weight_any, *rest):
    sources = rest[: 2 if group.direct else 1]
    (grad_any, df_any, loss, weight, grad, df_ref, logits, back, flipped, sems) = rest[len(sources) :]
    chunks = weight.shape[1] // HC
    plain = weight_any.shape[1] // HC
    moved = weight.at[:, pl.ds(plain * HC, (chunks - plain) * HC)]

    def weight_copy(j):
        return pltpu.make_async_copy(
            weight_any.at[:, block(j, HC)], weight.at[:, block(j, HC)], sems.at[0, j]
        )

    def grad_copy(j):
        return pltpu.make_async_copy(
            grad.at[:, block(j, HC)], grad_any.at[:, block(j, HC)], sems.at[1, j]
        )

    def df_copy(i):
        return pltpu.make_async_copy(
            df_ref.at[block(i, RB), :], df_any.at[block(i, RB), :], sems.at[2, i]
        )

    for j in range(plain):
        weight_copy(j).start()
    group.load(sources, [moved], [sems.at[0, plain]], count[4], count[5])
    loss[...] = jnp.zeros(loss.shape, F32)
    model = f_ref.shape[1]
    lane = iota((RB, HC), 1)

    def over_rows(i, _):
        rows = block(i, RB)
        normed = f_ref[rows, :]
        flipped[:, rows] = normed.astype(F32).T.astype(BF)
        target = t_ref[rows, 0:1].astype(jnp.int32)
        live = live_rows(i, count)

        def first(j, top):
            @pl.when((i == 0) & (j < plain))
            def _():
                weight_copy(j).wait()

            value = mm(normed, weight[:, block(j, HC)])
            logits[:, block(j, HC)] = value
            return by_lanes(jnp.maximum, top, value)

        top = lax.fori_loop(0, plain, first, jnp.full((RB, LANES), 3.0 * LOW, F32), unroll=plain)

        @pl.when(i == 0)
        def _():
            loaded(moved, sems.at[0, plain])

        for j in range(plain, chunks):
            value = mm(normed, weight[:, j * HC : (j + 1) * HC])
            if (j + 1) * HC > BINS:
                value = jnp.where(lane < BINS - j * HC, value, LOW)
            logits[:, j * HC : (j + 1) * HC] = value
            top = by_lanes(jnp.maximum, top, value)
        top = jnp.max(top, axis=1, keepdims=True)

        def second(j, carry):
            total, hit = carry
            value = logits[:, block(j, HC)]
            expo = jnp.exp(value - top)
            logits[:, block(j, HC)] = expo
            hit = by_lanes(jnp.add, hit, jnp.where(lane == target - j * HC, value, 0.0))
            return by_lanes(jnp.add, total, expo), hit

        zero = jnp.zeros((RB, LANES), F32)
        total, hit = lax.fori_loop(0, chunks, second, (zero, zero), unroll=5)
        total = jnp.sum(total, axis=1, keepdims=True)
        hit = jnp.sum(hit, axis=1, keepdims=True)
        part = live / rows_all[0:1, 0:1]
        share = part / total

        def third(j, held):
            hot = jnp.where(lane == target - j * HC, part, 0.0)
            found = (logits[:, block(j, HC)] * share - hot).astype(BF)
            back[rows, block(j, HC)] = found
            return held + mm_nt(found, weight[:, block(j, HC)])

        df_ref[rows, :] = lax.fori_loop(0, chunks, third, jnp.zeros((RB, model), F32), unroll=5)
        df_copy(i).start()
        loss[...] += jnp.sum(live * (top + jnp.log(total) - hit))
        return 0

    lax.fori_loop(0, count[2], over_rows, 0)

    for blocks in range(1, f_ref.shape[0] // RB + 1):

        @pl.when(count[2] == blocks)
        def _(blocks=blocks):
            def over_columns(j, _):
                grad[:, block(j, HC)] = mm(
                    flipped[:, : blocks * RB], back[: blocks * RB, block(j, HC)]
                ).astype(BF)
                grad_copy(j).start()
                return 0

            lax.fori_loop(0, chunks, over_columns, 0, unroll=5)
            for i in range(blocks):
                df_copy(i).wait()

    for j in range(chunks):
        grad_copy(j).wait()


def head_call(group, count, normed, targets, rows_all, weight, sources):
    local, model = normed.shape
    bins = weight.shape[1] + group.full_shapes()[0][1]
    return pl.pallas_call(
        functools.partial(head, group),
        out_shape=(shape((model, bins), BF), shape((local, model), F32), shape((8, LANES), F32)),
        in_specs=[in_smem()] + [in_vmem()] * 3 + [anywhere()] * (1 + len(sources)),
        out_specs=(anywhere(), anywhere(), in_vmem()),
        scratch_shapes=[
            pltpu.VMEM((model, bins), BF),
            pltpu.VMEM((model, bins), BF),
            pltpu.VMEM((local, model), F32),
            pltpu.VMEM((RB, bins), F32),
            pltpu.VMEM((local, bins), BF),
            pltpu.VMEM((model, local), BF),
            pltpu.SemaphoreType.DMA((3, bins // HC)),
        ],
        compiler_params=params(),
        cost_estimate=cost(35e9),
        name="head",
    )(count, normed, targets, rows_all, weight, *sources)


def over_row_blocks(count, total, body):
    for blocks in range(1, total // RB + 1):

        @pl.when(count[2] == blocks)
        def _(blocks=blocks):
            body(slice(0, blocks * RB))


def down_back(group, count, df_any, h2_any, gains, z_any, *rest):
    targets = rest[: len(group.out_shapes())]
    (dh2_out, dm_out, gain_out, df_all, h2_all, dh2_all, z_all, dm_all, g_down, r_sem, o_sem, g_sem) = rest[
        len(targets) :
    ]
    hidden = z_all.shape[1]
    loads = ((df_any, df_all), (h2_any, h2_all), (z_any, z_all))
    stores = ((dh2_all, dh2_out), (dm_all, dm_out))
    gain_out[...] = jnp.zeros(gain_out.shape, F32)

    def fetch(i, _):
        for k, (source, target) in enumerate(loads):
            pltpu.make_async_copy(source.at[block(i, RB)], target.at[block(i, RB)], r_sem.at[k, i]).start()
        return 0

    lax.fori_loop(0, count[2], fetch, 0)

    def over_rows(i, _):
        rows = block(i, RB)
        for k, (source, target) in enumerate(loads[:2]):
            pltpu.make_async_copy(source.at[rows], target.at[rows], r_sem.at[k, i]).wait()
        back, gain3 = rms_back(h2_all[rows, :], gains[2:3, :], df_all[rows, :])
        dh2_all[rows, :] = back
        dm_all[rows, :] = back.astype(BF)
        gain_out[...] += jnp.where(iota(gain_out.shape, 0) == 2, gain3, 0.0)
        for k, (source, target) in enumerate(stores):
            pltpu.make_async_copy(source.at[rows], target.at[rows], o_sem.at[k, i]).start()
        pltpu.make_async_copy(z_any.at[rows], z_all.at[rows], r_sem.at[2, i]).wait()
        return 0

    lax.fori_loop(0, count[2], over_rows, 0)
    sems = [g_sem.at[k] for k in range(len(targets))]

    def body(live):
        def columns(j, _):
            spot = block(j, HC)
            g_down[spot, :] = mm_tn(z_all[live, spot], dm_all[live, :]).astype(BF)
            return 0

        lax.fori_loop(0, hidden // HC, columns, 0, unroll=3)

    over_row_blocks(count, z_all.shape[0], body)
    group.store([g_down], targets, sems, count[4], count[5])

    def finish(i, _):
        rows = block(i, RB)
        for k, (source, target) in enumerate(stores):
            pltpu.make_async_copy(source.at[rows], target.at[rows], o_sem.at[k, i]).wait()
        return 0

    lax.fori_loop(0, count[2], finish, 0)
    group.stored(targets, sems)


def down_back_call(group, count, df, stream2, gains, active):
    local, model = df.shape
    hidden = active.shape[1]
    outs = group.out_shapes()
    return pl.pallas_call(
        functools.partial(down_back, group),
        in_specs=[in_smem(), anywhere(), anywhere(), in_vmem(), anywhere()],
        out_specs=(anywhere(),) * len(outs) + (anywhere(), anywhere(), in_vmem()),
        scratch_shapes=[
            pltpu.VMEM((local, model), F32),
            pltpu.VMEM((local, model), F32),
            pltpu.VMEM((local, model), F32),
            pltpu.VMEM((local, hidden), BF),
            pltpu.VMEM((local, model), BF),
            pltpu.VMEM((hidden, model), BF),
            pltpu.SemaphoreType.DMA((3, local // RB)),
            pltpu.SemaphoreType.DMA((2, local // RB)),
            pltpu.SemaphoreType.DMA((2,)),
        ],
        out_shape=tuple(outs) + (shape((local, model), F32), shape((local, model), BF), shape((8, model), F32)),
        compiler_params=params(),
        cost_estimate=cost(10e9),
        name="down_back",
    )(count, df, stream2, gains, active)


def feed_back(down_group, group, count, dh2_ref, dm_ref, h1_ref, gains, gain3, o_any, b_any, slope_any, *rest):
    sources = rest[: 3 if down_group.direct else 2]
    rest = rest[len(sources) :]
    targets = rest[: len(group.out_shapes())]
    (
        dh1_out,
        do_out,
        gain_out,
        w_out,
        w_up,
        w_down,
        g_out,
        g_up,
        o_all,
        b_all,
        slope_all,
        da_all,
        w_sem,
        r_sem,
        g_sem,
    ) = rest[len(targets) :]
    step = pl.program_id(0)
    hidden = w_up.shape[1]
    rows = block(step, RB)
    loads = ((slope_any, slope_all), (o_any, o_all), (b_any, b_all))

    @pl.when(step == 0)
    def _():
        load_feed(down_group, sources, [w_out, w_up, w_down], w_sem, count)
        gain_out[...] = gain3[...]

        def fetch(i, _):
            for k, (source, target) in enumerate(loads):
                pltpu.make_async_copy(
                    source.at[block(i, RB)], target.at[block(i, RB)], r_sem.at[k, i]
                ).start()
            return 0

        lax.fori_loop(0, count[2], fetch, 0)

    def need(k):
        @pl.when(step == 0)
        def _():
            loaded((w_out, w_up, w_down)[k], w_sem.at[k])

    @pl.when(step < count[2])
    def _():
        dm = dm_ref[...]
        for k, (source, target) in enumerate(loads):
            pltpu.make_async_copy(source.at[rows], target.at[rows], r_sem.at[k, step]).wait()
        need(2)
        need(1)

        def chunk(j, held):
            spot = block(j, HC)
            upper = mm_nt(dm, w_down[spot, :])
            found = (upper * slope_all[rows, spot].astype(F32)).astype(BF)
            slope_all[rows, spot] = found
            return held + mm_nt(found, w_up[:, spot])

        db = lax.fori_loop(0, hidden // HC, chunk, jnp.zeros(h1_ref.shape, F32), unroll=3)
        need(0)
        back1, gain2 = rms_back(h1_ref[...], gains[1:2, :], db)
        stream = dh2_ref[...] + back1
        dh1_out[...] = stream
        da = stream.astype(BF)
        da_all[rows, :] = da
        do_out[...] = mm_nt(da, w_out[...]).astype(BF)
        gain_out[...] += jnp.where(iota(gain_out.shape, 0) == 1, gain2, 0.0)

    @pl.when(step == pl.num_programs(0) - 1)
    def _():
        sems = [g_sem.at[k] for k in range(len(targets))]

        def body(live):
            def columns(j, _):
                spot = block(j, HC)
                g_up[:, spot] = mm_tn(b_all[live, :], slope_all[live, spot]).astype(BF)
                return 0

            lax.fori_loop(0, hidden // HC, columns, 0, unroll=3)
            g_out[...] = mm_tn(o_all[live, :], da_all[live, :]).astype(BF)

        over_row_blocks(count, slope_all.shape[0], body)
        group.store([g_out, g_up], targets, sems, count[4], count[5])
        group.stored(targets, sems)


def feed_back_call(down_group, group, count, dh2, dm, stream1, gains, gain3, attended, normed, slope, sources):
    local, model = dh2.shape
    hidden = slope.shape[1]
    outs = group.out_shapes()

    def rows(i, c):
        return (jnp.minimum(i, c[2] - 1), 0)

    def same(i, c):
        return (0, 0)

    narrow = pl.BlockSpec((RB, model), rows)
    fixed = pl.BlockSpec((8, model), same)
    return pl.pallas_call(
        functools.partial(feed_back, down_group, group),
        grid_spec=pltpu.PrefetchScalarGridSpec(
            num_scalar_prefetch=1,
            grid=(local // RB,),
            in_specs=[narrow, narrow, narrow, fixed, fixed] + [anywhere()] * (3 + len(sources)),
            out_specs=(anywhere(),) * len(outs) + (narrow, narrow, fixed),
            scratch_shapes=[
                pltpu.VMEM((model, model), BF),
                pltpu.VMEM((model, hidden), BF),
                pltpu.VMEM((hidden, model), BF),
                pltpu.VMEM((model, model), BF),
                pltpu.VMEM((model, hidden), BF),
                pltpu.VMEM((local, model), BF),
                pltpu.VMEM((local, model), BF),
                pltpu.VMEM((local, hidden), BF),
                pltpu.VMEM((local, model), BF),
                pltpu.SemaphoreType.DMA((3,)),
                pltpu.SemaphoreType.DMA((3, local // RB)),
                pltpu.SemaphoreType.DMA((2,)),
            ],
        ),
        out_shape=tuple(outs)
        + (shape((local, model), F32), shape((local, model), BF), shape((8, model), F32)),
        compiler_params=params(),
        cost_estimate=cost(25e9),
        name="feed_back",
    )(count, dh2, dm, stream1, gains, gain3, attended, normed, slope, *sources)


def project_back(
    groups, blocks, count, dq, aq, xq, dh1, h0, dk, dv, ac, xc, yc, gains, gains23, weight, *rest
):
    targets = rest[: sum(len(group.out_shapes()) for group in groups)]
    total, emb, small, out0, out1, g_sem = rest[len(targets) :]
    step = pl.program_id(0)
    steps = pl.num_programs(0)
    model = dq.shape[1]
    embed = slice(3 * model, 3 * model + LANES)

    @pl.when(step == 0)
    def _():
        total[...] = jnp.zeros(total.shape, F32)
        emb[...] = jnp.zeros(emb.shape, F32)
        small[...] = gains23[...]

    row = iota(small.shape, 0)

    @pl.when(step < count[2])
    def _():
        grad = dq[...]
        upper = mm_nt(grad, weight[:, :model])
        total[:, :model] += mm_tn(aq[...], grad)
        back, gain1 = rms_back(h0[...], gains[0:1, :], upper)
        stream = dh1[...] + back
        emb[...] += mm_tn(stream.astype(BF), xq[...])
        small[...] += jnp.where(row == 0, gain1, 0.0)

    @pl.when((step >= blocks) & (step < blocks + count[3]))
    def _():
        a = ac[...]
        label = yc[:, 0:1]
        stream = mm_nt(xc[...], weight[:, embed]) + label * gains[3:4, :]
        upper = jnp.zeros(stream.shape, F32)
        for part, ref in enumerate((dk, dv)):
            grad = ref[...]
            columns = slice((part + 1) * model, (part + 2) * model)
            upper += mm_nt(grad, weight[:, columns])
            total[:, columns] += mm_tn(a, grad)
        back, gain1 = rms_back(stream, gains[0:1, :], upper)
        emb[...] += mm_tn(back.astype(BF), xc[...])
        small[...] += jnp.where(row == 0, gain1, 0.0) + jnp.where(
            row == 3, jnp.sum(label * back, axis=0, keepdims=True), 0.0
        )

    @pl.when(step == steps - 1)
    def _():
        middle = out0.shape[1]
        out0[...] = total[:, :middle].astype(BF)
        out1[:, : 3 * model - middle] = total[:, middle:].astype(BF)
        out1[:, 3 * model - middle : 3 * model - middle + LANES] = emb[...].astype(BF)
        padded = jnp.concatenate([small[...], jnp.zeros((LANES - 8, small.shape[1]), F32)])
        out1[:, 3 * model - middle + LANES :] = padded.T.astype(BF)
        sems = [g_sem.at[k] for k in range(len(targets))]
        size = len(targets) // 2
        for k, (group, out) in enumerate(zip(groups, (out0, out1))):
            some = slice(k * size, (k + 1) * size)
            group.store([out], targets[some], sems[some], count[4], count[5])
        group.stored(targets, sems)


def project_back_call(groups, count, dq, aq, xq, dh1, h0, dk, dv, ac, xc, yc, gains, gains23, weight):
    local, model = dq.shape
    total = dk.shape[0]
    blocks_q, blocks_c = local // RB, total // CB
    outs = [found for group in groups for found in group.out_shapes()]

    def q_map(i, c):
        return (jnp.minimum(i, c[2] - 1), 0)

    def c_map(i, c):
        return (jnp.clip(i - blocks_q, 0, c[3] - 1), 0)

    def same(i, c):
        return (0, 0)

    query = pl.BlockSpec((RB, model), q_map)
    context = pl.BlockSpec((CB, model), c_map)
    thin = pl.BlockSpec((CB, LANES), c_map)
    fixed = pl.BlockSpec((8, model), same)
    return pl.pallas_call(
        functools.partial(project_back, groups, blocks_q),
        grid_spec=pltpu.PrefetchScalarGridSpec(
            num_scalar_prefetch=1,
            grid=(blocks_q + blocks_c,),
            in_specs=[
                query,
                query,
                pl.BlockSpec((RB, LANES), q_map),
                query,
                query,
                context,
                context,
                context,
                thin,
                thin,
                fixed,
                fixed,
                pl.BlockSpec((model, 3 * model + 2 * LANES), same),
            ],
            out_specs=(anywhere(),) * len(outs),
            scratch_shapes=[
                pltpu.VMEM((model, 3 * model), F32),
                pltpu.VMEM((model, LANES), F32),
                pltpu.VMEM((8, model), F32),
                pltpu.VMEM(groups[0].full_shapes()[0], BF),
                pltpu.VMEM(groups[1].full_shapes()[0], BF),
                pltpu.SemaphoreType.DMA((4,)),
            ],
        ),
        out_shape=tuple(outs),
        compiler_params=params(),
        cost_estimate=cost(20e9),
        name="project_back",
    )(count, dq, aq, xq, dh1, h0, dk, dv, ac, xc, yc, gains, gains23, weight)


def halves(tab, mine):
    other = swap(mine, "tab", 0)
    return jnp.where(tab == 0, mine, other), jnp.where(tab == 0, other, mine)


def on_device(
    count_fsdp,
    features,
    feature_counts,
    row_flags,
    target_bins,
    emb_weight,
    qkv_weight,
    out_weight,
    up_weight,
    down_weight,
    head_weight,
    vectors,
    mom_emb,
    mom_qkv,
    mom_out,
    mom_up,
    mom_down,
    mom_head,
    mom_vectors,
    ema_emb,
    ema_qkv,
    ema_out,
    ema_up,
    ema_down,
    ema_head,
    ema_vectors,
):
    masters = (emb_weight, qkv_weight, out_weight, up_weight, down_weight, head_weight, vectors)
    moms = (mom_emb, mom_qkv, mom_out, mom_up, mom_down, mom_head, mom_vectors)
    emas = (ema_emb, ema_qkv, ema_out, ema_up, ema_down, ema_head, ema_vectors)
    me = lax.axis_index("fsdp").astype(jnp.int32)
    tab = lax.axis_index("tab").astype(jnp.int32)
    local, nfeat = features.shape[1:]
    total = 2 * local
    rows = qkv_weight.shape[0]
    model = rows * count_fsdp
    half = model // 2
    hidden_half = up_weight.shape[1] // 2
    size = model // HEADS
    flags = row_flags[0]
    targets = target_bins[0]

    high_bits = [1 << k for k in reversed(range(1, count_fsdp.bit_length() - 1))]
    x_last = high_bits + ["tab"]
    y_last = high_bits[:-1] + ["tab", high_bits[-1]]
    wide = 3 * model
    quarter = (wide + 2 * LANES) // 4
    groups_a = [Group(order, rows, [(quarter, 1)], count_fsdp) for order in (x_last, y_last)]
    bins = -(-head_weight.shape[1] // HC) * HC
    plain = bins // HC * 7 // 10 * HC
    gather_d = Group(x_last, down_weight.shape[0], [(half, 1)], count_fsdp)
    gather_h = Group(x_last, rows, [((bins - plain) // 2, 1)], count_fsdp)
    groups_b = [
        Group(x_last, rows, [(half, 1), (hidden_half, 1)], count_fsdp),
        Group(y_last, down_weight.shape[0], [(half, 1)], count_fsdp),
    ]

    def side_of(weight, width):
        return jnp.where(tab == 0, weight[:, :width], weight[:, width : 2 * width])

    queries_here = jnp.sum(flags)
    marks = jnp.stack([queries_here // 32, queries_here % 32]).astype(F32)
    first_row = (jnp.arange(rows) == 0).astype(F32)[:, None]

    def tail(block_t):
        used = block_t.shape[0]
        return jnp.concatenate(
            [block_t.T, first_row * marks[None, :], jnp.zeros((rows, LANES - 2 - used), F32)], axis=1
        )

    piece_a = jnp.concatenate(
        [qkv_weight, tail(emb_weight), tail(vectors), out_weight, up_weight], axis=1
    ).astype(BF)
    spare = bins - head_weight.shape[1]
    piece_h = jnp.pad(head_weight[:, plain:], ((0, 0), (0, spare)))
    piece_h = side_of(piece_h, (bins - plain) // 2).astype(BF)

    whole_a = lax.all_gather(piece_a, "fsdp", axis=0, tiled=True)
    moved_d = gather_all(gather_d, side_of(down_weight, half).astype(BF))
    moved_h = gather_all(gather_h, piece_h)

    pack = jnp.concatenate(
        [
            features[0],
            jnp.stack([flags, targets // 64, targets % 64], axis=1).astype(BF),
            jnp.zeros((local, LANES - 3 - nfeat), BF),
        ],
        axis=1,
    )
    lower, upper = halves(tab, pack)
    table = jnp.concatenate([lower, upper])
    flag_rows = table[:, nfeat].astype(F32).reshape(total // LANES, LANES)
    asked = jnp.sum(flag_rows).astype(jnp.int32)
    here = (asked - tab + 1) // 2
    known = total - asked
    count = jnp.stack(
        [
            here,
            known,
            jnp.maximum((here + RB - 1) // RB, 1),
            (known + CB - 1) // CB,
            me,
            tab,
            feature_counts[0],
            jnp.maximum((here + QB - 1) // QB, 1),
        ]
    )
    x_query, t_query, x_context, y_context = sort_rows_call(nfeat, count, table, flag_rows)

    head_plain = after(head_weight[:, :plain].astype(BF), x_query)
    head_plain = lax.all_gather(head_plain, "fsdp", axis=0, tiled=True)
    x_query = after(x_query, moved_d, moved_h)
    queries, keys, values, a_query, a_context, stream0, gains = project_call(
        nfeat, count, x_query, x_context, y_context, whole_a
    )
    row_count = gains[4:5, :LANES]
    row_count = row_count + swap(row_count, "tab", 0)
    attended, logs = attend_call(size, count, queries, keys, values)
    sources_b = [whole_a, *gather_d.sources(*moved_d, me, tab)]
    stream1, normed2, active, slope, stream2, normed3, stats = feed_call(
        gather_d, count, attended, stream0, gains, sources_b
    )
    grad_head, df, loss = head_call(
        gather_h,
        count,
        normed3,
        t_query,
        row_count,
        head_plain,
        gather_h.sources(*moved_h, me, tab),
    )
    shard_h = lax.optimization_barrier(
        lax.psum_scatter(grad_head, "fsdp", scatter_dimension=0, tiled=True)
    )
    group_up, group_down = groups_b
    last = len(high_bits)

    def core_step(group, outs):
        near, far = group.targets(outs, me, tab)
        return near, swap(far, 1, count_fsdp)

    *outs_down, dh2, dm, gain3 = down_back_call(group_down, count, df, stream2, gains, active)
    down = core_step(group_down, outs_down)
    *outs_up, dh1, grad_o, gains23 = feed_back_call(
        gather_d, group_up, count, dh2, dm, stream1, gains, gain3, attended, normed2, slope, sources_b
    )
    up = core_step(group_up, outs_up)
    down = after(down, grad_o)
    sent = scatter_send(group_down, down, last)
    down = scatter_keep(down, sent)
    grad_o = after(grad_o, down[0])
    dq, dk, dv = attend_back_call(size, count, queries, keys, values, grad_o, attended, logs)
    up = after(up, dq)
    down = after(down, dq)
    sent = scatter_send(group_up, up, last)
    up = scatter_keep(up, sent)
    sent = scatter_send(group_down, down, last - 1)
    down = scatter_keep(down, sent)
    dq = after(dq, up[0], down[0])
    outs_a = project_back_call(
        groups_a,
        count,
        dq,
        a_query,
        x_query,
        dh1,
        stream0,
        dk,
        dv,
        a_context,
        x_context,
        y_context,
        gains,
        gains23,
        whole_a,
    )
    size_a = len(groups_a[0].out_shapes())
    low_a = core_step(groups_a[0], outs_a[:size_a])
    high_a = core_step(groups_a[1], outs_a[size_a:])
    up, down = after((up, down), outs_a)
    for at in reversed(range(last + 1)):
        sent_low = scatter_send(groups_a[0], low_a, at)
        sent_high = scatter_send(groups_a[1], high_a, at)
        if at < last:
            sent = scatter_send(group_up, up, at)
            up = scatter_keep(up, sent)
        if at < last - 1:
            sent = scatter_send(group_down, down, at)
            down = scatter_keep(down, sent)
        low_a = scatter_keep(low_a, sent_low)
        high_a = scatter_keep(high_a, sent_high)
        if at == last - 1:
            low_a, shard_h = lax.optimization_barrier((low_a, shard_h))
    shards_a = [added(pair, 0).astype(BF) for pair in (low_a, high_a)]
    shards_b = [added(pair, 0).astype(BF) for pair in (up, down)]

    shard_h = shard_h[:, : head_weight.shape[1]]
    grad_h = shard_h.astype(F32) + swap(shard_h, "tab", 0).astype(F32)
    place = jnp.arange(quarter)[None, :] + (2 + tab) * quarter - wide
    real = (place < nfeat) | ((place >= LANES) & (place < LANES + vectors.shape[0]))
    keep_a = jnp.where(real, shards_a[1].astype(F32), 0.0)
    squares = 0.5 * jnp.sum(grad_h * grad_h)
    for found in (shards_a[0], keep_a, *shards_b):
        found = found.astype(F32)
        squares = squares + jnp.sum(found * found)
    sums = jnp.concatenate([loss[0:1, 0:1], stats[0:3, 0:1], squares.reshape(1, 1)]).reshape(1, 5)
    sums = jnp.broadcast_to(jnp.pad(sums, ((0, 0), (0, LANES - 5))), (8, LANES))
    for step in [1] + high_bits + ["tab"]:
        sums = sums + swap(sums, step, count_fsdp)
    split_a = [halves(tab, found) for found in shards_a]
    split_b = [halves(tab, found) for found in shards_b]
    whole_grad = jnp.concatenate([side for found in split_a for side in found], axis=1).astype(F32)
    grad_qkv = whole_grad[:, :wide]
    grad_emb = whole_grad[:, wide : wide + nfeat].T
    grad_vectors = whole_grad[:, wide + LANES : wide + LANES + vectors.shape[0]].T
    grad_out = jnp.concatenate([side[:, :half] for side in split_b[0]], axis=1)
    grad_up = jnp.concatenate([side[:, half:] for side in split_b[0]], axis=1)
    grad_down = jnp.concatenate(split_b[1], axis=1)
    summed = (grad_emb, grad_qkv, grad_out, grad_up, grad_down, grad_h, grad_vectors)
    loss_sum = sums[0, 0]
    rms_sums = sums[0, 1:4]
    clip_norm = jnp.sqrt(sums[0, 4])
    row_count = row_count[0, 0]
    factor = jnp.minimum(1.0, CLIP / clip_norm)
    new_moms, new_weights, new_emas = ([], [], [])
    for weight, grad, moment, average in zip(masters, summed, moms, emas):
        clipped = grad.astype(F32) * factor
        moment_new = MOMENTUM * moment + clipped
        weight_new = weight - RATE * (clipped + MOMENTUM * moment_new)
        new_moms.append(moment_new)
        new_weights.append(weight_new)
        new_emas.append(AVERAGE * average + (1.0 - AVERAGE) * weight_new)
    return (loss_sum, row_count, rms_sums, clip_norm, *new_moms, *new_weights, *new_emas)


def solution(mesh):
    by_row, by_column = P("fsdp", None), P(None, "fsdp")
    weights = (by_column, by_row, by_row, by_row, by_row, by_row, by_column)
    return jax.shard_map(
        functools.partial(on_device, mesh.shape["fsdp"]),
        mesh=mesh,
        in_specs=(P("fsdp", "tab", None), P("fsdp"), P("fsdp", "tab"), P("fsdp", "tab")) + weights * 3,
        out_specs=(P(), P(), P(), P()) + weights * 3,
        check_vma=False,
    )
```

```python
import functools

import jax
import jax.numpy as jnp
import numpy as np
from jax import lax
from jax.experimental import pallas as pl
from jax.experimental.pallas import tpu as pltpu
from jax.sharding import PartitionSpec as P

HEADS = 12
BINS = 5000
CLIP = 0.005
RATE = 10000.0
MOMENTUM = 0.5
AVERAGE = 0.5

BF = jnp.bfloat16
F32 = jnp.float32
LANES = 128
QB = 256
AB = 256
FB = 256
RB = 512
CB = 512
HC = 512
VMEM = 60 * 1024 * 1024
LOW = -1e30


def mm(left, right):
    return jnp.dot(left, right, preferred_element_type=F32)


def mm_tn(left, right):
    return lax.dot_general(left, right, (((0,), (0,)), ((), ())), preferred_element_type=F32)


def mm_nt(left, right):
    return lax.dot_general(left, right, (((1,), (1,)), ((), ())), preferred_element_type=F32)


def iota(shape, axis):
    return lax.broadcasted_iota(jnp.int32, shape, axis)


def block(index, size):
    return pl.ds(pl.multiple_of(index * size, size), size)


def inverse_rms(stream):
    return lax.rsqrt(jnp.mean(stream * stream, axis=-1, keepdims=True) + 1e-06)


def rms_back(stream, gain, upstream):
    scale = inverse_rms(stream)
    unit = stream * scale
    weighted = upstream * gain
    back = scale * (weighted - unit * jnp.mean(weighted * unit, axis=-1, keepdims=True))
    return back, jnp.sum(upstream * unit, axis=0, keepdims=True)


def params():
    return pltpu.CompilerParams(vmem_limit_bytes=VMEM)


def cost(flops):
    return pl.CostEstimate(flops=int(flops), bytes_accessed=1 << 20, transcendentals=0)


def anywhere():
    return pl.BlockSpec(memory_space=pl.ANY)


def in_vmem():
    return pl.BlockSpec(memory_space=pltpu.VMEM)


def in_smem():
    return pl.BlockSpec(memory_space=pltpu.SMEM)


def shape(dims, dtype):
    return jax.ShapeDtypeStruct(dims, dtype)


class Group:
    def __init__(self, axis_bits, rows, parts, count):
        self.steps = axis_bits
        self.rows = rows
        self.parts = parts
        self.count = count
        self.width = sum(width * blocks for width, blocks in parts)
        self.pieces = 2 ** len(axis_bits)
        self.direct = rows % 16 == 0

    def place(self, piece, core):
        across, half = core, 0
        for bit, step in enumerate(self.steps):
            if piece >> bit & 1:
                if step == "tab":
                    half ^= 1
                else:
                    across ^= step
        return across, half

    def spans(self):
        start = 0
        for part, (width, blocks) in enumerate(self.parts):
            for at in range(blocks):
                yield part, start, width, at, blocks
                start += width

    def full_shapes(self):
        return [(self.count * self.rows * blocks, 2 * width) for width, blocks in self.parts]

    def table(self):
        order = np.zeros((self.count, 2), np.int32)
        for core in range(2):
            for piece in range(self.pieces):
                across, half = self.place(piece, core)
                order[across, half] = core * self.pieces + piece
        return order

    def to_whole(self, near, far, me, tab):
        places = np.arange(self.count, dtype=np.int32)[:, None] ^ me
        sides = np.arange(2, dtype=np.int32)[None, :] ^ tab
        index = jnp.asarray(self.table())[places, sides]
        every = jnp.take(jnp.concatenate([near, far]), index, axis=0)
        every = every.transpose(0, 2, 1, 3)
        whole = [[] for _ in self.parts]
        for part, start, width, _, _ in self.spans():
            whole[part].append(every[..., start : start + width])
        return [
            jnp.stack(found, axis=1).reshape(dims) for found, dims in zip(whole, self.full_shapes())
        ]

    def to_pieces(self, wholes, me, tab):
        columns = []
        for part, _, width, at, blocks in self.spans():
            split = wholes[part].reshape(self.count, blocks, self.rows, 2, width)
            columns.append(split[:, at])
        every = jnp.concatenate(columns, axis=-1).transpose(0, 2, 1, 3)
        every = every.reshape(2 * self.count, self.rows, self.width)
        where = np.array(
            [self.place(piece, core) for core in range(2) for piece in range(self.pieces)], np.int32
        )
        index = (where[:, 0] ^ me) * 2 + (where[:, 1] ^ tab)
        found = jnp.take(every, index, axis=0)
        return found[: self.pieces], found[self.pieces :]

    def pairs(self, wholes, moved, me, tab):
        for core in range(2):
            for piece in range(self.pieces):
                across, half = self.place(piece, core)
                shard = lax.bitwise_xor(me, jnp.int32(across))
                side = lax.bitwise_xor(tab, jnp.int32(half))
                for part, start, width, at, blocks in self.spans():
                    first = pl.multiple_of((shard * blocks + at) * self.rows, self.rows)
                    column = pl.multiple_of(side * width, LANES)
                    yield (
                        wholes[part].at[pl.ds(first, self.rows), pl.ds(column, width)],
                        moved[core].at[piece, :, pl.ds(start, width)],
                        part,
                        core,
                    )

    def load(self, sources, wholes, sems, me, tab):
        if not self.direct:
            for source, whole, sem in zip(sources, wholes, sems):
                pltpu.make_async_copy(source, whole, sem).start()
            return
        for whole, piece, part, _ in self.pairs(wholes, sources, me, tab):
            pltpu.make_async_copy(piece, whole, sems[part]).start()

    def store(self, wholes, targets, sems, me, tab):
        if not self.direct:
            for whole, target, sem in zip(wholes, targets, sems):
                pltpu.make_async_copy(whole, target, sem).start()
            return
        for whole, piece, _, core in self.pairs(wholes, targets, me, tab):
            pltpu.make_async_copy(whole, piece, sems[core]).start()

    def stored(self, targets, sems):
        for target, sem in zip(targets, sems):
            pltpu.make_async_copy(target, target, sem).wait()

    def out_shapes(self):
        if self.direct:
            return [shape((self.pieces, self.rows, self.width), BF)] * 2
        return [shape(dims, BF) for dims in self.full_shapes()]

    def sources(self, near, far, me, tab):
        return [near, far] if self.direct else self.to_whole(near, far, me, tab)

    def targets(self, outs, me, tab):
        return tuple(outs) if self.direct else self.to_pieces(outs, me, tab)


def loaded(whole, sem):
    pltpu.make_async_copy(whole, whole, sem).wait()


def swap(value, step, count):
    if step == "tab":
        return lax.ppermute(value, "tab", [(0, 1), (1, 0)])
    return lax.ppermute(value, "fsdp", [(i, i ^ step) for i in range(count)])


def after(value, *others):
    return lax.optimization_barrier((value, others))[0]


def gather_all(group, piece):
    held = piece[None]
    for step in group.steps:
        held = jnp.concatenate([held, swap(held, step, group.count)])
    return held, swap(held, 1, group.count)


def added(pair, part):
    return pair[0][part].astype(F32) + pair[1][part].astype(F32)


def scatter_send(group, pair, at):
    size = pair[0].shape[0] // 2
    return swap(added(pair, slice(size, None)).astype(BF), group.steps[at], group.count)


def scatter_keep(pair, found):
    size = pair[0].shape[0] // 2
    return added(pair, slice(0, size)).astype(BF), found


def sort_rows(nfeat, count, table, marks, x_query, t_query, x_context, y_context):
    total, _ = table.shape
    rows = total // LANES
    flags = marks[...]
    inside = mm(flags.astype(BF), (iota((LANES, LANES), 0) <= iota((LANES, LANES), 1)).astype(F32).astype(BF))
    sums = jnp.broadcast_to(jnp.sum(flags, axis=1, keepdims=True), (rows, LANES))
    below = (iota((rows, rows), 1) < iota((rows, rows), 0)).astype(F32)
    upto = inside + mm(below.astype(BF), sums.astype(BF))
    spot = (iota((rows, LANES), 0) * LANES + iota((rows, LANES), 1)).astype(F32)
    as_query = jnp.where(flags > 0, upto - 1.0, -1.0)
    as_context = jnp.where(flags > 0, -1.0, spot - upto)
    held = count[6]
    scale = jnp.sqrt(F32(nfeat) / jnp.full((1, LANES), held, jnp.int32).astype(F32))

    def pick(rank, dest):
        hot = jnp.concatenate(
            [(rank[k : k + 1, :] == dest).astype(F32).astype(BF) for k in range(rows)], axis=1
        )
        found = mm(hot, table[...])
        kept = jnp.where(iota(found.shape, 1) < held, found * scale, 0.0).astype(BF)
        return kept, found[:, nfeat + 1 : nfeat + 2] * 64.0 + found[:, nfeat + 2 : nfeat + 3]

    def query(i, _):
        dest = (2 * (i * QB + iota((QB, LANES), 0)) + count[5]).astype(F32)
        kept, target = pick(as_query, dest)
        x_query[block(i, QB), :] = kept
        t_query[block(i, QB), :] = jnp.broadcast_to(target, (QB, LANES))
        return 0

    def context(i, _):
        dest = i * QB + iota((QB, LANES), 0)
        kept, target = pick(as_context, dest.astype(F32))
        x_context[block(i, QB), :] = kept
        label = (jnp.broadcast_to(target, (QB, LANES)) + 0.5) * (2.0 / BINS) - 1.0
        y_context[block(i, QB), :] = jnp.where(dest < count[1], label, 0.0)
        return 0

    lax.fori_loop(0, count[2] * (RB // QB), query, 0)
    lax.fori_loop(0, count[3] * (CB // QB), context, 0)


def sort_rows_call(nfeat, count, table, marks):
    total = table.shape[0]
    local = total // 2
    return pl.pallas_call(
        functools.partial(sort_rows, nfeat),
        out_shape=(
            shape((local, LANES), BF),
            shape((local, LANES), F32),
            shape((total, LANES), BF),
            shape((total, LANES), F32),
        ),
        in_specs=[in_smem(), in_vmem(), in_vmem()],
        out_specs=(in_vmem(),) * 4,
        compiler_params=params(),
        cost_estimate=cost(7e9),
        name="sort_rows",
    )(count, table, marks)


def project(nfeat, blocks, count, x_query, x_context, y_context, weight, q_out, k_out, v_out, aq_out, ac_out, h_out, gains):
    step = pl.program_id(0)
    model = q_out.shape[1]
    embed = slice(3 * model, 3 * model + LANES)

    @pl.when(step == 0)
    def _():
        vectors = weight[:, 3 * model + LANES : 3 * model + 2 * LANES].astype(F32).T
        many = jnp.sum(vectors[4:5, :]) * 32.0 + jnp.sum(vectors[5:6, :])
        gains[...] = jnp.where(iota((8, model), 0) < 4, vectors[:8, :], many)

    def normed(stream):
        return (stream * inverse_rms(stream) * gains[0:1, :]).astype(BF)

    @pl.when(step < count[2])
    def _():
        stream = mm_nt(x_query[...], weight[:, embed])
        h_out[...] = stream
        a = normed(stream)
        aq_out[...] = a
        q_out[...] = mm(a, weight[:, :model]).astype(BF)

    @pl.when((step >= blocks) & (step < blocks + count[3]))
    def _():
        stream = mm_nt(x_context[...], weight[:, embed]) + y_context[:, 0:1] * gains[3:4, :]
        a = normed(stream)
        ac_out[...] = a
        k_out[...] = mm(a, weight[:, model : 2 * model]).astype(BF)
        v_out[...] = mm(a, weight[:, 2 * model : 3 * model]).astype(BF)


def project_call(nfeat, count, x_query, x_context, y_context, weight):
    local, total = x_query.shape[0], x_context.shape[0]
    model = weight.shape[0]
    blocks_q, blocks_c = local // RB, total // CB

    def q_map(i, c):
        return (jnp.minimum(i, c[2] - 1), 0)

    def c_map(i, c):
        return (jnp.clip(i - blocks_q, 0, c[3] - 1), 0)

    def same(i, c):
        return (0, 0)

    return pl.pallas_call(
        functools.partial(project, nfeat, blocks_q),
        grid_spec=pltpu.PrefetchScalarGridSpec(
            num_scalar_prefetch=1,
            grid=(blocks_q + blocks_c,),
            in_specs=[
                pl.BlockSpec((RB, LANES), q_map),
                pl.BlockSpec((CB, LANES), c_map),
                pl.BlockSpec((CB, LANES), c_map),
                pl.BlockSpec((model, 3 * model + 2 * LANES), same),
            ],
            out_specs=(
                pl.BlockSpec((RB, model), q_map),
                pl.BlockSpec((CB, model), c_map),
                pl.BlockSpec((CB, model), c_map),
                pl.BlockSpec((RB, model), q_map),
                pl.BlockSpec((CB, model), c_map),
                pl.BlockSpec((RB, model), q_map),
                pl.BlockSpec((8, model), same),
            ),
        ),
        out_shape=(
            shape((local, model), BF),
            shape((total, model), BF),
            shape((total, model), BF),
            shape((local, model), BF),
            shape((total, model), BF),
            shape((local, model), F32),
            shape((8, model), F32),
        ),
        compiler_params=params(),
        cost_estimate=cost(12e9),
        name="project",
    )(count, x_query, x_context, y_context, weight)


def head_masks(size):
    low = (iota((1, LANES), 1) < size).astype(F32)
    return low.astype(BF), (1.0 - low).astype(BF)


def dead_rows(j, count):
    return jnp.where(j * CB + iota((CB, 1), 0) < count[1], 0.0, LOW)


def clear_rest(ref, count):
    def clear(i, _):
        ref[block(i, QB), :] = jnp.zeros((QB, ref.shape[1]), ref.dtype)
        return 0

    lax.fori_loop(count[7], count[2] * (RB // QB), clear, 0)


def over_blocks(count, total, body):
    for blocks in range(1, total // CB + 1):

        @pl.when(count[3] == blocks)
        def _(blocks=blocks):
            body(blocks)


def context_scores(k_ref, head, blocks, count):
    scores = mm_nt(k_ref[: blocks * CB, :], head)
    tail = scores[-CB:] + dead_rows(blocks - 1, count)
    return tail if blocks == 1 else jnp.concatenate([scores[:-CB], tail])


def attend(size, count, q_ref, k_ref, v_ref, o_ref, lse_ref, v_low, v_high):
    scale = size ** (-0.5)
    masks = head_masks(size)

    def body(blocks):
        live = slice(0, blocks * CB)
        v_low[live, :] = v_ref[live, :] * masks[0] + masks[1]
        v_high[live, :] = v_ref[live, :] * masks[1] + masks[0]

        def over_queries(i, _):
            queries = q_ref[block(i, QB), :] * BF(scale)
            heads = [queries * mask for mask in masks]
            joined = []
            spots = [slice(j * AB, (j + 1) * AB) for j in range(blocks * CB // AB)]
            dead = dead_rows(blocks - 1, count)
            scores = [[mm_nt(k_ref[spot, :], head) for spot in spots] for head in heads]
            for side, parts in enumerate(scores):
                for k in range(CB // AB):
                    at = len(spots) - CB // AB + k
                    parts[at] = parts[at] + dead[k * AB : (k + 1) * AB]
                top = functools.reduce(jnp.maximum, [jnp.max(part, axis=0, keepdims=True) for part in parts])
                sums = jnp.zeros((LANES, QB), F32)
                for spot, part in zip(spots, parts):
                    expo = jnp.exp(part - top)
                    sums = sums + mm_tn((v_low, v_high)[side][spot, :], expo.astype(BF))
                total = sums[(1 - side) * size : (1 - side) * size + 1]
                joined.append((sums * (1.0 / total))[side * size : (side + 1) * size])
                lse_ref[side : side + 1, block(i, QB)] = top + jnp.log(total)
            o_ref[block(i, QB), :] = jnp.concatenate(joined).T.astype(BF)
            return 0

        lax.fori_loop(0, count[7], over_queries, 0)

    over_blocks(count, k_ref.shape[0], body)
    clear_rest(o_ref, count)


def attend_call(size, count, queries, keys, values):
    local, model = queries.shape
    total = keys.shape[0]
    pairs = model // LANES

    def column(i, c):
        return (0, i)

    return pl.pallas_call(
        functools.partial(attend, size),
        grid_spec=pltpu.PrefetchScalarGridSpec(
            num_scalar_prefetch=1,
            grid=(pairs,),
            in_specs=[
                pl.BlockSpec((local, LANES), column),
                pl.BlockSpec((total, LANES), column),
                pl.BlockSpec((total, LANES), column),
            ],
            out_specs=(
                pl.BlockSpec((local, LANES), column),
                pl.BlockSpec((None, 8, local), lambda i, c: (i, 0, 0)),
            ),
            scratch_shapes=[pltpu.VMEM((total, LANES), BF)] * 2,
        ),
        out_shape=(shape((local, model), BF), shape((pairs, 8, local), F32)),
        compiler_params=params(),
        cost_estimate=cost(35e9),
        name="attend",
    )(count, queries, keys, values)


def attend_back(size, count, q_ref, k_ref, v_ref, do_ref, o_ref, lse_ref, dq_ref, dk_ref, dv_ref, dk_sum, dv_sum):
    scale = size ** (-0.5)
    masks = head_masks(size)

    def body(blocks):
        def over_queries(i, _):
            rows = block(i, QB)
            queries = q_ref[rows, :] * BF(scale)
            grads = do_ref[rows, :]
            heads = [queries * mask for mask in masks]
            ups = [grads * mask for mask in masks]
            both_q = jnp.concatenate(heads)
            both_up = jnp.concatenate(ups)
            product = (grads.astype(F32) * o_ref[rows, :].astype(F32)).T
            back, probs, joined = [], [], []
            live = slice(0, blocks * CB)
            for side, head in enumerate(heads):
                delta = jnp.sum(product[side * size : (side + 1) * size], axis=0, keepdims=True)
                prob = jnp.exp(context_scores(k_ref, head, blocks, count) - lse_ref[side : side + 1, rows])
                upper = mm_nt(v_ref[live, :], ups[side])
                found = (prob * (upper - delta)).astype(BF)
                joined.append(mm_tn(k_ref[live, :], found)[side * size : (side + 1) * size])
                back.append(found)
                probs.append(prob.astype(BF))
            dq_ref[rows, :] = (jnp.concatenate(joined).T * scale).astype(BF)

            dk = mm(jnp.concatenate(back, axis=1), both_q)
            dv = mm(jnp.concatenate(probs, axis=1), both_up)
            dk_sum[live, :] = jnp.where(i == 0, 0.0, dk_sum[live, :]) + dk
            dv_sum[live, :] = jnp.where(i == 0, 0.0, dv_sum[live, :]) + dv
            return 0

        lax.fori_loop(0, count[7], over_queries, 0)

    over_blocks(count, k_ref.shape[0], body)
    clear_rest(dq_ref, count)

    def out(j, _):
        spot = block(j, CB)
        dk_ref[spot, :] = dk_sum[spot, :].astype(BF)
        dv_ref[spot, :] = dv_sum[spot, :].astype(BF)
        return 0

    lax.fori_loop(0, count[3], out, 0)


def attend_back_call(size, count, queries, keys, values, grads, outs, logs):
    local, model = queries.shape
    total = keys.shape[0]
    pairs = model // LANES

    def column(i, c):
        return (0, i)

    narrow = pl.BlockSpec((local, LANES), column)
    wide = pl.BlockSpec((total, LANES), column)
    return pl.pallas_call(
        functools.partial(attend_back, size),
        grid_spec=pltpu.PrefetchScalarGridSpec(
            num_scalar_prefetch=1,
            grid=(pairs,),
            in_specs=[
                narrow,
                wide,
                wide,
                narrow,
                narrow,
                pl.BlockSpec((None, 8, local), lambda i, c: (i, 0, 0)),
            ],
            out_specs=(narrow, wide, wide),
            scratch_shapes=[pltpu.VMEM((total, LANES), F32)] * 2,
        ),
        out_shape=(shape((local, model), BF), shape((total, model), BF), shape((total, model), BF)),
        compiler_params=params(),
        cost_estimate=cost(35e9),
        name="attend_back",
    )(count, queries, keys, values, grads, outs, logs)


def live_rows(i, count, size=RB):
    return (i * size + iota((size, 1), 0) < count[0]).astype(F32)


def row_total(values, live):
    return jnp.sum(jnp.sqrt(jnp.mean(values * values, axis=-1, keepdims=True) + 1e-06) * live)


def gelu_both(value):
    inner = 0.7978845608028654 * (value + 0.044715 * value * value * value)
    bend = jnp.tanh(inner)
    slope = 0.7978845608028654 * (1.0 + 3.0 * 0.044715 * value * value)
    return 0.5 * value * (1.0 + bend), 0.5 * (1.0 + bend) + 0.5 * value * (1.0 - bend * bend) * slope


def load_feed(group, sources, wholes, sem, count):
    w_out, w_up, w_down = wholes
    start = sources[0].shape[1] - w_up.shape[1]
    out = sources[0].at[:, pl.ds(start - w_out.shape[1], w_out.shape[1])]
    pltpu.make_async_copy(out, w_out, sem.at[0]).start()
    pltpu.make_async_copy(sources[0].at[:, pl.ds(start, w_up.shape[1])], w_up, sem.at[1]).start()
    group.load(sources[1:], [w_down], [sem.at[2]], count[4], count[5])


def feed(down_group, count, o_ref, h_ref, gains, *rest):
    sources = rest[: 3 if down_group.direct else 2]
    (h1_out, b_out, z_out, slope_out, h2_out, f_out, stats, w_out, w_up, w_down, sem) = rest[len(sources) :]
    step = pl.program_id(0)
    hidden = w_up.shape[1]

    @pl.when(step == 0)
    def _():
        load_feed(down_group, sources, [w_out, w_up, w_down], sem, count)
        stats[...] = jnp.zeros(stats.shape, F32)

    def need(k):
        @pl.when(step == 0)
        def _():
            loaded((w_out, w_up, w_down)[k], sem.at[k])

    @pl.when(step < count[2] * (RB // FB))
    def _():
        live = live_rows(step, count, FB)
        attended = o_ref[...]
        need(0)
        branch = mm(attended, w_out[...])
        stream1 = h_ref[...] + branch
        h1_out[...] = stream1
        normed = (stream1 * inverse_rms(stream1) * gains[1:2, :]).astype(BF)
        b_out[...] = normed

        need(1)

        def chunk(j, _):
            value, slope = gelu_both(mm(normed, w_up[:, block(j, HC)]))
            z_out[:, block(j, HC)] = value.astype(BF)
            slope_out[:, block(j, HC)] = slope.astype(BF)
            return 0

        lax.fori_loop(0, hidden // HC, chunk, 0, unroll=3)
        need(2)
        branch2 = mm(z_out[...], w_down[...])
        stream2 = stream1 + branch2
        h2_out[...] = stream2
        f_out[...] = (stream2 * inverse_rms(stream2) * gains[2:3, :]).astype(BF)
        row = iota(stats.shape, 0)
        stats[...] += (
            jnp.where(row == 0, row_total(stream2, live), 0.0)
            + jnp.where(row == 1, row_total(branch, live), 0.0)
            + jnp.where(row == 2, row_total(branch2, live), 0.0)
        )


def feed_call(down_group, count, attended, stream0, gains, sources):
    local, model = attended.shape
    hidden = down_group.full_shapes()[0][0]
    whole = [(model, model), (model, hidden), (hidden, model)]

    def rows(i, c):
        return (jnp.minimum(i, c[2] * (RB // FB) - 1), 0)

    def same(i, c):
        return (0, 0)

    narrow = pl.BlockSpec((FB, model), rows)
    wide = pl.BlockSpec((FB, hidden), rows)
    return pl.pallas_call(
        functools.partial(feed, down_group),
        grid_spec=pltpu.PrefetchScalarGridSpec(
            num_scalar_prefetch=1,
            grid=(local // FB,),
            in_specs=[narrow, narrow, pl.BlockSpec((8, model), same)] + [anywhere()] * len(sources),
            out_specs=(narrow, narrow, wide, wide, narrow, narrow, pl.BlockSpec((8, LANES), same)),
            scratch_shapes=[pltpu.VMEM(dims, BF) for dims in whole] + [pltpu.SemaphoreType.DMA((3,))],
        ),
        out_shape=(
            shape((local, model), F32),
            shape((local, model), BF),
            shape((local, hidden), BF),
            shape((local, hidden), BF),
            shape((local, model), F32),
            shape((local, model), BF),
            shape((8, LANES), F32),
        ),
        compiler_params=params(),
        cost_estimate=cost(20e9),
        name="feed",
    )(count, attended, stream0, gains, *sources)


def by_lanes(fold, held, value):
    for k in range(value.shape[1] // LANES):
        held = fold(held, value[:, k * LANES : (k + 1) * LANES])
    return held


def head(group, count, f_ref, t_ref, rows_all, weight_any, *rest):
    sources = rest[: 2 if group.direct else 1]
    (grad_any, df_any, loss, weight, grad, df_ref, logits, back, flipped, sems) = rest[len(sources) :]
    chunks = weight.shape[1] // HC
    plain = weight_any.shape[1] // HC
    moved = weight.at[:, pl.ds(plain * HC, (chunks - plain) * HC)]

    def weight_copy(j):
        return pltpu.make_async_copy(
            weight_any.at[:, block(j, HC)], weight.at[:, block(j, HC)], sems.at[0, j]
        )

    def grad_copy(j):
        return pltpu.make_async_copy(
            grad.at[:, block(j, HC)], grad_any.at[:, block(j, HC)], sems.at[1, j]
        )

    def df_copy(i):
        return pltpu.make_async_copy(
            df_ref.at[block(i, RB), :], df_any.at[block(i, RB), :], sems.at[2, i]
        )

    for j in range(plain):
        weight_copy(j).start()
    group.load(sources, [moved], [sems.at[0, plain]], count[4], count[5])
    loss[...] = jnp.zeros(loss.shape, F32)
    model = f_ref.shape[1]
    lane = iota((RB, HC), 1)

    def over_rows(i, _):
        rows = block(i, RB)
        normed = f_ref[rows, :]
        flipped[:, rows] = normed.astype(F32).T.astype(BF)
        target = t_ref[rows, 0:1].astype(jnp.int32)
        live = live_rows(i, count)

        def first(j, top):
            @pl.when((i == 0) & (j < plain))
            def _():
                weight_copy(j).wait()

            value = mm(normed, weight[:, block(j, HC)])
            logits[:, block(j, HC)] = value
            return by_lanes(jnp.maximum, top, value)

        top = lax.fori_loop(0, plain, first, jnp.full((RB, LANES), 3.0 * LOW, F32), unroll=plain)

        @pl.when(i == 0)
        def _():
            loaded(moved, sems.at[0, plain])

        for j in range(plain, chunks):
            value = mm(normed, weight[:, j * HC : (j + 1) * HC])
            if (j + 1) * HC > BINS:
                value = jnp.where(lane < BINS - j * HC, value, LOW)
            logits[:, j * HC : (j + 1) * HC] = value
            top = by_lanes(jnp.maximum, top, value)
        top = jnp.max(top, axis=1, keepdims=True)

        def second(j, carry):
            total, hit = carry
            value = logits[:, block(j, HC)]
            expo = jnp.exp(value - top)
            logits[:, block(j, HC)] = expo
            hit = by_lanes(jnp.add, hit, jnp.where(lane == target - j * HC, value, 0.0))
            return by_lanes(jnp.add, total, expo), hit

        zero = jnp.zeros((RB, LANES), F32)
        total, hit = lax.fori_loop(0, chunks, second, (zero, zero), unroll=5)
        total = jnp.sum(total, axis=1, keepdims=True)
        hit = jnp.sum(hit, axis=1, keepdims=True)
        part = live / rows_all[0:1, 0:1]
        share = part / total

        def third(j, held):
            hot = jnp.where(lane == target - j * HC, part, 0.0)
            found = (logits[:, block(j, HC)] * share - hot).astype(BF)
            back[rows, block(j, HC)] = found
            return held + mm_nt(found, weight[:, block(j, HC)])

        df_ref[rows, :] = lax.fori_loop(0, chunks, third, jnp.zeros((RB, model), F32), unroll=5)
        df_copy(i).start()
        loss[...] += jnp.sum(live * (top + jnp.log(total) - hit))
        return 0

    lax.fori_loop(0, count[2], over_rows, 0)

    for blocks in range(1, f_ref.shape[0] // RB + 1):

        @pl.when(count[2] == blocks)
        def _(blocks=blocks):
            def over_columns(j, _):
                grad[:, block(j, HC)] = mm(
                    flipped[:, : blocks * RB], back[: blocks * RB, block(j, HC)]
                ).astype(BF)
                grad_copy(j).start()
                return 0

            lax.fori_loop(0, chunks, over_columns, 0, unroll=5)
            for i in range(blocks):
                df_copy(i).wait()

    for j in range(chunks):
        grad_copy(j).wait()


def head_call(group, count, normed, targets, rows_all, weight, sources):
    local, model = normed.shape
    bins = weight.shape[1] + group.full_shapes()[0][1]
    return pl.pallas_call(
        functools.partial(head, group),
        out_shape=(shape((model, bins), BF), shape((local, model), F32), shape((8, LANES), F32)),
        in_specs=[in_smem()] + [in_vmem()] * 3 + [anywhere()] * (1 + len(sources)),
        out_specs=(anywhere(), anywhere(), in_vmem()),
        scratch_shapes=[
            pltpu.VMEM((model, bins), BF),
            pltpu.VMEM((model, bins), BF),
            pltpu.VMEM((local, model), F32),
            pltpu.VMEM((RB, bins), F32),
            pltpu.VMEM((local, bins), BF),
            pltpu.VMEM((model, local), BF),
            pltpu.SemaphoreType.DMA((3, bins // HC)),
        ],
        compiler_params=params(),
        cost_estimate=cost(35e9),
        name="head",
    )(count, normed, targets, rows_all, weight, *sources)


def over_row_blocks(count, total, body):
    for blocks in range(1, total // RB + 1):

        @pl.when(count[2] == blocks)
        def _(blocks=blocks):
            body(slice(0, blocks * RB))


def down_back(group, count, df_any, h2_any, gains, z_any, *rest):
    targets = rest[: len(group.out_shapes())]
    (dh2_out, dm_out, gain_out, df_all, h2_all, dh2_all, z_all, dm_all, g_down, r_sem, o_sem, g_sem) = rest[
        len(targets) :
    ]
    hidden = z_all.shape[1]
    loads = ((df_any, df_all), (h2_any, h2_all), (z_any, z_all))
    stores = ((dh2_all, dh2_out), (dm_all, dm_out))
    gain_out[...] = jnp.zeros(gain_out.shape, F32)

    def fetch(i, _):
        for k, (source, target) in enumerate(loads):
            pltpu.make_async_copy(source.at[block(i, RB)], target.at[block(i, RB)], r_sem.at[k, i]).start()
        return 0

    lax.fori_loop(0, count[2], fetch, 0)

    def over_rows(i, _):
        rows = block(i, RB)
        for k, (source, target) in enumerate(loads[:2]):
            pltpu.make_async_copy(source.at[rows], target.at[rows], r_sem.at[k, i]).wait()
        back, gain3 = rms_back(h2_all[rows, :], gains[2:3, :], df_all[rows, :])
        dh2_all[rows, :] = back
        dm_all[rows, :] = back.astype(BF)
        gain_out[...] += jnp.where(iota(gain_out.shape, 0) == 2, gain3, 0.0)
        for k, (source, target) in enumerate(stores):
            pltpu.make_async_copy(source.at[rows], target.at[rows], o_sem.at[k, i]).start()
        pltpu.make_async_copy(z_any.at[rows], z_all.at[rows], r_sem.at[2, i]).wait()
        return 0

    lax.fori_loop(0, count[2], over_rows, 0)
    sems = [g_sem.at[k] for k in range(len(targets))]

    def body(live):
        def columns(j, _):
            spot = block(j, HC)
            g_down[spot, :] = mm_tn(z_all[live, spot], dm_all[live, :]).astype(BF)
            return 0

        lax.fori_loop(0, hidden // HC, columns, 0, unroll=3)

    over_row_blocks(count, z_all.shape[0], body)
    group.store([g_down], targets, sems, count[4], count[5])

    def finish(i, _):
        rows = block(i, RB)
        for k, (source, target) in enumerate(stores):
            pltpu.make_async_copy(source.at[rows], target.at[rows], o_sem.at[k, i]).wait()
        return 0

    lax.fori_loop(0, count[2], finish, 0)
    group.stored(targets, sems)


def down_back_call(group, count, df, stream2, gains, active):
    local, model = df.shape
    hidden = active.shape[1]
    outs = group.out_shapes()
    return pl.pallas_call(
        functools.partial(down_back, group),
        in_specs=[in_smem(), anywhere(), anywhere(), in_vmem(), anywhere()],
        out_specs=(anywhere(),) * len(outs) + (anywhere(), anywhere(), in_vmem()),
        scratch_shapes=[
            pltpu.VMEM((local, model), F32),
            pltpu.VMEM((local, model), F32),
            pltpu.VMEM((local, model), F32),
            pltpu.VMEM((local, hidden), BF),
            pltpu.VMEM((local, model), BF),
            pltpu.VMEM((hidden, model), BF),
            pltpu.SemaphoreType.DMA((3, local // RB)),
            pltpu.SemaphoreType.DMA((2, local // RB)),
            pltpu.SemaphoreType.DMA((2,)),
        ],
        out_shape=tuple(outs) + (shape((local, model), F32), shape((local, model), BF), shape((8, model), F32)),
        compiler_params=params(),
        cost_estimate=cost(10e9),
        name="down_back",
    )(count, df, stream2, gains, active)


def feed_back(down_group, group, count, dh2_ref, dm_ref, h1_ref, gains, gain3, o_any, b_any, slope_any, *rest):
    sources = rest[: 3 if down_group.direct else 2]
    rest = rest[len(sources) :]
    targets = rest[: len(group.out_shapes())]
    (
        dh1_out,
        do_out,
        gain_out,
        w_out,
        w_up,
        w_down,
        g_out,
        g_up,
        o_all,
        b_all,
        slope_all,
        da_all,
        w_sem,
        r_sem,
        g_sem,
    ) = rest[len(targets) :]
    step = pl.program_id(0)
    hidden = w_up.shape[1]
    rows = block(step, RB)
    loads = ((slope_any, slope_all), (o_any, o_all), (b_any, b_all))

    @pl.when(step == 0)
    def _():
        load_feed(down_group, sources, [w_out, w_up, w_down], w_sem, count)
        gain_out[...] = gain3[...]

        def fetch(i, _):
            for k, (source, target) in enumerate(loads):
                pltpu.make_async_copy(
                    source.at[block(i, RB)], target.at[block(i, RB)], r_sem.at[k, i]
                ).start()
            return 0

        lax.fori_loop(0, count[2], fetch, 0)

    def need(k):
        @pl.when(step == 0)
        def _():
            loaded((w_out, w_up, w_down)[k], w_sem.at[k])

    @pl.when(step < count[2])
    def _():
        dm = dm_ref[...]
        for k, (source, target) in enumerate(loads):
            pltpu.make_async_copy(source.at[rows], target.at[rows], r_sem.at[k, step]).wait()
        need(2)
        need(1)

        def chunk(j, held):
            spot = block(j, HC)
            upper = mm_nt(dm, w_down[spot, :])
            found = (upper * slope_all[rows, spot].astype(F32)).astype(BF)
            slope_all[rows, spot] = found
            return held + mm_nt(found, w_up[:, spot])

        db = lax.fori_loop(0, hidden // HC, chunk, jnp.zeros(h1_ref.shape, F32), unroll=3)
        need(0)
        back1, gain2 = rms_back(h1_ref[...], gains[1:2, :], db)
        stream = dh2_ref[...] + back1
        dh1_out[...] = stream
        da = stream.astype(BF)
        da_all[rows, :] = da
        do_out[...] = mm_nt(da, w_out[...]).astype(BF)
        gain_out[...] += jnp.where(iota(gain_out.shape, 0) == 1, gain2, 0.0)

    @pl.when(step == pl.num_programs(0) - 1)
    def _():
        sems = [g_sem.at[k] for k in range(len(targets))]

        def body(live):
            def columns(j, _):
                spot = block(j, HC)
                g_up[:, spot] = mm_tn(b_all[live, :], slope_all[live, spot]).astype(BF)
                return 0

            lax.fori_loop(0, hidden // HC, columns, 0, unroll=3)
            g_out[...] = mm_tn(o_all[live, :], da_all[live, :]).astype(BF)

        over_row_blocks(count, slope_all.shape[0], body)
        group.store([g_out, g_up], targets, sems, count[4], count[5])
        group.stored(targets, sems)


def feed_back_call(down_group, group, count, dh2, dm, stream1, gains, gain3, attended, normed, slope, sources):
    local, model = dh2.shape
    hidden = slope.shape[1]
    outs = group.out_shapes()

    def rows(i, c):
        return (jnp.minimum(i, c[2] - 1), 0)

    def same(i, c):
        return (0, 0)

    narrow = pl.BlockSpec((RB, model), rows)
    fixed = pl.BlockSpec((8, model), same)
    return pl.pallas_call(
        functools.partial(feed_back, down_group, group),
        grid_spec=pltpu.PrefetchScalarGridSpec(
            num_scalar_prefetch=1,
            grid=(local // RB,),
            in_specs=[narrow, narrow, narrow, fixed, fixed] + [anywhere()] * (3 + len(sources)),
            out_specs=(anywhere(),) * len(outs) + (narrow, narrow, fixed),
            scratch_shapes=[
                pltpu.VMEM((model, model), BF),
                pltpu.VMEM((model, hidden), BF),
                pltpu.VMEM((hidden, model), BF),
                pltpu.VMEM((model, model), BF),
                pltpu.VMEM((model, hidden), BF),
                pltpu.VMEM((local, model), BF),
                pltpu.VMEM((local, model), BF),
                pltpu.VMEM((local, hidden), BF),
                pltpu.VMEM((local, model), BF),
                pltpu.SemaphoreType.DMA((3,)),
                pltpu.SemaphoreType.DMA((3, local // RB)),
                pltpu.SemaphoreType.DMA((2,)),
            ],
        ),
        out_shape=tuple(outs)
        + (shape((local, model), F32), shape((local, model), BF), shape((8, model), F32)),
        compiler_params=params(),
        cost_estimate=cost(25e9),
        name="feed_back",
    )(count, dh2, dm, stream1, gains, gain3, attended, normed, slope, *sources)


def project_back(
    groups, blocks, count, dq, aq, xq, dh1, h0, dk, dv, ac, xc, yc, gains, gains23, weight, *rest
):
    targets = rest[: sum(len(group.out_shapes()) for group in groups)]
    total, emb, small, out0, out1, g_sem = rest[len(targets) :]
    step = pl.program_id(0)
    steps = pl.num_programs(0)
    model = dq.shape[1]
    embed = slice(3 * model, 3 * model + LANES)

    @pl.when(step == 0)
    def _():
        total[...] = jnp.zeros(total.shape, F32)
        emb[...] = jnp.zeros(emb.shape, F32)
        small[...] = gains23[...]

    row = iota(small.shape, 0)

    @pl.when(step < count[2])
    def _():
        grad = dq[...]
        upper = mm_nt(grad, weight[:, :model])
        total[:, :model] += mm_tn(aq[...], grad)
        back, gain1 = rms_back(h0[...], gains[0:1, :], upper)
        stream = dh1[...] + back
        emb[...] += mm_tn(stream.astype(BF), xq[...])
        small[...] += jnp.where(row == 0, gain1, 0.0)

    @pl.when((step >= blocks) & (step < blocks + count[3]))
    def _():
        a = ac[...]
        label = yc[:, 0:1]
        stream = mm_nt(xc[...], weight[:, embed]) + label * gains[3:4, :]
        upper = jnp.zeros(stream.shape, F32)
        for part, ref in enumerate((dk, dv)):
            grad = ref[...]
            columns = slice((part + 1) * model, (part + 2) * model)
            upper += mm_nt(grad, weight[:, columns])
            total[:, columns] += mm_tn(a, grad)
        back, gain1 = rms_back(stream, gains[0:1, :], upper)
        emb[...] += mm_tn(back.astype(BF), xc[...])
        small[...] += jnp.where(row == 0, gain1, 0.0) + jnp.where(
            row == 3, jnp.sum(label * back, axis=0, keepdims=True), 0.0
        )

    @pl.when(step == steps - 1)
    def _():
        middle = out0.shape[1]
        out0[...] = total[:, :middle].astype(BF)
        out1[:, : 3 * model - middle] = total[:, middle:].astype(BF)
        out1[:, 3 * model - middle : 3 * model - middle + LANES] = emb[...].astype(BF)
        padded = jnp.concatenate([small[...], jnp.zeros((LANES - 8, small.shape[1]), F32)])
        out1[:, 3 * model - middle + LANES :] = padded.T.astype(BF)
        sems = [g_sem.at[k] for k in range(len(targets))]
        size = len(targets) // 2
        for k, (group, out) in enumerate(zip(groups, (out0, out1))):
            some = slice(k * size, (k + 1) * size)
            group.store([out], targets[some], sems[some], count[4], count[5])
        group.stored(targets, sems)


def project_back_call(groups, count, dq, aq, xq, dh1, h0, dk, dv, ac, xc, yc, gains, gains23, weight):
    local, model = dq.shape
    total = dk.shape[0]
    blocks_q, blocks_c = local // RB, total // CB
    outs = [found for group in groups for found in group.out_shapes()]

    def q_map(i, c):
        return (jnp.minimum(i, c[2] - 1), 0)

    def c_map(i, c):
        return (jnp.clip(i - blocks_q, 0, c[3] - 1), 0)

    def same(i, c):
        return (0, 0)

    query = pl.BlockSpec((RB, model), q_map)
    context = pl.BlockSpec((CB, model), c_map)
    thin = pl.BlockSpec((CB, LANES), c_map)
    fixed = pl.BlockSpec((8, model), same)
    return pl.pallas_call(
        functools.partial(project_back, groups, blocks_q),
        grid_spec=pltpu.PrefetchScalarGridSpec(
            num_scalar_prefetch=1,
            grid=(blocks_q + blocks_c,),
            in_specs=[
                query,
                query,
                pl.BlockSpec((RB, LANES), q_map),
                query,
                query,
                context,
                context,
                context,
                thin,
                thin,
                fixed,
                fixed,
                pl.BlockSpec((model, 3 * model + 2 * LANES), same),
            ],
            out_specs=(anywhere(),) * len(outs),
            scratch_shapes=[
                pltpu.VMEM((model, 3 * model), F32),
                pltpu.VMEM((model, LANES), F32),
                pltpu.VMEM((8, model), F32),
                pltpu.VMEM(groups[0].full_shapes()[0], BF),
                pltpu.VMEM(groups[1].full_shapes()[0], BF),
                pltpu.SemaphoreType.DMA((4,)),
            ],
        ),
        out_shape=tuple(outs),
        compiler_params=params(),
        cost_estimate=cost(20e9),
        name="project_back",
    )(count, dq, aq, xq, dh1, h0, dk, dv, ac, xc, yc, gains, gains23, weight)


def halves(tab, mine):
    other = swap(mine, "tab", 0)
    return jnp.where(tab == 0, mine, other), jnp.where(tab == 0, other, mine)


def on_device(
    count_fsdp,
    features,
    feature_counts,
    row_flags,
    target_bins,
    emb_weight,
    qkv_weight,
    out_weight,
    up_weight,
    down_weight,
    head_weight,
    vectors,
    mom_emb,
    mom_qkv,
    mom_out,
    mom_up,
    mom_down,
    mom_head,
    mom_vectors,
    ema_emb,
    ema_qkv,
    ema_out,
    ema_up,
    ema_down,
    ema_head,
    ema_vectors,
):
    masters = (emb_weight, qkv_weight, out_weight, up_weight, down_weight, head_weight, vectors)
    moms = (mom_emb, mom_qkv, mom_out, mom_up, mom_down, mom_head, mom_vectors)
    emas = (ema_emb, ema_qkv, ema_out, ema_up, ema_down, ema_head, ema_vectors)
    me = lax.axis_index("fsdp").astype(jnp.int32)
    tab = lax.axis_index("tab").astype(jnp.int32)
    local, nfeat = features.shape[1:]
    total = 2 * local
    rows = qkv_weight.shape[0]
    model = rows * count_fsdp
    half = model // 2
    hidden_half = up_weight.shape[1] // 2
    size = model // HEADS
    flags = row_flags[0]
    targets = target_bins[0]

    high_bits = [1 << k for k in reversed(range(1, count_fsdp.bit_length() - 1))]
    x_last = high_bits + ["tab"]
    y_last = high_bits[:-1] + ["tab", high_bits[-1]]
    wide = 3 * model
    quarter = (wide + 2 * LANES) // 4
    groups_a = [Group(order, rows, [(quarter, 1)], count_fsdp) for order in (x_last, y_last)]
    bins = -(-head_weight.shape[1] // HC) * HC
    plain = bins // HC * 7 // 10 * HC
    gather_d = Group(x_last, down_weight.shape[0], [(half, 1)], count_fsdp)
    gather_h = Group(x_last, rows, [((bins - plain) // 2, 1)], count_fsdp)
    groups_b = [
        Group(x_last, rows, [(half, 1), (hidden_half, 1)], count_fsdp),
        Group(x_last, down_weight.shape[0], [(half, 1)], count_fsdp),
    ]

    def side_of(weight, width):
        return jnp.where(tab == 0, weight[:, :width], weight[:, width : 2 * width])

    queries_here = jnp.sum(flags)
    marks = jnp.stack([queries_here // 32, queries_here % 32]).astype(F32)
    first_row = (jnp.arange(rows) == 0).astype(F32)[:, None]

    def tail(block_t):
        used = block_t.shape[0]
        return jnp.concatenate(
            [block_t.T, first_row * marks[None, :], jnp.zeros((rows, LANES - 2 - used), F32)], axis=1
        )

    piece_a = jnp.concatenate(
        [qkv_weight, tail(emb_weight), tail(vectors), out_weight, up_weight], axis=1
    ).astype(BF)
    spare = bins - head_weight.shape[1]
    piece_h = jnp.pad(head_weight[:, plain:], ((0, 0), (0, spare)))
    piece_h = side_of(piece_h, (bins - plain) // 2).astype(BF)

    whole_a = lax.all_gather(piece_a, "fsdp", axis=0, tiled=True)
    moved_d = gather_all(gather_d, side_of(down_weight, half).astype(BF))
    moved_h = gather_all(gather_h, piece_h)

    pack = jnp.concatenate(
        [
            features[0],
            jnp.stack([flags, targets // 64, targets % 64], axis=1).astype(BF),
            jnp.zeros((local, LANES - 3 - nfeat), BF),
        ],
        axis=1,
    )
    lower, upper = halves(tab, pack)
    table = jnp.concatenate([lower, upper])
    flag_rows = table[:, nfeat].astype(F32).reshape(total // LANES, LANES)
    asked = jnp.sum(flag_rows).astype(jnp.int32)
    here = (asked - tab + 1) // 2
    known = total - asked
    count = jnp.stack(
        [
            here,
            known,
            jnp.maximum((here + RB - 1) // RB, 1),
            (known + CB - 1) // CB,
            me,
            tab,
            feature_counts[0],
            jnp.maximum((here + QB - 1) // QB, 1),
        ]
    )
    x_query, t_query, x_context, y_context = sort_rows_call(nfeat, count, table, flag_rows)

    head_plain = after(head_weight[:, :plain].astype(BF), x_query)
    head_plain = lax.all_gather(head_plain, "fsdp", axis=0, tiled=True)
    x_query = after(x_query, moved_d, moved_h)
    queries, keys, values, a_query, a_context, stream0, gains = project_call(
        nfeat, count, x_query, x_context, y_context, whole_a
    )
    row_count = gains[4:5, :LANES]
    row_count = row_count + swap(row_count, "tab", 0)
    attended, logs = attend_call(size, count, queries, keys, values)
    sources_b = [whole_a, *gather_d.sources(*moved_d, me, tab)]
    stream1, normed2, active, slope, stream2, normed3, stats = feed_call(
        gather_d, count, attended, stream0, gains, sources_b
    )
    grad_head, df, loss = head_call(
        gather_h,
        count,
        normed3,
        t_query,
        row_count,
        head_plain,
        gather_h.sources(*moved_h, me, tab),
    )
    shard_h = lax.optimization_barrier(
        lax.psum_scatter(grad_head, "fsdp", scatter_dimension=0, tiled=True)
    )
    group_up, group_down = groups_b
    last = len(high_bits)

    def core_step(group, outs):
        near, far = group.targets(outs, me, tab)
        return near, swap(far, 1, count_fsdp)

    *outs_down, dh2, dm, gain3 = down_back_call(group_down, count, df, stream2, gains, active)
    down = core_step(group_down, outs_down)
    *outs_up, dh1, grad_o, gains23 = feed_back_call(
        gather_d, group_up, count, dh2, dm, stream1, gains, gain3, attended, normed2, slope, sources_b
    )
    up = core_step(group_up, outs_up)
    down = after(down, grad_o)
    sent = scatter_send(group_down, down, last)
    down = scatter_keep(down, sent)
    grad_o = after(grad_o, down[0])
    dq, dk, dv = attend_back_call(size, count, queries, keys, values, grad_o, attended, logs)
    up = after(up, dq)
    down = after(down, dq)
    sent = scatter_send(group_up, up, last)
    up = scatter_keep(up, sent)
    sent = scatter_send(group_down, down, last - 1)
    down = scatter_keep(down, sent)
    dq = after(dq, up[0], down[0])
    outs_a = project_back_call(
        groups_a,
        count,
        dq,
        a_query,
        x_query,
        dh1,
        stream0,
        dk,
        dv,
        a_context,
        x_context,
        y_context,
        gains,
        gains23,
        whole_a,
    )
    size_a = len(groups_a[0].out_shapes())
    low_a = core_step(groups_a[0], outs_a[:size_a])
    high_a = core_step(groups_a[1], outs_a[size_a:])
    up, down = after((up, down), outs_a)
    for at in reversed(range(last + 1)):
        sent_low = scatter_send(groups_a[0], low_a, at)
        sent_high = scatter_send(groups_a[1], high_a, at)
        if at < last:
            sent = scatter_send(group_up, up, at)
            up = scatter_keep(up, sent)
        if at < last - 1:
            sent = scatter_send(group_down, down, at)
            down = scatter_keep(down, sent)
        low_a = scatter_keep(low_a, sent_low)
        high_a = scatter_keep(high_a, sent_high)
        if at == last - 1:
            low_a, shard_h = lax.optimization_barrier((low_a, shard_h))
    shards_a = [added(pair, 0).astype(BF) for pair in (low_a, high_a)]
    shards_b = [added(pair, 0).astype(BF) for pair in (up, down)]

    shard_h = shard_h[:, : head_weight.shape[1]]
    grad_h = shard_h.astype(F32) + swap(shard_h, "tab", 0).astype(F32)
    place = jnp.arange(quarter)[None, :] + (2 + tab) * quarter - wide
    real = (place < nfeat) | ((place >= LANES) & (place < LANES + vectors.shape[0]))
    keep_a = jnp.where(real, shards_a[1].astype(F32), 0.0)
    squares = 0.5 * jnp.sum(grad_h * grad_h)
    for found in (shards_a[0], keep_a, *shards_b):
        found = found.astype(F32)
        squares = squares + jnp.sum(found * found)
    sums = jnp.concatenate([loss[0:1, 0:1], stats[0:3, 0:1], squares.reshape(1, 1)]).reshape(1, 5)
    sums = jnp.broadcast_to(jnp.pad(sums, ((0, 0), (0, LANES - 5))), (8, LANES))
    for step in [1] + high_bits + ["tab"]:
        sums = sums + swap(sums, step, count_fsdp)
    split_a = [halves(tab, found) for found in shards_a]
    split_b = [halves(tab, found) for found in shards_b]
    whole_grad = jnp.concatenate([side for found in split_a for side in found], axis=1).astype(F32)
    grad_qkv = whole_grad[:, :wide]
    grad_emb = whole_grad[:, wide : wide + nfeat].T
    grad_vectors = whole_grad[:, wide + LANES : wide + LANES + vectors.shape[0]].T
    grad_out = jnp.concatenate([side[:, :half] for side in split_b[0]], axis=1)
    grad_up = jnp.concatenate([side[:, half:] for side in split_b[0]], axis=1)
    grad_down = jnp.concatenate(split_b[1], axis=1)
    summed = (grad_emb, grad_qkv, grad_out, grad_up, grad_down, grad_h, grad_vectors)
    loss_sum = sums[0, 0]
    rms_sums = sums[0, 1:4]
    clip_norm = jnp.sqrt(sums[0, 4])
    row_count = row_count[0, 0]
    factor = jnp.minimum(1.0, CLIP / clip_norm)
    new_moms, new_weights, new_emas = ([], [], [])
    for weight, grad, moment, average in zip(masters, summed, moms, emas):
        clipped = grad.astype(F32) * factor
        moment_new = MOMENTUM * moment + clipped
        weight_new = weight - RATE * (clipped + MOMENTUM * moment_new)
        new_moms.append(moment_new)
        new_weights.append(weight_new)
        new_emas.append(AVERAGE * average + (1.0 - AVERAGE) * weight_new)
    return (loss_sum, row_count, rms_sums, clip_norm, *new_moms, *new_weights, *new_emas)


def solution(mesh):
    by_row, by_column = P("fsdp", None), P(None, "fsdp")
    weights = (by_column, by_row, by_row, by_row, by_row, by_row, by_column)
    return jax.shard_map(
        functools.partial(on_device, mesh.shape["fsdp"]),
        mesh=mesh,
        in_specs=(P("fsdp", "tab", None), P("fsdp"), P("fsdp", "tab"), P("fsdp", "tab")) + weights * 3,
        out_specs=(P(), P(), P(), P()) + weights * 3,
        check_vma=False,
    )
```
